32 devices in a mesh: groups: 1, lat: 16 (over z, y, x), lon: 2 (over core).
Axes of the slice: x: 2, y: 2, z: 4, core: 2. Of those that a mesh axis runs over, the one named last changes fastest.
Arguments:
- fields: bfloat16 [64, 128, 256], P('groups', 'lat', 'lon'), may hold values from -6 to 6
- conv_first: bfloat16 [64, 64, 3, 3], replicated, may hold values from -0.25 to 0.25
- conv_second: bfloat16 [64, 64, 3, 3], replicated, may hold values from -0.25 to 0.25
- mixing: bfloat16 [64, 64, 64], P(None, 'lon'), may hold values from -0.75 to 0.75
Outputs:
- result: bfloat16 [64, 128, 256], P(('groups', 'lon'), 'lat')
The draws below stay inside these ranges and needn't reach their ends.
All inputs are finite; a program needn't handle non-finite values.
Results may differ from the reference program's by a relative error of at most 0.0095.
Values may be sent and summed in bfloat16 or wider, within the bound.
No kernel may reach another device: no remote copies, remote signals or barrier semaphores. Data moves between devices by JAX's collectives and lax.ppermute only.
A program may use at most 64 MiB of HBM per device.

```python
import math
import jax
import jax.numpy as jnp
from jax import lax

C = 64
NLAT = 128
NLON = 256
MMAX = 64
LDEG = 64
N_LAT = 16


def steps_of(key, dims, split, smallest, largest):
    def one(axis_at, blocks):
        draws = jax.random.uniform(jax.random.fold_in(jax.random.fold_in(key, 6), axis_at), (blocks,), jnp.float32, smallest / len(split), largest / len(split))
        return jnp.repeat(jnp.exp(draws), dims[axis_at] // blocks).reshape((-1,) + (1,) * (len(dims) - axis_at - 1))

    factor_of = one(*split[0])
    for cut in split[1:]:
        factor_of = factor_of * one(*cut)
    return factor_of


def centred(stream_key, shape, deviation, limit, shards=(), held_as=jnp.bfloat16):
    values = jax.random.normal(stream_key, shape, jnp.float32) * deviation
    if len(shards) > 0:
        values = steps_of(stream_key, shape, shards, -0.22, 0.18) * values
    return jnp.clip(values, min=-limit, max=limit).astype(held_as)


def setup_inputs(seed: int = 0, part: int = 0) -> dict:
    splits = jax.random.split(jax.random.key(seed), 5)
    own_keys = jax.random.split(jax.random.fold_in(splits[4], part), 5)
    fields = centred(own_keys[0], (C, NLAT, NLON), 1.0, 6.0, ((1, 16), (2, 2)))
    conv_first = centred(splits[1], (C, C, 3, 3), (9 * C) ** -0.5, 0.25)
    conv_second = centred(splits[2], (C, C, 3, 3), (9 * C) ** -0.5, 0.25)
    mixing = centred(splits[3], (LDEG, C, C), C ** -0.5, 0.75, ((1, 2),))
    return {"fields": fields, "conv_first": conv_first, "conv_second": conv_second, "mixing": mixing}


def forward_table(lon_total, orders):
    points = jnp.arange(lon_total, dtype=jnp.int32)[:, None]
    waves = jnp.arange(orders, dtype=jnp.int32)[None, :]
    angle = (points * waves % lon_total).astype(jnp.float32) * (2.0 * math.pi / lon_total)
    stacked = jnp.stack([jnp.cos(angle), -jnp.sin(angle)], axis=-1)
    return stacked.reshape(lon_total, 2 * orders).astype(jnp.bfloat16)

def inverse_table(lon_total, orders):
    waves = jnp.arange(orders, dtype=jnp.int32)[:, None]
    points = jnp.arange(lon_total, dtype=jnp.int32)[None, :]
    angle = (points * waves % lon_total).astype(jnp.float32) * (2.0 * math.pi / lon_total)
    factor = jnp.where(waves == 0, 1.0, 2.0).astype(jnp.float32)
    stacked = jnp.stack([factor * jnp.cos(angle), -factor * jnp.sin(angle)], axis=1)
    return stacked.reshape(2 * orders, lon_total).astype(jnp.bfloat16)

def quadrature(lat_total, lon_total):
    lat_rows = jnp.arange(lat_total, dtype=jnp.int32).astype(jnp.float32)
    colatitude = (lat_rows + 0.5) * (math.pi / lat_total)
    return jnp.sin(colatitude) * (math.pi / lat_total / lon_total)

def legendre_table(order_ids, degrees, lat_total):
    half_rows = lat_total // 2
    lat_rows = jnp.arange(half_rows, dtype=jnp.int32).astype(jnp.float32)
    colatitude = (lat_rows + 0.5) * (math.pi / lat_total)
    cosine = jnp.cos(colatitude)[None, :]
    sine_theta = jnp.sin(colatitude)[None, :]
    orders = order_ids.astype(jnp.float32)[:, None]
    counter = jnp.arange(1, degrees + 1, dtype=jnp.int32).astype(jnp.float32)
    log_terms = jnp.log((2.0 * counter - 1.0) / (2.0 * counter))
    below = counter[None, :] <= orders
    log_start = 0.5 * jnp.log(orders + 0.5) + 0.5 * lax.optimization_barrier(jnp.sum(jnp.where(below, log_terms[None, :], 0.0), axis=1, keepdims=True))
    log_start = log_start + orders * jnp.log(sine_theta)
    block_span = 32 if degrees % 32 == 0 else degrees

    def advance(carry, block_index):
        current, previous, log_scale = carry
        emitted = []
        for offset in range(block_span):
            degree = (block_index * block_span + offset).astype(jnp.float32)
            earlier = degree - 1.0
            coef_a = jnp.sqrt(jnp.maximum(4.0 * degree * degree - 1.0, 1.0) / jnp.maximum(degree * degree - orders * orders, 1.0))
            coef_b = jnp.sqrt(jnp.maximum(earlier * earlier - orders * orders, 0.0) / jnp.maximum(4.0 * earlier * earlier - 1.0, 1.0))
            newest = coef_a * (cosine * current - coef_b * previous)
            is_start = degree == orders
            before = degree < orders
            newest = jnp.where(before, 0.0, jnp.where(is_start, 1.0, newest))
            log_scale = jnp.where(is_start, log_start, log_scale)
            previous = jnp.where(is_start | before, 0.0, current)
            current = newest
            emitted.append(newest * jnp.exp(log_scale))
        size_now = jnp.maximum(jnp.abs(current), jnp.abs(previous))
        safe_size = jnp.where(size_now > 0.0, size_now, 1.0)
        carry_out = (current / safe_size, previous / safe_size, log_scale + jnp.log(safe_size))
        return (carry_out, jnp.stack(emitted, axis=-1))
    zeros = jnp.zeros((order_ids.shape[0], half_rows), jnp.float32)
    blocks = jnp.arange(degrees // block_span, dtype=jnp.int32)
    unused, stacked = lax.scan(advance, (zeros, zeros, zeros), blocks)
    northern = jnp.transpose(stacked, (1, 2, 0, 3)).reshape(order_ids.shape[0], half_rows, degrees)
    degree_ids = jnp.arange(degrees, dtype=jnp.int32)
    parity = (1 - 2 * ((degree_ids[None, :] + order_ids[:, None]) % 2)).astype(jnp.float32)
    southern = northern[:, ::-1, :] * parity[:, None, :]
    return jnp.concatenate([northern, southern], axis=1).astype(jnp.bfloat16)

def conv_layer(values, kernel):
    padded = jnp.pad(values, ((0, 0), (1, 1), (0, 0)))
    padded = jnp.concatenate([padded[:, :, -1:], padded, padded[:, :, :1]], axis=2)
    result = lax.conv_general_dilated(padded[None].astype(jnp.float32), kernel.astype(jnp.float32), (1, 1), 'VALID', dimension_numbers=('NCHW', 'OIHW', 'NCHW'), precision=lax.Precision.HIGHEST)[0]
    return jnp.maximum(result, 0.0).astype(jnp.bfloat16)

def reference(fields, conv_first, conv_second, mixing):
    hidden = conv_layer(conv_layer(fields, conv_first), conv_second)
    lat_total = NLAT
    lon_total = NLON
    orders = MMAX
    spectra = jnp.dot(hidden.reshape(C * lat_total, lon_total), forward_table(lon_total, orders), preferred_element_type=jnp.float32)
    spectra = spectra.reshape(C, lat_total, 2 * orders)
    coeffs = (spectra * quadrature(lat_total, lon_total)[None, :, None]).astype(jnp.bfloat16)
    per_group = orders // N_LAT
    pieces = jnp.moveaxis(coeffs.reshape(C, lat_total, N_LAT, per_group, 2), 2, 0)

    def one_group(inputs):
        group_index, item_block = inputs
        order_ids = (group_index * per_group + jnp.arange(per_group, dtype=jnp.int32)).astype(jnp.int32)
        legendre = legendre_table(order_ids, LDEG, lat_total).astype(jnp.float32)
        spectral = jnp.einsum('cjmr,mjl->lcmr', item_block.astype(jnp.float32), legendre).astype(jnp.bfloat16)
        mixed_coef = jnp.einsum('lcmr,loc->lomr', spectral.astype(jnp.float32), mixing.astype(jnp.float32)).astype(jnp.bfloat16)
        return jnp.einsum('lomr,mjl->ojmr', mixed_coef.astype(jnp.float32), legendre).astype(jnp.bfloat16)
    synthesis = lax.map(one_group, (jnp.arange(N_LAT, dtype=jnp.int32), pieces))
    synthesis = jnp.moveaxis(synthesis, 0, 2).reshape(C * lat_total, 2 * orders)
    result = jnp.dot(synthesis, inverse_table(lon_total, orders), preferred_element_type=jnp.float32)
    return result.reshape(C, lat_total, lon_total).astype(jnp.bfloat16)
```

```python
import math

import jax
import jax.numpy as jnp
from jax import lax
from jax.sharding import PartitionSpec as P


def forward_table(lon_total, orders):
    points = jnp.arange(lon_total, dtype=jnp.int32)[:, None]
    waves = jnp.arange(orders, dtype=jnp.int32)[None, :]
    angle = (points * waves % lon_total).astype(jnp.float32) * (2.0 * math.pi / lon_total)
    stacked = jnp.stack([jnp.cos(angle), -jnp.sin(angle)], axis=-1)
    return stacked.reshape(lon_total, 2 * orders).astype(jnp.bfloat16)


def inverse_table(lon_total, orders):
    waves = jnp.arange(orders, dtype=jnp.int32)[:, None]
    points = jnp.arange(lon_total, dtype=jnp.int32)[None, :]
    angle = (points * waves % lon_total).astype(jnp.float32) * (2.0 * math.pi / lon_total)
    factor = jnp.where(waves == 0, 1.0, 2.0).astype(jnp.float32)
    stacked = jnp.stack([factor * jnp.cos(angle), -factor * jnp.sin(angle)], axis=1)
    return stacked.reshape(2 * orders, lon_total).astype(jnp.bfloat16)


def quadrature(lat_total, lon_total):
    lat_rows = jnp.arange(lat_total, dtype=jnp.int32).astype(jnp.float32)
    colatitude = (lat_rows + 0.5) * (math.pi / lat_total)
    return jnp.sin(colatitude) * (math.pi / lat_total / lon_total)


def legendre_table(order_ids, degrees, lat_total):
    half_rows = lat_total // 2
    lat_rows = jnp.arange(half_rows, dtype=jnp.int32).astype(jnp.float32)
    colatitude = (lat_rows + 0.5) * (math.pi / lat_total)
    cosine = jnp.cos(colatitude)[None, :]
    sine_theta = jnp.sin(colatitude)[None, :]
    orders = order_ids.astype(jnp.float32)[:, None]
    counter = jnp.arange(1, degrees + 1, dtype=jnp.int32).astype(jnp.float32)
    log_terms = jnp.log((2.0 * counter - 1.0) / (2.0 * counter))
    below = counter[None, :] <= orders
    log_start = 0.5 * jnp.log(orders + 0.5) + 0.5 * jnp.sum(
        jnp.where(below, log_terms[None, :], 0.0), axis=1, keepdims=True
    )
    log_start = log_start + orders * jnp.log(sine_theta)
    block_span = 32

    def advance(carry, block_index):
        current, previous, log_scale = carry
        emitted = []
        for offset in range(block_span):
            degree = (block_index * block_span + offset).astype(jnp.float32)
            earlier = degree - 1.0
            coef_a = jnp.sqrt(
                jnp.maximum(4.0 * degree * degree - 1.0, 1.0)
                / jnp.maximum(degree * degree - orders * orders, 1.0)
            )
            coef_b = jnp.sqrt(
                jnp.maximum(earlier * earlier - orders * orders, 0.0)
                / jnp.maximum(4.0 * earlier * earlier - 1.0, 1.0)
            )
            newest = coef_a * (cosine * current - coef_b * previous)
            is_start = degree == orders
            before = degree < orders
            newest = jnp.where(before, 0.0, jnp.where(is_start, 1.0, newest))
            log_scale = jnp.where(is_start, log_start, log_scale)
            previous = jnp.where(is_start | before, 0.0, current)
            current = newest
            emitted.append(newest * jnp.exp(log_scale))
        size_now = jnp.maximum(jnp.abs(current), jnp.abs(previous))
        safe_size = jnp.where(size_now > 0.0, size_now, 1.0)
        carry_out = (current / safe_size, previous / safe_size, log_scale + jnp.log(safe_size))
        return (carry_out, jnp.stack(emitted, axis=-1))

    zeros = jnp.zeros((order_ids.shape[0], half_rows), jnp.float32)
    blocks = jnp.arange(degrees // block_span, dtype=jnp.int32)
    unused, stacked = lax.scan(advance, (zeros, zeros, zeros), blocks)
    northern = jnp.transpose(stacked, (1, 2, 0, 3)).reshape(order_ids.shape[0], half_rows, degrees)
    degree_ids = jnp.arange(degrees, dtype=jnp.int32)
    parity = (1 - 2 * ((degree_ids[None, :] + order_ids[:, None]) % 2)).astype(jnp.float32)
    southern = northern[:, ::-1, :] * parity[:, None, :]
    return jnp.concatenate([northern, southern], axis=1).astype(jnp.bfloat16)

def convolve(padded, kernel):
    padded = jnp.concatenate([padded[:, :, -1:], padded, padded[:, :, :1]], axis=2)
    return lax.conv_general_dilated(
        padded[None],
        kernel,
        (1, 1),
        "VALID",
        dimension_numbers=("NCHW", "OIHW", "NCHW"),
        preferred_element_type=jnp.float32,
    )[0]


def local(fields, conv_first, conv_second, mixing):
    lat_count = lax.axis_size("lat")
    lon_count = lax.axis_size("lon")
    assert lon_count == 2
    channels, row_count, _ = fields.shape
    lat_total = row_count * lat_count
    lon_total = fields.shape[2] * lon_count
    orders = lat_total // 2
    degrees = mixing.shape[0]
    owners = lat_count * lon_count
    per_device = orders // owners
    half = row_count // 2
    lat_index = lax.axis_index("lat")
    side = lax.axis_index("lon")
    swap = [(0, 1), (1, 0)]
    both = ("lat", "lon")

    other = lax.ppermute(fields, "lon", swap)
    other_mixing = lax.ppermute(mixing, "lon", swap)
    upper = side == 0
    full = jnp.concatenate(
        [jnp.where(upper, fields, other), jnp.where(upper, other, fields)], axis=2
    )
    message = jnp.where(upper, full[:, :2], full[:, row_count - 2 :])
    pairs = []
    for i in range(lat_count - 1):
        pairs.append((2 * i + 1, 2 * (i + 1)))
        pairs.append((2 * (i + 1), 2 * i + 1))
    halo = lax.ppermute(message, both, pairs)
    rows = jnp.where(
        upper,
        jnp.concatenate([halo, full[:, : half + 2]], axis=1),
        jnp.concatenate([full[:, half - 2 :], halo], axis=1),
    )

    first_row = lat_index * row_count + side * half
    hidden = jnp.maximum(convolve(rows, conv_first), 0.0)
    row_ids = first_row - 1 + jnp.arange(half + 2, dtype=jnp.int32)
    inside = (row_ids >= 0) & (row_ids < lat_total)
    hidden = jnp.where(inside[None, :, None], hidden, 0.0).astype(jnp.bfloat16)
    hidden = jnp.maximum(convolve(hidden, conv_second), 0.0).astype(jnp.bfloat16)

    table = forward_table(lon_total, orders).reshape(lon_total, owners, per_device, 2)
    spectra = jnp.einsum("cjk,kdmr->dmjrc", hidden, table, preferred_element_type=jnp.float32)
    weights = lax.dynamic_slice_in_dim(quadrature(lat_total, lon_total), first_row, half, 0)
    coeffs = (spectra * weights[None, None, :, None, None]).astype(jnp.bfloat16)
    coeffs = coeffs.reshape(owners, per_device * half, 2 * channels)
    pieces = lax.all_to_all(coeffs, both, split_axis=0, concat_axis=0, tiled=True)
    pieces = pieces.reshape(owners, per_device, half, 2, channels)

    order_ids = (2 * lat_index + side) * per_device + jnp.arange(per_device, dtype=jnp.int32)
    legendre = legendre_table(order_ids, degrees, lat_total)
    mixing = jnp.concatenate(
        [jnp.where(upper, mixing, other_mixing), jnp.where(upper, other_mixing, mixing)], axis=1
    )
    split = legendre.reshape(per_device, owners, half, degrees)
    spectral = jnp.einsum(
        "dmjrc,mdjl->lcmr", pieces, split, preferred_element_type=jnp.float32
    ).astype(jnp.bfloat16)
    spectral = spectral.reshape(degrees, channels, 2 * per_device)
    mixed = jnp.einsum(
        "lcx,loc->lox", spectral, mixing, preferred_element_type=jnp.float32
    ).astype(jnp.bfloat16)
    mixed = mixed.reshape(degrees, 2, channels // 2, per_device, 2)
    bands = legendre.reshape(per_device, lat_count, row_count, degrees)
    synthesis = jnp.einsum(
        "lhomr,mbjl->bhjmro", mixed, bands, preferred_element_type=jnp.float32
    ).astype(jnp.bfloat16)
    synthesis = synthesis.reshape(owners, row_count, per_device * channels)

    back = lax.all_to_all(synthesis, both, split_axis=0, concat_axis=0, tiled=True)
    back = back.reshape(owners, row_count, per_device, 2, channels // 2)
    inverse = inverse_table(lon_total, orders).reshape(owners, per_device, 2, lon_total)
    return jnp.einsum(
        "djmro,dmrk->ojk", back, inverse, preferred_element_type=jnp.float32
    ).astype(jnp.bfloat16)


def solution(mesh):
    in_specs = (P("groups", "lat", "lon"), P(), P(), P(None, "lon", None))
    out_specs = P(("groups", "lon"), "lat", None)
    return jax.shard_map(local, mesh=mesh, in_specs=in_specs, out_specs=out_specs, check_vma=False)
```

```python
import functools
import math

import jax
import jax.numpy as jnp
from jax import lax
from jax.experimental import pallas as pl
from jax.experimental.pallas import tpu as pltpu
from jax.sharding import PartitionSpec as P

VMEM = pl.BlockSpec(memory_space=pltpu.VMEM)
SMEM = pl.BlockSpec(memory_space=pltpu.SMEM)
LIMIT = 48 * 1024 * 1024


def call(kernel, out_shape, scratch, in_specs, cost):
    return pl.pallas_call(
        kernel,
        out_shape=out_shape,
        in_specs=in_specs,
        out_specs=jax.tree.map(lambda _: VMEM, out_shape),
        scratch_shapes=scratch,
        compiler_params=pltpu.CompilerParams(vmem_limit_bytes=LIMIT),
        cost_estimate=cost,
    )


def wave_angles(lon_total, waves):
    points = jnp.arange(lon_total, dtype=jnp.int32)[None, :]
    return (points * waves[:, None] % lon_total).astype(jnp.float32) * (2.0 * math.pi / lon_total)


def forward_table(lon_total, orders):
    angle = wave_angles(lon_total, jnp.arange(orders, dtype=jnp.int32))
    return jnp.concatenate([jnp.cos(angle), -jnp.sin(angle)], axis=0).astype(jnp.bfloat16)


def inverse_table(lon_total, owners, per_device, groups):
    orders = owners * per_device
    waves = jnp.arange(orders, dtype=jnp.int32)
    angle = wave_angles(lon_total, waves)
    factor = jnp.where(waves == 0, 1.0, 2.0).astype(jnp.float32)[:, None]
    table = jnp.stack([factor * jnp.cos(angle), -factor * jnp.sin(angle)], axis=1)
    table = table.astype(jnp.bfloat16).reshape(owners, 1, 2 * per_device, 1, lon_total)
    same = jnp.eye(groups, dtype=jnp.bfloat16)[None, :, None, :, None]
    return (table * same).reshape(2 * orders * groups, groups * lon_total)


def quadrature(lat_rows, lat_total, lon_total):
    colatitude = (lat_rows.astype(jnp.float32) + 0.5) * (math.pi / lat_total)
    return jnp.sin(colatitude) * (math.pi / lat_total / lon_total)


def legendre_kernel(span, lanes_ref, analysis_ref, synthesis_ref, first_ref, second_ref):
    degrees = first_ref.shape[0]
    cosine, log_start, orders = lanes_ref[0], lanes_ref[1], lanes_ref[2]
    even_sign, odd_sign = lanes_ref[3], lanes_ref[4]
    orders_squared = orders * orders

    def advance(block, carry):
        current, previous, log_scale = carry
        for offset in range(span):
            degree_id = block * span + offset
            degree = jnp.float32(1.0) * degree_id
            earlier = degree - 1.0
            coef_a = jnp.sqrt(
                jnp.maximum(4.0 * degree * degree - 1.0, 1.0)
                / jnp.maximum(degree * degree - orders_squared, 1.0)
            )
            coef_b = jnp.sqrt(
                jnp.maximum(earlier * earlier - orders_squared, 0.0)
                / jnp.maximum(4.0 * earlier * earlier - 1.0, 1.0)
            )
            newest = coef_a * (cosine * current - coef_b * previous)
            is_start = degree == orders
            before = degree < orders
            newest = jnp.where(before, 0.0, jnp.where(is_start, 1.0, newest))
            log_scale = jnp.where(is_start, log_start, log_scale)
            previous = jnp.where(is_start | before, 0.0, current)
            current = newest
            sign = even_sign if offset % 2 == 0 else odd_sign
            emitted = newest * jnp.exp(log_scale) * sign
            first_ref[pl.ds(degree_id, 1), :] = emitted[0:1]
            second_ref[pl.ds(degree_id, 1), :] = emitted[1:2]
        size_now = jnp.maximum(jnp.abs(current), jnp.abs(previous))
        safe_size = jnp.where(size_now > 0.0, size_now, 1.0)
        return current / safe_size, previous / safe_size, log_scale + jnp.log(safe_size)

    zeros = jnp.zeros_like(cosine)
    lax.fori_loop(0, degrees // span, advance, (zeros, zeros, zeros))
    per_device = analysis_ref.shape[0] // degrees
    rows = synthesis_ref.shape[0]
    own_order = lanes_ref[5][0:1]
    values = first_ref[...]
    for m in range(per_device):
        analysis_ref[m * degrees : (m + 1) * degrees, :] = jnp.where(
            own_order == m, values, 0.0
        ).astype(jnp.bfloat16)
    stacked = jnp.concatenate(
        [second_ref[:, m * rows : (m + 1) * rows] for m in range(per_device)], axis=0
    )
    synthesis_ref[...] = stacked.T.astype(jnp.bfloat16)


def legendre_tables(first_order, per_device, degrees, lat_total, row_count, half):
    bands = lat_total // row_count
    lane = jnp.arange(lat_total * per_device, dtype=jnp.int32)
    own_first = lane // half % per_device
    row_first = lane // (half * per_device) * half + lane % half
    own_second = lane // lat_total
    row_second = lane % bands * row_count + lane // bands % row_count
    own = jnp.stack([own_first, own_second])
    row = jnp.stack([row_first, row_second])
    south = row >= lat_total // 2
    row = jnp.where(south, lat_total - 1 - row, row)
    colatitude = (row.astype(jnp.float32) + 0.5) * (math.pi / lat_total)
    order_ids = first_order + own
    orders = order_ids.astype(jnp.float32)
    counter = jnp.arange(1, degrees + 1, dtype=jnp.int32).astype(jnp.float32)
    log_terms = jnp.log((2.0 * counter - 1.0) / (2.0 * counter))
    own_orders = (first_order + jnp.arange(per_device, dtype=jnp.int32)).astype(jnp.float32)
    starts = 0.5 * jnp.log(own_orders + 0.5) + 0.5 * jnp.sum(
        jnp.where(counter[None, :] <= own_orders[:, None], log_terms[None, :], 0.0), axis=1
    )
    log_start = starts[0]
    for m in range(1, per_device):
        log_start = jnp.where(own == m, starts[m], log_start)
    log_start = log_start + orders * jnp.log(jnp.sin(colatitude))
    parity = (1 - 2 * (order_ids % 2)).astype(jnp.float32)
    lanes = jnp.stack(
        [
            jnp.cos(colatitude),
            log_start,
            orders,
            jnp.where(south, parity, 1.0),
            jnp.where(south, -parity, 1.0),
            own.astype(jnp.float32),
        ]
    )
    width = lane.shape[0]
    span = 32 if degrees % 32 == 0 else degrees
    return call(
        functools.partial(legendre_kernel, span),
        (
            jax.ShapeDtypeStruct((per_device * degrees, width), jnp.bfloat16),
            jax.ShapeDtypeStruct((lat_total, per_device * degrees), jnp.bfloat16),
        ),
        [pltpu.VMEM((degrees, width), jnp.float32), pltpu.VMEM((degrees, width), jnp.float32)],
        [VMEM],
        pl.CostEstimate(flops=40 * degrees * width, bytes_accessed=1 << 20, transcendentals=0),
    )(lanes)


def convolve_kernel(
    lat_total, row_ref, quad_ref, rows_ref, first_ref, second_ref, dft_ref, out_ref, mid_ref, hidden_ref, coeffs_ref
):
    channels, lon_total = rows_ref.shape[1:]
    half = hidden_ref.shape[0]

    def layer(source_ref, weights, row):
        taps = source_ref[row : row + 3].reshape(3 * channels, lon_total)
        sums = jnp.dot(weights, taps, preferred_element_type=jnp.float32)
        total = (
            sums[channels : 2 * channels]
            + pltpu.roll(sums[:channels], 1, 1)
            + pltpu.roll(sums[2 * channels :], lon_total - 1, 1)
        )
        return jnp.maximum(total, 0.0)

    weights = first_ref[...]
    for row in range(half + 2):
        values = layer(rows_ref, weights, row)
        if row == 0 or row == half + 1:
            place = row_ref[0] - 1 + row
            values = jnp.where((place >= 0) & (place < lat_total), values, 0.0)
        mid_ref[row] = values.astype(jnp.bfloat16)
    weights = second_ref[...]
    for row in range(half):
        hidden_ref[row] = layer(mid_ref, weights, row).astype(jnp.bfloat16)
    hidden = hidden_ref[...].reshape(half * channels, lon_total)
    spectra = lax.dot_general(
        dft_ref[...], hidden, (((1,), (1,)), ((), ())), preferred_element_type=jnp.float32
    )
    orders = spectra.shape[0] // 2
    for row in range(half):
        columns = slice(row * channels, (row + 1) * channels)
        both = jnp.concatenate([spectra[:orders, columns], spectra[orders:, columns]], axis=1)
        coeffs_ref[pl.ds(row, orders, stride=half), :] = both * quad_ref[row]
    out_ref[...] = coeffs_ref[...].astype(jnp.bfloat16).reshape(out_ref.shape)


def spectral_kernel(
    per_device, pieces_ref, analysis_ref, synthesis_ref, mixing_ref, out_ref, spectral_ref, chunk_ref
):
    owners, chunk_rows, width = pieces_ref.shape
    channels, _, columns = mixing_ref.shape
    degrees = columns // per_device
    parts = 2 * per_device
    kept = channels // 2
    groups = chunk_rows // parts
    packed = width // kept
    bands = synthesis_ref.shape[0] // (groups * packed)

    pieces = pieces_ref[...].reshape(owners * chunk_rows, width)
    spectral = jnp.dot(analysis_ref[...], pieces, preferred_element_type=jnp.float32)
    spectral_ref[...] = spectral.T.astype(jnp.bfloat16).astype(jnp.float32)

    def add_channel(channel, totals):
        weights = mixing_ref[channel].astype(jnp.float32)
        return tuple(
            total + weights * spectral_ref[pl.ds(part * channels + channel, 1), :]
            for part, total in enumerate(totals)
        )

    zeros = jnp.zeros((channels, columns), jnp.float32)
    mixed = lax.fori_loop(0, channels, add_channel, (zeros, zeros), unroll=8)
    lane = lax.broadcasted_iota(jnp.int32, (kept, columns), 1)
    blocks = []
    for side in range(2):
        for m in range(per_device):
            own = (lane >= m * degrees) & (lane < (m + 1) * degrees)
            for part in range(2):
                block = mixed[part][side * kept : (side + 1) * kept]
                blocks.append(jnp.where(own, block, 0.0).astype(jnp.bfloat16))
    values = lax.dot_general(
        synthesis_ref[...],
        jnp.concatenate(blocks, axis=0),
        (((1,), (1,)), ((), ())),
        preferred_element_type=jnp.float32,
    )
    for side in range(2):
        for group in range(groups):
            for part in range(parts):
                start = (side * parts + part) * kept
                pieces = [
                    values[(group * packed + i) * bands : (group * packed + i + 1) * bands, start : start + kept]
                    for i in range(packed)
                ]
                place = (side * groups + group) * parts + part
                chunk_ref[pl.ds(place, bands, stride=2 * groups * parts), :] = jnp.concatenate(
                    pieces, axis=1
                )
    out_ref[...] = chunk_ref[...].astype(jnp.bfloat16).reshape(out_ref.shape)


def inverse_kernel(pieces_ref, inverse_ref, out_ref, rows_ref):
    owners, chunk_rows, width = pieces_ref.shape
    kept, row_count, lon_total = out_ref.shape
    packed = width // kept
    pieces = pieces_ref[...].reshape(owners * chunk_rows, width)
    values = lax.dot_general(
        pieces, inverse_ref[...], (((0,), (0,)), ((), ())), preferred_element_type=jnp.float32
    )
    for row in range(row_count):
        group, place = row // packed, row % packed
        block = values[place * kept : (place + 1) * kept, group * lon_total : (group + 1) * lon_total]
        for tile in range(lon_total // 128):
            rows_ref[tile, pl.ds(row, kept, stride=row_count), :] = block[:, tile * 128 : (tile + 1) * 128]
    for tile in range(lon_total // 128):
        out_ref[:, :, tile * 128 : (tile + 1) * 128] = (
            rows_ref[tile].astype(jnp.bfloat16).reshape(kept, row_count, 128)
        )


def local(fields, conv_first, conv_second, mixing):
    lat_count = lax.axis_size("lat")
    lon_count = lax.axis_size("lon")
    channels, row_count, lon_part = fields.shape
    lat_total = row_count * lat_count
    lon_total = lon_part * lon_count
    orders = lat_total // 2
    degrees = mixing.shape[0]
    owners = lat_count * lon_count
    per_device = orders // owners
    half = row_count // 2
    kept = channels // 2
    lat_index = lax.axis_index("lat")
    side = lax.axis_index("lon")
    swap = [(0, 1), (1, 0)]
    both = ("lat", "lon")
    upper = side == 0

    other = lax.ppermute(fields, "lon", swap)
    other_mixing = lax.ppermute(mixing, "lon", swap)
    mine, theirs = jnp.transpose(fields, (1, 0, 2)), jnp.transpose(other, (1, 0, 2))
    full = jnp.concatenate(
        [jnp.where(upper, mine, theirs), jnp.where(upper, theirs, mine)], axis=2
    )
    message = jnp.where(upper, full[:2], full[row_count - 2 :])
    pairs = []
    for i in range(lat_count - 1):
        pairs.append((2 * i + 1, 2 * (i + 1)))
        pairs.append((2 * (i + 1), 2 * i + 1))
    halo = lax.ppermute(message, both, pairs)
    rows = jnp.where(
        upper,
        jnp.concatenate([halo, full[: half + 2]], axis=0),
        jnp.concatenate([full[half - 2 :], halo], axis=0),
    )

    first_row = lat_index * row_count + side * half
    weights = [
        jnp.transpose(kernel, (3, 0, 2, 1)).reshape(3 * channels, 3 * channels)
        for kernel in (conv_first, conv_second)
    ]
    row_ids = first_row + jnp.arange(half, dtype=jnp.int32)
    coeffs = call(
        functools.partial(convolve_kernel, lat_total),
        jax.ShapeDtypeStruct((owners, per_device * half, 2 * channels), jnp.bfloat16),
        [
            pltpu.VMEM((half + 2, channels, lon_total), jnp.bfloat16),
            pltpu.VMEM((half, channels, lon_total), jnp.bfloat16),
            pltpu.VMEM((orders * half, 2 * channels), jnp.float32),
        ],
        [SMEM, SMEM, VMEM, VMEM, VMEM, VMEM],
        pl.CostEstimate(flops=1 << 28, bytes_accessed=1 << 20, transcendentals=0),
    )(
        first_row[None],
        quadrature(row_ids, lat_total, lon_total),
        rows,
        weights[0],
        weights[1],
        forward_table(lon_total, orders),
    )
    pieces = lax.all_to_all(coeffs, both, split_axis=0, concat_axis=0, tiled=True)

    first_order = (2 * lat_index + side) * per_device
    analysis, synthesis = legendre_tables(
        first_order, per_device, degrees, lat_total, row_count, half
    )
    mixing = jnp.concatenate(
        [jnp.where(upper, mixing, other_mixing), jnp.where(upper, other_mixing, mixing)], axis=1
    )
    mixing = jnp.concatenate([jnp.transpose(mixing, (2, 1, 0))] * per_device, axis=2)
    width = 128
    chunk_rows = row_count * 2 * per_device * kept // width
    chunks = call(
        functools.partial(spectral_kernel, per_device),
        jax.ShapeDtypeStruct((owners, chunk_rows, width), jnp.bfloat16),
        [
            pltpu.VMEM((2 * channels, per_device * degrees), jnp.float32),
            pltpu.VMEM((owners * chunk_rows, width), jnp.float32),
        ],
        [VMEM] * 4,
        pl.CostEstimate(flops=1 << 24, bytes_accessed=1 << 20, transcendentals=0),
    )(pieces, analysis, synthesis, mixing)

    back = lax.all_to_all(chunks, both, split_axis=0, concat_axis=0, tiled=True)
    groups = chunk_rows // (2 * per_device)
    return call(
        inverse_kernel,
        jax.ShapeDtypeStruct((kept, row_count, lon_total), jnp.bfloat16),
        [pltpu.VMEM((lon_total // 128, kept * row_count, 128), jnp.float32)],
        [VMEM] * 2,
        pl.CostEstimate(flops=1 << 24, bytes_accessed=1 << 19, transcendentals=0),
    )(back, inverse_table(lon_total, owners, per_device, groups))


def solution(mesh):
    in_specs = (P("groups", "lat", "lon"), P(), P(), P(None, "lon", None))
    out_specs = P(("groups", "lon"), "lat", None)
    return jax.shard_map(local, mesh=mesh, in_specs=in_specs, out_specs=out_specs, check_vma=False)
```

```python
import functools
import math

import jax
import jax.numpy as jnp
from jax import lax
from jax.experimental import pallas as pl
from jax.experimental.pallas import tpu as pltpu
from jax.sharding import PartitionSpec as P

VMEM = pl.BlockSpec(memory_space=pltpu.VMEM)
ANY = pl.BlockSpec(memory_space=pl.ANY)
LIMIT = 40 * 1024 * 1024
LANES = 128


def call(kernel, out_shape, scratch, in_specs, cost):
    return pl.pallas_call(
        kernel,
        out_shape=out_shape,
        in_specs=in_specs,
        out_specs=jax.tree.map(lambda _: VMEM, out_shape),
        scratch_shapes=scratch,
        compiler_params=pltpu.CompilerParams(vmem_limit_bytes=LIMIT),
        cost_estimate=cost,
    )


def unpack_rows(source_ref, rows_ref):
    channels, row_count, lon_part = source_ref.shape
    for tile in range(lon_part // LANES):
        rows_ref[tile] = (
            source_ref[:, :, tile * LANES : (tile + 1) * LANES]
            .astype(jnp.float32)
            .reshape(channels * row_count, LANES)
        )


def packed_row(rows_ref, row, channels):
    tiles, count, _ = rows_ref.shape
    found = [
        rows_ref[tile, pl.ds(row, channels, stride=count // channels), :] for tile in range(tiles)
    ]
    return jnp.concatenate(found, axis=1).astype(jnp.bfloat16)


def rows_kernel(source_ref, out_ref, rows_ref):
    unpack_rows(source_ref, rows_ref)
    for row in range(out_ref.shape[0]):
        out_ref[row] = packed_row(rows_ref, row, out_ref.shape[1])


def place_row(out_ref, place, side, mine, theirs):
    lon_part = mine.shape[1]
    for position, values in ((side, mine), (1 - side, theirs)):
        start = pl.multiple_of(position * lon_part, LANES)
        out_ref[place, :, pl.ds(start, lon_part)] = values


def message_kernel(own_ref, other_ref, out_ref, rows_ref):
    row_count, channels, _ = own_ref.shape
    side = lax.axis_index("lon")
    unpack_rows(other_ref, rows_ref)
    for i in range(2):
        row = side * (row_count - 2) + i
        place_row(out_ref, i, side, own_ref[row], packed_row(rows_ref, row, channels))


def layer(source_ref, weights, row):
    channels, lon_total = source_ref.shape[1:]
    taps = source_ref[row : row + 3].reshape(3 * channels, lon_total)
    sums = jnp.dot(weights, taps, preferred_element_type=jnp.float32)
    total = (
        sums[channels : 2 * channels]
        + pltpu.roll(sums[:channels], 1, 1)
        + pltpu.roll(sums[2 * channels :], lon_total - 1, 1)
    )
    return jnp.maximum(total, 0.0)


def row_weight(row, lat_total, lon_total):
    place = jnp.full((1, LANES), row, jnp.int32).astype(jnp.float32)
    return jnp.sin((place + 0.5) * (math.pi / lat_total)) * (math.pi / lat_total / lon_total)


def row_spectra(dft, hidden, first_row, lat_total):
    count, channels, lon_total = hidden.shape
    spectra = lax.dot_general(
        dft,
        hidden.reshape(count * channels, lon_total),
        (((1,), (1,)), ((), ())),
        preferred_element_type=jnp.float32,
    )
    orders = spectra.shape[0] // 2
    found = []
    for i in range(count):
        columns = slice(i * channels, (i + 1) * channels)
        parts = jnp.concatenate([spectra[:orders, columns], spectra[orders:, columns]], axis=1)
        found.append(parts * row_weight(first_row + i, lat_total, lon_total))
    return found


def interior_kernel(
    lat_total,
    own_ref,
    other_ref,
    first_ref,
    second_ref,
    after_ref,
    first_out,
    second_out,
    dft_out,
    near_out,
    coeffs_out,
    rows_ref,
    band_ref,
    mid_ref,
    hidden_ref,
):
    del after_ref
    row_count, channels, lon_part = own_ref.shape
    lon_total = 2 * lon_part
    half = row_count // 2
    side = lax.axis_index("lon")
    for source, target in ((first_ref, first_out), (second_ref, second_out)):
        for b in range(3):
            target[b * channels : (b + 1) * channels, :] = jnp.concatenate(
                [source[a, b] for a in range(3)], axis=1
            )
    orders = dft_out.shape[0] // 2
    waves = lax.broadcasted_iota(jnp.int32, (orders, lon_total), 0)
    points = lax.broadcasted_iota(jnp.int32, (orders, lon_total), 1)
    angle = ((waves * points) & (lon_total - 1)).astype(jnp.float32) * (2.0 * math.pi / lon_total)
    dft_out[:orders, :] = jnp.cos(angle).astype(jnp.bfloat16)
    dft_out[orders:, :] = (-jnp.sin(angle)).astype(jnp.bfloat16)
    unpack_rows(other_ref, rows_ref)
    for i in range(half + 2):
        row = 2 * side + i
        place_row(band_ref, i, side, own_ref[row], packed_row(rows_ref, row, channels))
    weights = first_out[...]
    for i in range(half):
        mid_ref[i] = layer(band_ref, weights, i).astype(jnp.bfloat16)
    near_out[...] = mid_ref[pl.ds((half - 2) * side, 2)]
    weights = second_out[...]
    for i in range(half - 2):
        hidden_ref[i] = layer(mid_ref, weights, i).astype(jnp.bfloat16)
    first_row = lax.axis_index("lat") * row_count + side * half + 2 * (1 - side)
    found = row_spectra(dft_out[...], hidden_ref[...], first_row, lat_total)
    for i, values in enumerate(found):
        coeffs_out[i] = values


def edge_kernel(
    lat_total,
    half,
    halo_ref,
    message_ref,
    near_ref,
    first_ref,
    second_ref,
    dft_ref,
    coeffs_ref,
    after_ref,
    out_ref,
    band_ref,
    mid_ref,
    hidden_ref,
    packed_ref,
):
    del after_ref
    side = lax.axis_index("lon")
    first_row = lax.axis_index("lat") * (2 * half) + side * half
    band_ref[pl.ds(2 * side, 2)] = halo_ref[...]
    band_ref[pl.ds(2 - 2 * side, 2)] = message_ref[...]
    mid_ref[pl.ds(2 - 2 * side, 2)] = near_ref[...]
    weights = first_ref[...]
    for i in range(2):
        place = first_row - 1 + side * half + i
        values = layer(band_ref, weights, i)
        values = jnp.where((place >= 0) & (place < lat_total), values, 0.0)
        mid_ref[2 * side + i] = values.astype(jnp.bfloat16)
    weights = second_ref[...]
    for i in range(2):
        hidden_ref[i] = layer(mid_ref, weights, i).astype(jnp.bfloat16)
    edge = side * (half - 2)
    found = row_spectra(dft_ref[...], hidden_ref[...], first_row + edge, lat_total)
    orders = dft_ref.shape[0] // 2
    for i in range(2):
        packed_ref[pl.ds(edge + i, orders, stride=half), :] = found[i]
    for i in range(half - 2):
        packed_ref[pl.ds(2 - 2 * side + i, orders, stride=half), :] = coeffs_ref[i]
    out_ref[...] = packed_ref[...].astype(jnp.bfloat16).reshape(out_ref.shape)


def mixing_kernel(per_device, mixing_ref, after_ref, out_ref, source_ref, target_ref):
    del after_ref
    degrees, kept, channels = mixing_ref.shape
    source_ref[:, :channels] = mixing_ref[...].astype(jnp.float32).reshape(degrees * kept, channels)
    tiles = per_device * degrees // LANES
    for o in range(kept):
        block = source_ref[pl.ds(o, degrees, stride=kept), :].T[:channels]
        block = jnp.concatenate([block] * per_device, axis=1)
        for tile in range(tiles):
            target_ref[tile, pl.ds(o, channels, stride=kept), :] = block[
                :, tile * LANES : (tile + 1) * LANES
            ]
    for tile in range(tiles):
        out_ref[:, :, tile * LANES : (tile + 1) * LANES] = (
            target_ref[tile].astype(jnp.bfloat16).reshape(channels, kept, LANES)
        )


def split_index(index, size):
    quotient = ((index.astype(jnp.float32) + 0.5) * (1.0 / size)).astype(jnp.int32)
    return quotient, index - quotient * size


def legendre_kernel(
    span, bands, row_count, per_device, after_ref, analysis_ref, synthesis_ref, first_ref, second_ref
):
    del after_ref
    degrees, width = first_ref.shape
    lat_total = bands * row_count
    half = row_count // 2
    first_order = (2 * lax.axis_index("lat") + lax.axis_index("lon")) * per_device
    lane = lax.broadcasted_iota(jnp.int32, (2, width), 1)
    form = lax.broadcasted_iota(jnp.int32, (2, width), 0)
    rest, low = split_index(lane, half)
    device, own_first = split_index(rest, per_device)
    rest, band = split_index(lane, bands)
    own_second, inner = split_index(rest, row_count)
    own = jnp.where(form == 0, own_first, own_second)
    row = jnp.where(form == 0, device * half + low, band * row_count + inner)
    south = row >= lat_total // 2
    row = jnp.where(south, lat_total - 1 - row, row)
    colatitude = (row.astype(jnp.float32) + 0.5) * (math.pi / lat_total)
    cosine, sine_theta = jnp.cos(colatitude), jnp.sin(colatitude)
    order_ids = first_order + own
    orders = order_ids.astype(jnp.float32)
    counter = 1.0 + lax.broadcasted_iota(jnp.int32, (1, max(degrees, LANES)), 1).astype(jnp.float32)
    log_terms = jnp.log((2.0 * counter - 1.0) / (2.0 * counter))
    log_start = 0.5 * jnp.log(orders + 0.5) + orders * jnp.log(sine_theta)
    for m in range(per_device):
        below = counter <= jnp.full(counter.shape, first_order + m, jnp.int32).astype(jnp.float32)
        total = jnp.sum(jnp.where(below, log_terms, 0.0), axis=1, keepdims=True)
        log_start = log_start + jnp.where(own == m, 0.5 * total, 0.0)
    parity = (1 - 2 * (order_ids & 1)).astype(jnp.float32)
    even_sign, odd_sign = jnp.where(south, parity, 1.0), jnp.where(south, -parity, 1.0)
    orders_squared = orders * orders

    def advance(block, carry):
        current, previous, log_scale = carry
        for offset in range(span):
            degree_id = block * span + offset
            degree = jnp.full(orders.shape, degree_id, jnp.int32).astype(jnp.float32)
            earlier = degree - 1.0
            coef_a = jnp.sqrt(
                jnp.maximum(4.0 * degree * degree - 1.0, 1.0)
                / jnp.maximum(degree * degree - orders_squared, 1.0)
            )
            coef_b = jnp.sqrt(
                jnp.maximum(earlier * earlier - orders_squared, 0.0)
                / jnp.maximum(4.0 * earlier * earlier - 1.0, 1.0)
            )
            newest = coef_a * (cosine * current - coef_b * previous)
            is_start = degree == orders
            before = degree < orders
            newest = jnp.where(before, 0.0, jnp.where(is_start, 1.0, newest))
            log_scale = jnp.where(is_start, log_start, log_scale)
            previous = jnp.where(is_start | before, 0.0, current)
            current = newest
            sign = even_sign if offset % 2 == 0 else odd_sign
            emitted = newest * jnp.exp(log_scale) * sign
            first_ref[pl.ds(degree_id, 1), :] = emitted[0:1]
            second_ref[pl.ds(degree_id, 1), :] = emitted[1:2]
        size_now = jnp.maximum(jnp.abs(current), jnp.abs(previous))
        safe_size = jnp.where(size_now > 0.0, size_now, 1.0)
        return current / safe_size, previous / safe_size, log_scale + jnp.log(safe_size)

    zeros = jnp.zeros_like(cosine)
    lax.fori_loop(0, degrees // span, advance, (zeros, zeros, zeros))
    values = first_ref[...]
    for m in range(per_device):
        analysis_ref[m * degrees : (m + 1) * degrees, :] = jnp.where(
            own[0:1] == m, values, 0.0
        ).astype(jnp.bfloat16)
    stacked = jnp.concatenate(
        [second_ref[:, m * lat_total : (m + 1) * lat_total] for m in range(per_device)], axis=0
    )
    synthesis_ref[...] = stacked.T.astype(jnp.bfloat16)


def spectral_kernel(
    per_device,
    pieces_ref,
    analysis_ref,
    synthesis_ref,
    mine_ref,
    theirs_ref,
    out_ref,
    spectral_ref,
    chunk_ref,
):
    owners, chunk_rows, width = pieces_ref.shape
    channels, kept, columns = mine_ref.shape
    degrees = columns // per_device
    parts = 2 * per_device
    groups = chunk_rows // parts
    packed = width // kept
    bands = synthesis_ref.shape[0] // (groups * packed)

    pieces = pieces_ref[...].reshape(owners * chunk_rows, width)
    spectral = jnp.dot(analysis_ref[...], pieces, preferred_element_type=jnp.float32)
    spectral_ref[...] = spectral.T.astype(jnp.bfloat16).astype(jnp.float32)

    def add_channel(channel, totals):
        rows = [spectral_ref[pl.ds(part * channels + channel, 1), :] for part in range(2)]
        mine = mine_ref[channel].astype(jnp.float32)
        theirs = theirs_ref[channel].astype(jnp.float32)
        return (
            totals[0] + mine * rows[0],
            totals[1] + mine * rows[1],
            totals[2] + theirs * rows[0],
            totals[3] + theirs * rows[1],
        )

    zeros = jnp.zeros((kept, columns), jnp.float32)
    totals = lax.fori_loop(0, channels, add_channel, (zeros,) * 4, unroll=8)
    upper = lax.axis_index("lon") == 0
    mixed = [
        [jnp.where(upper, totals[part], totals[2 + part]) for part in range(2)],
        [jnp.where(upper, totals[2 + part], totals[part]) for part in range(2)],
    ]
    lane = lax.broadcasted_iota(jnp.int32, (kept, columns), 1)
    blocks = []
    for side in range(2):
        for m in range(per_device):
            own = (lane >= m * degrees) & (lane < (m + 1) * degrees)
            for part in range(2):
                blocks.append(jnp.where(own, mixed[side][part], 0.0).astype(jnp.bfloat16))
    values = lax.dot_general(
        synthesis_ref[...],
        jnp.concatenate(blocks, axis=0),
        (((1,), (1,)), ((), ())),
        preferred_element_type=jnp.float32,
    )
    for side in range(2):
        for group in range(groups):
            for part in range(parts):
                start = (side * parts + part) * kept
                pieces = [
                    values[(group * packed + i) * bands : (group * packed + i + 1) * bands, start : start + kept]
                    for i in range(packed)
                ]
                place = (side * groups + group) * parts + part
                chunk_ref[pl.ds(place, bands, stride=2 * groups * parts), :] = jnp.concatenate(
                    pieces, axis=1
                )
    out_ref[...] = chunk_ref[...].astype(jnp.bfloat16).reshape(out_ref.shape)


def inverse_table_kernel(groups, per_device, after_ref, out_ref):
    del after_ref
    height, width = out_ref.shape
    lon_total = width // groups
    row = lax.broadcasted_iota(jnp.int32, (height, lon_total), 0)
    points = lax.broadcasted_iota(jnp.int32, (height, lon_total), 1)
    rest, part = split_index(row, 2)
    rest, order = split_index(rest, per_device)
    owner, group = split_index(rest, groups)
    waves = owner * per_device + order
    angle = ((waves * points) & (lon_total - 1)).astype(jnp.float32) * (2.0 * math.pi / lon_total)
    values = jnp.where(part == 0, jnp.cos(angle), -jnp.sin(angle))
    values = jnp.where(waves == 0, 1.0, 2.0) * values
    for i in range(groups):
        out_ref[:, i * lon_total : (i + 1) * lon_total] = jnp.where(
            group == i, values, 0.0
        ).astype(jnp.bfloat16)


def inverse_kernel(pieces_ref, inverse_ref, out_ref, rows_ref):
    owners, chunk_rows, width = pieces_ref.shape
    kept, row_count, lon_total = out_ref.shape
    packed = width // kept
    pieces = pieces_ref[...].reshape(owners * chunk_rows, width)
    values = lax.dot_general(
        pieces, inverse_ref[...], (((0,), (0,)), ((), ())), preferred_element_type=jnp.float32
    )
    for row in range(row_count):
        group, place = row // packed, row % packed
        block = values[place * kept : (place + 1) * kept, group * lon_total : (group + 1) * lon_total]
        for tile in range(lon_total // LANES):
            rows_ref[tile, pl.ds(row, kept, stride=row_count), :] = block[:, tile * LANES : (tile + 1) * LANES]
    for tile in range(lon_total // LANES):
        out_ref[:, :, tile * LANES : (tile + 1) * LANES] = (
            rows_ref[tile].astype(jnp.bfloat16).reshape(kept, row_count, LANES)
        )


def local(fields, conv_first, conv_second, mixing):
    lat_count = lax.axis_size("lat")
    lon_count = lax.axis_size("lon")
    channels, row_count, lon_part = fields.shape
    lat_total = row_count * lat_count
    lon_total = lon_part * lon_count
    orders = lat_total // 2
    degrees = mixing.shape[0]
    owners = lat_count * lon_count
    per_device = orders // owners
    half = row_count // 2
    kept = channels // 2
    swap = [(0, 1), (1, 0)]
    both = ("lat", "lon")
    bfloat = functools.partial(jax.ShapeDtypeStruct, dtype=jnp.bfloat16)

    other = lax.ppermute(fields, "lon", swap)
    other_mixing = lax.ppermute(mixing, "lon", swap)
    unpacked = pltpu.VMEM((lon_part // LANES, channels * row_count, LANES), jnp.float32)
    own = call(
        rows_kernel,
        bfloat((row_count, channels, lon_part)),
        [unpacked],
        [VMEM],
        pl.CostEstimate(flops=1 << 16, bytes_accessed=1 << 18, transcendentals=0),
    )(fields)
    message = call(
        message_kernel,
        bfloat((2, channels, lon_total)),
        [unpacked],
        [VMEM, VMEM],
        pl.CostEstimate(flops=1 << 16, bytes_accessed=1 << 18, transcendentals=0),
    )(own, other)
    pairs = []
    for i in range(lat_count - 1):
        pairs.append((2 * i + 1, 2 * (i + 1)))
        pairs.append((2 * (i + 1), 2 * i + 1))
    halo = lax.ppermute(message, both, pairs)

    taps = (3 * channels, 3 * channels)
    first, second, dft, near, interior = call(
        functools.partial(interior_kernel, lat_total),
        (
            bfloat(taps),
            bfloat(taps),
            bfloat((2 * orders, lon_total)),
            bfloat((2, channels, lon_total)),
            jax.ShapeDtypeStruct((half - 2, orders, 2 * channels), jnp.float32),
        ),
        [
            unpacked,
            pltpu.VMEM((half + 2, channels, lon_total), jnp.bfloat16),
            pltpu.VMEM((half, channels, lon_total), jnp.bfloat16),
            pltpu.VMEM((half - 2, channels, lon_total), jnp.bfloat16),
        ],
        [VMEM, VMEM, VMEM, VMEM, ANY],
        pl.CostEstimate(flops=1 << 28, bytes_accessed=1 << 22, transcendentals=0),
    )(
        own,
        other,
        jnp.transpose(conv_first, (2, 3, 0, 1)),
        jnp.transpose(conv_second, (2, 3, 0, 1)),
        message,
    )
    columns = per_device * degrees
    columns = per_device * degrees
    def mixing_table(values, after):
        return call(
            functools.partial(mixing_kernel, per_device),
            bfloat((channels, kept, columns)),
            [
                pltpu.VMEM((degrees * kept, LANES), jnp.float32),
                pltpu.VMEM((columns // LANES, channels * kept, LANES), jnp.float32),
            ],
            [VMEM, ANY],
            pl.CostEstimate(flops=1 << 20, bytes_accessed=1 << 22, transcendentals=0),
        )(values, after)

    mine = mixing_table(mixing, near)
    coeffs = call(
        functools.partial(edge_kernel, lat_total, half),
        bfloat((owners, per_device * half, 2 * channels)),
        [
            pltpu.VMEM((4, channels, lon_total), jnp.bfloat16),
            pltpu.VMEM((4, channels, lon_total), jnp.bfloat16),
            pltpu.VMEM((2, channels, lon_total), jnp.bfloat16),
            pltpu.VMEM((orders * half, 2 * channels), jnp.float32),
        ],
        [VMEM] * 7 + [ANY],
        pl.CostEstimate(flops=1 << 26, bytes_accessed=1 << 20, transcendentals=0),
    )(halo, message, near, first, second, dft, interior, mine)
    pieces = lax.all_to_all(coeffs, both, split_axis=0, concat_axis=0, tiled=True)

    theirs = mixing_table(other_mixing, coeffs)
    span = 32 if degrees % 32 == 0 else degrees
    width = lat_total * per_device
    analysis, synthesis = call(
        functools.partial(legendre_kernel, span, lat_count, row_count, per_device),
        (bfloat((columns, width)), bfloat((lat_total, columns))),
        [pltpu.VMEM((degrees, width), jnp.float32), pltpu.VMEM((degrees, width), jnp.float32)],
        [ANY],
        pl.CostEstimate(flops=1 << 20, bytes_accessed=1 << 21, transcendentals=0),
    )(coeffs)
    chunk_rows = row_count * 2 * per_device * kept // LANES
    chunks = call(
        functools.partial(spectral_kernel, per_device),
        bfloat((owners, chunk_rows, LANES)),
        [
            pltpu.VMEM((2 * channels, columns), jnp.float32),
            pltpu.VMEM((owners * chunk_rows, LANES), jnp.float32),
        ],
        [VMEM] * 5,
        pl.CostEstimate(flops=1 << 24, bytes_accessed=1 << 20, transcendentals=0),
    )(pieces, analysis, synthesis, mine, theirs)

    back = lax.all_to_all(chunks, both, split_axis=0, concat_axis=0, tiled=True)
    groups = chunk_rows // (2 * per_device)
    table = call(
        functools.partial(inverse_table_kernel, groups, per_device),
        bfloat((owners * chunk_rows, groups * lon_total)),
        [],
        [ANY],
        pl.CostEstimate(flops=1 << 22, bytes_accessed=1 << 21, transcendentals=0),
    )(chunks)
    return call(
        inverse_kernel,
        bfloat((kept, row_count, lon_total)),
        [pltpu.VMEM((lon_total // LANES, kept * row_count, LANES), jnp.float32)],
        [VMEM] * 2,
        pl.CostEstimate(flops=1 << 24, bytes_accessed=1 << 19, transcendentals=0),
    )(back, table)


def solution(mesh):
    in_specs = (P("groups", "lat", "lon"), P(), P(), P(None, "lon", None))
    out_specs = P(("groups", "lon"), "lat", None)
    return jax.shard_map(local, mesh=mesh, in_specs=in_specs, out_specs=out_specs, check_vma=False)
```

```python
import functools
import math

import jax
import jax.numpy as jnp
from jax import lax
from jax.experimental import pallas as pl
from jax.experimental.pallas import tpu as pltpu
from jax.sharding import PartitionSpec as P

VMEM = pl.BlockSpec(memory_space=pltpu.VMEM)
ANY = pl.BlockSpec(memory_space=pl.ANY)
HBM = pl.BlockSpec(memory_space=pltpu.HBM)
LIMIT = 40 * 1024 * 1024
LANES = 128


def call(kernel, out_shape, scratch, in_specs, cost):
    return pl.pallas_call(
        kernel,
        out_shape=out_shape,
        in_specs=in_specs,
        out_specs=jax.tree.map(lambda _: VMEM, out_shape),
        scratch_shapes=scratch,
        compiler_params=pltpu.CompilerParams(vmem_limit_bytes=LIMIT),
        cost_estimate=cost,
    )


def split_index(index, size):
    quotient = ((index.astype(jnp.float32) + 0.5) * (1.0 / size)).astype(jnp.int32)
    return quotient, index - quotient * size


def row_half():
    return (lax.axis_index("lat") + lax.axis_index("lon") + 1) & 1


def unpack_rows(source_ref, rows_ref):
    channels, row_count, lon_part = source_ref.shape
    for tile in range(lon_part // LANES):
        rows_ref[tile] = (
            source_ref[:, :, tile * LANES : (tile + 1) * LANES]
            .astype(jnp.float32)
            .reshape(channels * row_count, LANES)
        )


def packed_row(rows_ref, row, channels):
    tiles, count, _ = rows_ref.shape
    found = [
        rows_ref[tile, pl.ds(row, channels, stride=count // channels), :] for tile in range(tiles)
    ]
    return jnp.concatenate(found, axis=1).astype(jnp.bfloat16)


def load_kernel(
    fields_ref,
    conv_first_ref,
    conv_second_ref,
    own_ref,
    first_ref,
    second_ref,
    fields_copy_ref,
    rows_ref,
    arrived,
):
    copies = [
        pltpu.make_async_copy(source, target, arrived.at[i])
        for i, (source, target) in enumerate(
            (
                (fields_ref, fields_copy_ref),
                (conv_first_ref, first_ref),
                (conv_second_ref, second_ref),
            )
        )
    ]
    for copy in copies:
        copy.start()
    copies[0].wait()
    unpack_rows(fields_copy_ref, rows_ref)
    for row in range(own_ref.shape[0]):
        own_ref[row] = packed_row(rows_ref, row, own_ref.shape[1])
    for copy in copies[1:]:
        copy.wait()


def place_row(out_ref, place, side, mine, theirs):
    lon_part = mine.shape[1]
    for position, values in ((side, mine), (1 - side, theirs)):
        start = pl.multiple_of(position * lon_part, LANES)
        out_ref[place, :, pl.ds(start, lon_part)] = values


def message_kernel(own_ref, other_ref, out_ref, rows_ref):
    row_count, channels, _ = own_ref.shape
    side = lax.axis_index("lon")
    unpack_rows(other_ref, rows_ref)
    for i in range(2):
        row = row_half() * (row_count - 2) + i
        place_row(out_ref, i, side, own_ref[row], packed_row(rows_ref, row, channels))


def layer(source_ref, weights, row):
    channels, lon_total = source_ref.shape[1:]
    taps = source_ref[row : row + 3].reshape(3 * channels, lon_total)
    sums = jnp.dot(weights, taps, preferred_element_type=jnp.float32)
    total = (
        sums[channels : 2 * channels]
        + pltpu.roll(sums[:channels], 1, 1)
        + pltpu.roll(sums[2 * channels :], lon_total - 1, 1)
    )
    return jnp.maximum(total, 0.0)


def row_weight(row, lat_total, lon_total):
    place = jnp.full((1, LANES), row, jnp.int32).astype(jnp.float32)
    return jnp.sin((place + 0.5) * (math.pi / lat_total)) * (math.pi / lat_total / lon_total)


def row_spectra(dft, hidden, first_row, lat_total):
    count, channels, lon_total = hidden.shape
    spectra = lax.dot_general(
        dft,
        hidden.reshape(count * channels, lon_total),
        (((1,), (1,)), ((), ())),
        preferred_element_type=jnp.float32,
    )
    orders = spectra.shape[0] // 2
    found = []
    for i in range(count):
        columns = slice(i * channels, (i + 1) * channels)
        parts = jnp.concatenate([spectra[:orders, columns], spectra[orders:, columns]], axis=1)
        found.append(parts * row_weight(first_row + i, lat_total, lon_total))
    return found


def interior_kernel(
    lat_total,
    owners,
    own_ref,
    other_ref,
    first_ref,
    second_ref,
    after_ref,
    first_out,
    second_out,
    dft_out,
    near_out,
    coeffs_out,
    rows_ref,
    band_ref,
    mid_ref,
    hidden_ref,
):
    del after_ref
    row_count, channels, lon_part = own_ref.shape
    lon_total = 2 * lon_part
    half = row_count // 2
    side, part = lax.axis_index("lon"), row_half()
    for source, target in ((first_ref, first_out), (second_ref, second_out)):
        for b in range(3):
            target[b * channels : (b + 1) * channels, :] = jnp.concatenate(
                [source[a, b] for a in range(3)], axis=1
            )
    orders = dft_out.shape[0] // 2
    place = lax.broadcasted_iota(jnp.int32, (orders, lon_total), 0)
    order, owner = split_index(place, owners)
    waves = owner * (orders // owners) + order
    points = lax.broadcasted_iota(jnp.int32, (orders, lon_total), 1)
    angle = ((waves * points) & (lon_total - 1)).astype(jnp.float32) * (2.0 * math.pi / lon_total)
    dft_out[:orders, :] = jnp.cos(angle).astype(jnp.bfloat16)
    dft_out[orders:, :] = (-jnp.sin(angle)).astype(jnp.bfloat16)
    unpack_rows(other_ref, rows_ref)
    for i in range(half + 2):
        row = 2 * part + i
        place_row(band_ref, i, side, own_ref[row], packed_row(rows_ref, row, channels))
    weights = first_out[...]
    for i in range(half):
        mid_ref[i] = layer(band_ref, weights, i).astype(jnp.bfloat16)
    near_out[...] = mid_ref[pl.ds((half - 2) * part, 2)]
    weights = second_out[...]
    for i in range(half - 2):
        hidden_ref[i] = layer(mid_ref, weights, i).astype(jnp.bfloat16)
    first_row = lax.axis_index("lat") * row_count + part * half + 2 * (1 - part)
    found = row_spectra(dft_out[...], hidden_ref[...], first_row, lat_total)
    for i, values in enumerate(found):
        coeffs_out[i] = values


def edge_kernel(
    lat_total,
    half,
    halo_ref,
    message_ref,
    near_ref,
    first_ref,
    second_ref,
    dft_ref,
    coeffs_ref,
    mine_ref,
    theirs_ref,
    analysis_ref,
    out_ref,
    band_ref,
    mid_ref,
    hidden_ref,
    packed_ref,
):
    del mine_ref, theirs_ref, analysis_ref
    part = row_half()
    first_row = lax.axis_index("lat") * (2 * half) + part * half
    band_ref[pl.ds(2 * part, 2)] = halo_ref[...]
    band_ref[pl.ds(2 - 2 * part, 2)] = message_ref[...]
    mid_ref[pl.ds(2 - 2 * part, 2)] = near_ref[...]
    weights = first_ref[...]
    for i in range(2):
        place = first_row - 1 + part * half + i
        values = layer(band_ref, weights, i)
        values = jnp.where((place >= 0) & (place < lat_total), values, 0.0)
        mid_ref[2 * part + i] = values.astype(jnp.bfloat16)
    weights = second_ref[...]
    for i in range(2):
        hidden_ref[i] = layer(mid_ref, weights, i).astype(jnp.bfloat16)
    edge = part * (half - 2)
    found = row_spectra(dft_ref[...], hidden_ref[...], first_row + edge, lat_total)
    owners, chunk_rows, _ = out_ref.shape
    for m in range(chunk_rows // half):
        own = slice(m * owners, (m + 1) * owners)
        for i in range(2):
            start = m * half + edge + i
            packed_ref[pl.ds(start, owners, stride=chunk_rows), :] = found[i][own]
        for i in range(half - 2):
            start = m * half + 2 - 2 * part + i
            packed_ref[pl.ds(start, owners, stride=chunk_rows), :] = coeffs_ref[i, own]
    out_ref[...] = packed_ref[...].astype(jnp.bfloat16).reshape(out_ref.shape)


def mixing_kernel(per_device, mixing_ref, after_ref, out_ref):
    del after_ref
    values = jnp.transpose(mixing_ref[...].astype(jnp.float32), (1, 0, 2))
    blocks = [
        jnp.concatenate([values[o]] * per_device, axis=0).T for o in range(values.shape[0])
    ]
    out_ref[...] = jnp.transpose(jnp.stack(blocks), (1, 0, 2)).astype(jnp.bfloat16)


def legendre_kernel(
    span, bands, row_count, per_device, after_ref, analysis_ref, synthesis_ref, values_ref
):
    del after_ref
    tiles, count, _ = values_ref.shape
    degrees, width = count // 2, tiles * LANES
    lat_total = bands * row_count
    half = row_count // 2
    first_order = (2 * lax.axis_index("lat") + lax.axis_index("lon")) * per_device
    lane = lax.broadcasted_iota(jnp.int32, (2, width), 1)
    form = lax.broadcasted_iota(jnp.int32, (2, width), 0)
    rest, low = split_index(lane, half)
    device, own_first = split_index(rest, per_device)
    rest, band = split_index(lane, bands)
    own_second, inner = split_index(rest, row_count)
    own = jnp.where(form == 0, own_first, own_second)
    place = (device >> 1) * row_count + (((device >> 1) + device + 1) & 1) * half + low
    row = jnp.where(form == 0, place, band * row_count + inner)
    south = row >= lat_total // 2
    row = jnp.where(south, lat_total - 1 - row, row)
    colatitude = (row.astype(jnp.float32) + 0.5) * (math.pi / lat_total)
    cosine, sine_theta = jnp.cos(colatitude), jnp.sin(colatitude)
    order_ids = first_order + own
    orders = order_ids.astype(jnp.float32)
    counter = 1.0 + lax.broadcasted_iota(jnp.int32, (1, max(degrees, LANES)), 1).astype(jnp.float32)
    log_terms = jnp.log((2.0 * counter - 1.0) / (2.0 * counter))
    log_start = 0.5 * jnp.log(orders + 0.5) + orders * jnp.log(sine_theta)
    for m in range(per_device):
        below = counter <= jnp.full(counter.shape, first_order + m, jnp.int32).astype(jnp.float32)
        total = jnp.sum(jnp.where(below, log_terms, 0.0), axis=1, keepdims=True)
        log_start = log_start + jnp.where(own == m, 0.5 * total, 0.0)
    parity = (1 - 2 * (order_ids & 1)).astype(jnp.float32)
    even_sign, odd_sign = jnp.where(south, parity, 1.0), jnp.where(south, -parity, 1.0)
    orders_squared = orders * orders
    start_scale = jnp.exp(log_start)
    current = previous = scale = log_scale = jnp.zeros_like(cosine)
    root = jnp.zeros_like(cosine)
    for degree in range(degrees):
        distance = float(degree * degree) - orders_squared
        inverse_root = lax.rsqrt(jnp.maximum(distance, 1.0))
        above = math.sqrt(max(4.0 * degree * degree - 1.0, 1.0))
        below = math.sqrt(max(4.0 * (degree - 1) * (degree - 1) - 1.0, 1.0))
        newest = (above * inverse_root) * (cosine * current - (root * (1.0 / below)) * previous)
        root = jnp.maximum(distance, 0.0) * inverse_root
        is_start = orders == float(degree)
        newest = jnp.where(is_start, 1.0, newest)
        scale = jnp.where(is_start, start_scale, scale)
        log_scale = jnp.where(is_start, log_start, log_scale)
        previous, current = current, newest
        emitted = newest * scale * (even_sign if degree % 2 == 0 else odd_sign)
        for tile in range(tiles):
            values_ref[tile, 2 * degree : 2 * degree + 2, :] = emitted[
                :, tile * LANES : (tile + 1) * LANES
            ]
        if degree % span == span - 1 and degree < degrees - 1:
            size_now = jnp.maximum(jnp.abs(current), jnp.abs(previous))
            safe_size = jnp.where(size_now > 0.0, size_now, 1.0)
            current, previous = current / safe_size, previous / safe_size
            log_scale = log_scale + jnp.log(safe_size)
            scale = jnp.where(degree >= orders, jnp.exp(log_scale), 0.0)
    first, second = (
        jnp.concatenate(
            [values_ref[tile, pl.ds(i, degrees, stride=2), :] for tile in range(tiles)], axis=1
        )
        for i in range(2)
    )
    for m in range(per_device):
        analysis_ref[m * degrees : (m + 1) * degrees, :] = jnp.where(
            own[0:1] == m, first, 0.0
        ).astype(jnp.bfloat16)
    stacked = jnp.concatenate(
        [second[:, m * lat_total : (m + 1) * lat_total] for m in range(per_device)], axis=0
    )
    synthesis_ref[...] = stacked.T.astype(jnp.bfloat16)


def spectral_kernel(
    per_device,
    pieces_ref,
    analysis_ref,
    synthesis_ref,
    mine_ref,
    theirs_ref,
    out_ref,
    spectral_ref,
    chunk_ref,
):
    owners, chunk_rows, width = pieces_ref.shape
    channels, kept, columns = mine_ref.shape
    degrees = columns // per_device
    parts = 2 * per_device
    groups = chunk_rows // parts
    packed = width // kept
    bands = synthesis_ref.shape[0] // (groups * packed)

    pieces = pieces_ref[...].reshape(owners * chunk_rows, width)
    spectral = jnp.dot(analysis_ref[...], pieces, preferred_element_type=jnp.float32)
    spectral_ref[...] = spectral.T.astype(jnp.bfloat16).astype(jnp.float32)

    def add_channel(channel, totals):
        rows = [spectral_ref[pl.ds(part * channels + channel, 1), :] for part in range(2)]
        mine = mine_ref[channel].astype(jnp.float32)
        theirs = theirs_ref[channel].astype(jnp.float32)
        return (
            totals[0] + mine * rows[0],
            totals[1] + mine * rows[1],
            totals[2] + theirs * rows[0],
            totals[3] + theirs * rows[1],
        )

    zeros = jnp.zeros((kept, columns), jnp.float32)
    totals = lax.fori_loop(0, channels, add_channel, (zeros,) * 4, unroll=8)
    upper = lax.axis_index("lon") == 0
    mixed = [
        [jnp.where(upper, totals[part], totals[2 + part]) for part in range(2)],
        [jnp.where(upper, totals[2 + part], totals[part]) for part in range(2)],
    ]
    lane = lax.broadcasted_iota(jnp.int32, (kept, columns), 1)
    blocks = []
    for side in range(2):
        for m in range(per_device):
            own = (lane >= m * degrees) & (lane < (m + 1) * degrees)
            for part in range(2):
                blocks.append(jnp.where(own, mixed[side][part], 0.0).astype(jnp.bfloat16))
    values = lax.dot_general(
        synthesis_ref[...],
        jnp.concatenate(blocks, axis=0),
        (((1,), (1,)), ((), ())),
        preferred_element_type=jnp.float32,
    )
    for side in range(2):
        for group in range(groups):
            for part in range(parts):
                start = (side * parts + part) * kept
                pieces = [
                    values[(group * packed + i) * bands : (group * packed + i + 1) * bands, start : start + kept]
                    for i in range(packed)
                ]
                place = (side * groups + group) * parts + part
                chunk_ref[pl.ds(place, bands, stride=2 * groups * parts), :] = jnp.concatenate(
                    pieces, axis=1
                )
    out_ref[...] = chunk_ref[...].astype(jnp.bfloat16).reshape(out_ref.shape)


def inverse_kernel(per_device, pieces_ref, dft_ref, out_ref, pieces_32_ref, rows_ref):
    owners, chunk_rows, width = pieces_ref.shape
    kept, row_count, lon_total = out_ref.shape
    packed = width // kept
    parts = 2 * per_device
    pieces_32_ref[...] = pieces_ref[...].astype(jnp.float32).reshape(owners * chunk_rows, width)
    dft = dft_ref[...]
    place = lax.broadcasted_iota(jnp.int32, (2 * owners * per_device, width), 0)
    factor = jnp.where((place == 0) | (place == owners * per_device), 1.0, 2.0)
    for group in range(chunk_rows // parts):
        found = [
            pieces_32_ref[pl.ds(group * parts + 2 * m + part, owners, stride=chunk_rows), :]
            for part in range(2)
            for m in range(per_device)
        ]
        found = (jnp.concatenate(found, axis=0) * factor).astype(jnp.bfloat16)
        values = lax.dot_general(
            found, dft, (((0,), (0,)), ((), ())), preferred_element_type=jnp.float32
        )
        for i in range(packed):
            for tile in range(lon_total // LANES):
                rows_ref[tile, pl.ds(group * packed + i, kept, stride=row_count), :] = values[
                    i * kept : (i + 1) * kept, tile * LANES : (tile + 1) * LANES
                ]
    for tile in range(lon_total // LANES):
        out_ref[:, :, tile * LANES : (tile + 1) * LANES] = (
            rows_ref[tile].astype(jnp.bfloat16).reshape(kept, row_count, LANES)
        )


def local(fields, conv_first, conv_second, mixing):
    lat_count = lax.axis_size("lat")
    lon_count = lax.axis_size("lon")
    channels, row_count, lon_part = fields.shape
    lat_total = row_count * lat_count
    lon_total = lon_part * lon_count
    orders = lat_total // 2
    degrees = mixing.shape[0]
    owners = lat_count * lon_count
    per_device = orders // owners
    half = row_count // 2
    kept = channels // 2
    swap = [(0, 1), (1, 0)]
    both = ("lat", "lon")
    bfloat = functools.partial(jax.ShapeDtypeStruct, dtype=jnp.bfloat16)

    other = lax.ppermute(fields, "lon", swap)
    unpacked = pltpu.VMEM((lon_part // LANES, channels * row_count, LANES), jnp.float32)
    columns = per_device * degrees
    span = 32 if degrees % 32 == 0 else degrees
    width = lat_total * per_device
    arguments = [
        pltpu.with_memory_space_constraint(value, pltpu.HBM)
        for value in (
            fields,
            jnp.transpose(conv_first, (2, 3, 0, 1)),
            jnp.transpose(conv_second, (2, 3, 0, 1)),
        )
    ]
    own, taps_first, taps_second = call(
        load_kernel,
        (
            bfloat((row_count, channels, lon_part)),
            bfloat(arguments[1].shape),
            bfloat(arguments[2].shape),
        ),
        [pltpu.VMEM(fields.shape, jnp.bfloat16), unpacked, pltpu.SemaphoreType.DMA((3,))],
        [HBM] * 3,
        pl.CostEstimate(flops=1 << 16, bytes_accessed=1 << 21, transcendentals=0),
    )(*arguments)
    own, other, late_mixing = lax.optimization_barrier((own, other, mixing))
    other_mixing = lax.ppermute(late_mixing, "lon", swap)
    message = call(
        message_kernel,
        bfloat((2, channels, lon_total)),
        [unpacked],
        [VMEM, VMEM],
        pl.CostEstimate(flops=1 << 16, bytes_accessed=1 << 18, transcendentals=0),
    )(own, other)
    pairs = []
    for i in range(lat_count - 1):
        lower, upper = 2 * i + i % 2, 2 * (i + 1) + i % 2
        pairs += [(lower, upper), (upper, lower)]
    halo = lax.ppermute(message, both, pairs)

    taps = (3 * channels, 3 * channels)
    first, second, dft, near, interior = call(
        functools.partial(interior_kernel, lat_total, owners),
        (
            bfloat(taps),
            bfloat(taps),
            bfloat((2 * orders, lon_total)),
            bfloat((2, channels, lon_total)),
            jax.ShapeDtypeStruct((half - 2, orders, 2 * channels), jnp.float32),
        ),
        [
            unpacked,
            pltpu.VMEM((half + 2, channels, lon_total), jnp.bfloat16),
            pltpu.VMEM((half, channels, lon_total), jnp.bfloat16),
            pltpu.VMEM((half - 2, channels, lon_total), jnp.bfloat16),
        ],
        [VMEM, VMEM, VMEM, VMEM, ANY],
        pl.CostEstimate(flops=1 << 28, bytes_accessed=1 << 22, transcendentals=0),
    )(
        own,
        other,
        taps_first,
        taps_second,
        message,
    )

    def mixing_table(values, after):
        return call(
            functools.partial(mixing_kernel, per_device),
            bfloat((channels, kept, columns)),
            [],
            [VMEM, ANY],
            pl.CostEstimate(flops=1 << 20, bytes_accessed=1 << 22, transcendentals=0),
        )(values, after)

    mine = mixing_table(mixing, near)
    theirs = mixing_table(other_mixing, near)
    analysis, synthesis = call(
        functools.partial(legendre_kernel, span, lat_count, row_count, per_device),
        (bfloat((columns, width)), bfloat((lat_total, columns))),
        [pltpu.VMEM((width // LANES, 2 * degrees, LANES), jnp.float32)],
        [ANY],
        pl.CostEstimate(flops=1 << 20, bytes_accessed=1 << 21, transcendentals=0),
    )(near)
    coeffs = call(
        functools.partial(edge_kernel, lat_total, half),
        bfloat((owners, per_device * half, 2 * channels)),
        [
            pltpu.VMEM((4, channels, lon_total), jnp.bfloat16),
            pltpu.VMEM((4, channels, lon_total), jnp.bfloat16),
            pltpu.VMEM((2, channels, lon_total), jnp.bfloat16),
            pltpu.VMEM((orders * half, 2 * channels), jnp.float32),
        ],
        [VMEM] * 7 + [ANY] * 3,
        pl.CostEstimate(flops=1 << 26, bytes_accessed=1 << 20, transcendentals=0),
    )(halo, message, near, first, second, dft, interior, mine, theirs, analysis)
    pieces = lax.all_to_all(coeffs, both, split_axis=0, concat_axis=0, tiled=True)

    chunk_rows = row_count * 2 * per_device * kept // LANES
    chunks = call(
        functools.partial(spectral_kernel, per_device),
        bfloat((owners, chunk_rows, LANES)),
        [
            pltpu.VMEM((2 * channels, columns), jnp.float32),
            pltpu.VMEM((owners * chunk_rows, LANES), jnp.float32),
        ],
        [VMEM] * 5,
        pl.CostEstimate(flops=1 << 24, bytes_accessed=1 << 20, transcendentals=0),
    )(pieces, analysis, synthesis, mine, theirs)

    back = lax.all_to_all(chunks, both, split_axis=0, concat_axis=0, tiled=True)
    return call(
        functools.partial(inverse_kernel, per_device),
        bfloat((kept, row_count, lon_total)),
        [
            pltpu.VMEM((owners * chunk_rows, LANES), jnp.float32),
            pltpu.VMEM((lon_total // LANES, kept * row_count, LANES), jnp.float32),
        ],
        [VMEM] * 2,
        pl.CostEstimate(flops=1 << 24, bytes_accessed=1 << 19, transcendentals=0),
    )(back, dft)


def solution(mesh):
    in_specs = (P("groups", "lat", "lon"), P(), P(), P(None, "lon", None))
    out_specs = P(("groups", "lon"), "lat", None)
    return jax.shard_map(local, mesh=mesh, in_specs=in_specs, out_specs=out_specs, check_vma=False)
```

```python
import functools
import math

import jax
import jax.numpy as jnp
from jax import lax
from jax.experimental import pallas as pl
from jax.experimental.pallas import tpu as pltpu
from jax.sharding import PartitionSpec as P

VMEM = pl.BlockSpec(memory_space=pltpu.VMEM)
ANY = pl.BlockSpec(memory_space=pl.ANY)
HBM = pl.BlockSpec(memory_space=pltpu.HBM)
LIMIT = 40 * 1024 * 1024
LANES = 128


def call(kernel, out_shape, scratch, in_specs, cost):
    return pl.pallas_call(
        kernel,
        out_shape=out_shape,
        in_specs=in_specs,
        out_specs=jax.tree.map(lambda _: VMEM, out_shape),
        scratch_shapes=scratch,
        compiler_params=pltpu.CompilerParams(vmem_limit_bytes=LIMIT),
        cost_estimate=cost,
    )


def split_index(index, size):
    quotient = ((index.astype(jnp.float32) + 0.5) * (1.0 / size)).astype(jnp.int32)
    return quotient, index - quotient * size


def row_half():
    return (lax.axis_index("lat") + lax.axis_index("lon") + 1) & 1


def unpack_rows(source_ref, rows_ref):
    channels, row_count, lon_part = source_ref.shape
    for tile in range(lon_part // LANES):
        rows_ref[tile] = (
            source_ref[:, :, tile * LANES : (tile + 1) * LANES]
            .astype(jnp.float32)
            .reshape(channels * row_count, LANES)
        )


def packed_row(rows_ref, row, channels):
    tiles, count, _ = rows_ref.shape
    found = [
        rows_ref[tile, pl.ds(row, channels, stride=count // channels), :] for tile in range(tiles)
    ]
    return jnp.concatenate(found, axis=1).astype(jnp.bfloat16)


def load_kernel(
    fields_ref,
    conv_first_ref,
    conv_second_ref,
    own_ref,
    first_ref,
    second_ref,
    fields_copy_ref,
    rows_ref,
    arrived,
):
    copies = [
        pltpu.make_async_copy(source, target, arrived.at[i])
        for i, (source, target) in enumerate(
            (
                (fields_ref, fields_copy_ref),
                (conv_first_ref, first_ref),
                (conv_second_ref, second_ref),
            )
        )
    ]
    for copy in copies:
        copy.start()
    copies[0].wait()
    unpack_rows(fields_copy_ref, rows_ref)
    for row in range(own_ref.shape[0]):
        own_ref[row] = packed_row(rows_ref, row, own_ref.shape[1])
    for copy in copies[1:]:
        copy.wait()


def place_row(out_ref, place, side, mine, theirs):
    lon_part = mine.shape[1]
    for position, values in ((side, mine), (1 - side, theirs)):
        start = pl.multiple_of(position * lon_part, LANES)
        out_ref[place, :, pl.ds(start, lon_part)] = values


def message_kernel(own_ref, other_ref, out_ref, rows_ref):
    row_count, channels, _ = own_ref.shape
    side = lax.axis_index("lon")
    unpack_rows(other_ref, rows_ref)
    for i in range(2):
        row = row_half() * (row_count - 2) + i
        place_row(out_ref, i, side, own_ref[row], packed_row(rows_ref, row, channels))


def layer(source_ref, weights, row):
    channels, lon_total = source_ref.shape[1:]
    taps = source_ref[row : row + 3].reshape(3 * channels, lon_total)
    sums = jnp.dot(weights, taps, preferred_element_type=jnp.float32)
    total = (
        sums[channels : 2 * channels]
        + pltpu.roll(sums[:channels], 1, 1)
        + pltpu.roll(sums[2 * channels :], lon_total - 1, 1)
    )
    return jnp.maximum(total, 0.0)


def row_weight(row, lat_total, lon_total):
    place = jnp.full((1, LANES), row, jnp.int32).astype(jnp.float32)
    return jnp.sin((place + 0.5) * (math.pi / lat_total)) * (math.pi / lat_total / lon_total)


def row_spectra(dft, hidden, first_row, lat_total):
    count, channels, lon_total = hidden.shape
    spectra = lax.dot_general(
        dft,
        hidden.reshape(count * channels, lon_total),
        (((1,), (1,)), ((), ())),
        preferred_element_type=jnp.float32,
    )
    orders = spectra.shape[0] // 2
    found = []
    for i in range(count):
        columns = slice(i * channels, (i + 1) * channels)
        parts = jnp.concatenate([spectra[:orders, columns], spectra[orders:, columns]], axis=1)
        found.append(parts * row_weight(first_row + i, lat_total, lon_total))
    return found


def interior_kernel(
    lat_total,
    owners,
    own_ref,
    other_ref,
    first_ref,
    second_ref,
    after_ref,
    first_out,
    second_out,
    dft_out,
    near_out,
    coeffs_out,
    rows_ref,
    band_ref,
    mid_ref,
    hidden_ref,
):
    del after_ref
    row_count, channels, lon_part = own_ref.shape
    lon_total = 2 * lon_part
    half = row_count // 2
    side, part = lax.axis_index("lon"), row_half()
    for source, target in ((first_ref, first_out), (second_ref, second_out)):
        for b in range(3):
            target[b * channels : (b + 1) * channels, :] = jnp.concatenate(
                [source[a, b] for a in range(3)], axis=1
            )
    orders = dft_out.shape[0] // 2
    place = lax.broadcasted_iota(jnp.int32, (orders, lon_total), 0)
    order, owner = split_index(place, owners)
    waves = owner * (orders // owners) + order
    points = lax.broadcasted_iota(jnp.int32, (orders, lon_total), 1)
    angle = ((waves * points) & (lon_total - 1)).astype(jnp.float32) * (2.0 * math.pi / lon_total)
    dft_out[:orders, :] = jnp.cos(angle).astype(jnp.bfloat16)
    dft_out[orders:, :] = (-jnp.sin(angle)).astype(jnp.bfloat16)
    unpack_rows(other_ref, rows_ref)
    for i in range(half + 2):
        row = 2 * part + i
        place_row(band_ref, i, side, own_ref[row], packed_row(rows_ref, row, channels))
    weights = first_out[...]
    for i in range(half):
        mid_ref[i] = layer(band_ref, weights, i).astype(jnp.bfloat16)
    near_out[...] = mid_ref[pl.ds((half - 2) * part, 2)]
    weights = second_out[...]
    for i in range(half - 2):
        hidden_ref[i] = layer(mid_ref, weights, i).astype(jnp.bfloat16)
    first_row = lax.axis_index("lat") * row_count + part * half + 2 * (1 - part)
    found = row_spectra(dft_out[...], hidden_ref[...], first_row, lat_total)
    for i, values in enumerate(found):
        coeffs_out[i] = values


def edge_kernel(
    lat_total,
    half,
    halo_ref,
    message_ref,
    near_ref,
    first_ref,
    second_ref,
    dft_ref,
    coeffs_ref,
    mine_ref,
    analysis_ref,
    out_ref,
    band_ref,
    mid_ref,
    hidden_ref,
    packed_ref,
):
    del mine_ref, analysis_ref
    part = row_half()
    first_row = lax.axis_index("lat") * (2 * half) + part * half
    band_ref[pl.ds(2 * part, 2)] = halo_ref[...]
    band_ref[pl.ds(2 - 2 * part, 2)] = message_ref[...]
    mid_ref[pl.ds(2 - 2 * part, 2)] = near_ref[...]
    weights = first_ref[...]
    for i in range(2):
        place = first_row - 1 + part * half + i
        values = layer(band_ref, weights, i)
        values = jnp.where((place >= 0) & (place < lat_total), values, 0.0)
        mid_ref[2 * part + i] = values.astype(jnp.bfloat16)
    weights = second_ref[...]
    for i in range(2):
        hidden_ref[i] = layer(mid_ref, weights, i).astype(jnp.bfloat16)
    edge = part * (half - 2)
    found = row_spectra(dft_ref[...], hidden_ref[...], first_row + edge, lat_total)
    owners, chunk_rows, _ = out_ref.shape
    for m in range(chunk_rows // half):
        own = slice(m * owners, (m + 1) * owners)
        for i in range(2):
            start = m * half + edge + i
            packed_ref[pl.ds(start, owners, stride=chunk_rows), :] = found[i][own]
        for i in range(half - 2):
            start = m * half + 2 - 2 * part + i
            packed_ref[pl.ds(start, owners, stride=chunk_rows), :] = coeffs_ref[i, own]
    out_ref[...] = packed_ref[...].astype(jnp.bfloat16).reshape(out_ref.shape)


def mixing_kernel(per_device, mixing_ref, after_ref, out_ref):
    del after_ref
    values = jnp.transpose(mixing_ref[...].astype(jnp.float32), (1, 0, 2))
    blocks = [
        jnp.concatenate([values[o]] * per_device, axis=0).T for o in range(values.shape[0])
    ]
    out_ref[...] = jnp.transpose(jnp.stack(blocks), (1, 0, 2)).astype(jnp.bfloat16)


def legendre_kernel(
    span, bands, row_count, per_device, after_ref, analysis_ref, synthesis_ref, values_ref
):
    del after_ref
    tiles, count, _ = values_ref.shape
    degrees, width = count // 2, tiles * LANES
    lat_total = bands * row_count
    half = row_count // 2
    first_order = (2 * lax.axis_index("lat") + lax.axis_index("lon")) * per_device
    lane = lax.broadcasted_iota(jnp.int32, (2, width), 1)
    form = lax.broadcasted_iota(jnp.int32, (2, width), 0)
    rest, low = split_index(lane, half)
    device, own_first = split_index(rest, per_device)
    rest, band = split_index(lane, bands)
    own_second, inner = split_index(rest, row_count)
    own = jnp.where(form == 0, own_first, own_second)
    place = (device >> 1) * row_count + (((device >> 1) + device + 1) & 1) * half + low
    row = jnp.where(form == 0, place, band * row_count + inner)
    south = row >= lat_total // 2
    row = jnp.where(south, lat_total - 1 - row, row)
    colatitude = (row.astype(jnp.float32) + 0.5) * (math.pi / lat_total)
    cosine, sine_theta = jnp.cos(colatitude), jnp.sin(colatitude)
    order_ids = first_order + own
    orders = order_ids.astype(jnp.float32)
    counter = 1.0 + lax.broadcasted_iota(jnp.int32, (1, max(degrees, LANES)), 1).astype(jnp.float32)
    log_terms = jnp.log((2.0 * counter - 1.0) / (2.0 * counter))
    log_start = 0.5 * jnp.log(orders + 0.5) + orders * jnp.log(sine_theta)
    for m in range(per_device):
        below = counter <= jnp.full(counter.shape, first_order + m, jnp.int32).astype(jnp.float32)
        total = jnp.sum(jnp.where(below, log_terms, 0.0), axis=1, keepdims=True)
        log_start = log_start + jnp.where(own == m, 0.5 * total, 0.0)
    parity = (1 - 2 * (order_ids & 1)).astype(jnp.float32)
    even_sign, odd_sign = jnp.where(south, parity, 1.0), jnp.where(south, -parity, 1.0)
    orders_squared = orders * orders
    start_scale = jnp.exp(log_start)
    current = previous = scale = log_scale = jnp.zeros_like(cosine)
    root = jnp.zeros_like(cosine)
    for degree in range(degrees):
        distance = float(degree * degree) - orders_squared
        inverse_root = lax.rsqrt(jnp.maximum(distance, 1.0))
        above = math.sqrt(max(4.0 * degree * degree - 1.0, 1.0))
        below = math.sqrt(max(4.0 * (degree - 1) * (degree - 1) - 1.0, 1.0))
        newest = (above * inverse_root) * (cosine * current - (root * (1.0 / below)) * previous)
        root = jnp.maximum(distance, 0.0) * inverse_root
        is_start = orders == float(degree)
        newest = jnp.where(is_start, 1.0, newest)
        scale = jnp.where(is_start, start_scale, scale)
        log_scale = jnp.where(is_start, log_start, log_scale)
        previous, current = current, newest
        emitted = newest * scale * (even_sign if degree % 2 == 0 else odd_sign)
        for tile in range(tiles):
            values_ref[tile, 2 * degree : 2 * degree + 2, :] = emitted[
                :, tile * LANES : (tile + 1) * LANES
            ]
        if degree % span == span - 1 and degree < degrees - 1:
            size_now = jnp.maximum(jnp.abs(current), jnp.abs(previous))
            safe_size = jnp.where(size_now > 0.0, size_now, 1.0)
            current, previous = current / safe_size, previous / safe_size
            log_scale = log_scale + jnp.log(safe_size)
            scale = jnp.where(degree >= orders, jnp.exp(log_scale), 0.0)
    first, second = (
        jnp.concatenate(
            [values_ref[tile, pl.ds(i, degrees, stride=2), :] for tile in range(tiles)], axis=1
        )
        for i in range(2)
    )
    for m in range(per_device):
        analysis_ref[m * degrees : (m + 1) * degrees, :] = jnp.where(
            own[0:1] == m, first, 0.0
        ).astype(jnp.bfloat16)
    stacked = jnp.concatenate(
        [second[:, m * lat_total : (m + 1) * lat_total] for m in range(per_device)], axis=0
    )
    synthesis_ref[...] = stacked.T.astype(jnp.bfloat16)


def spectral_kernel(
    per_device,
    pieces_ref,
    analysis_ref,
    synthesis_ref,
    mine_ref,
    theirs_ref,
    out_ref,
    spectral_ref,
    chunk_ref,
):
    owners, chunk_rows, width = pieces_ref.shape
    channels, kept, columns = mine_ref.shape
    degrees = columns // per_device
    parts = 2 * per_device
    groups = chunk_rows // parts
    packed = width // kept
    bands = synthesis_ref.shape[0] // (groups * packed)

    pieces = pieces_ref[...].reshape(owners * chunk_rows, width)
    spectral = jnp.dot(analysis_ref[...], pieces, preferred_element_type=jnp.float32)
    spectral_ref[...] = spectral.T.astype(jnp.bfloat16).astype(jnp.float32)

    def add_channel(channel, totals):
        rows = [spectral_ref[pl.ds(part * channels + channel, 1), :] for part in range(2)]
        mine = mine_ref[channel].astype(jnp.float32)
        theirs = theirs_ref[channel].astype(jnp.float32)
        return (
            totals[0] + mine * rows[0],
            totals[1] + mine * rows[1],
            totals[2] + theirs * rows[0],
            totals[3] + theirs * rows[1],
        )

    zeros = jnp.zeros((kept, columns), jnp.float32)
    totals = lax.fori_loop(0, channels, add_channel, (zeros,) * 4, unroll=8)
    upper = lax.axis_index("lon") == 0
    mixed = [
        [jnp.where(upper, totals[part], totals[2 + part]) for part in range(2)],
        [jnp.where(upper, totals[2 + part], totals[part]) for part in range(2)],
    ]
    lane = lax.broadcasted_iota(jnp.int32, (kept, columns), 1)
    blocks = []
    for side in range(2):
        for m in range(per_device):
            own = (lane >= m * degrees) & (lane < (m + 1) * degrees)
            for part in range(2):
                blocks.append(jnp.where(own, mixed[side][part], 0.0).astype(jnp.bfloat16))
    values = lax.dot_general(
        synthesis_ref[...],
        jnp.concatenate(blocks, axis=0),
        (((1,), (1,)), ((), ())),
        preferred_element_type=jnp.float32,
    )
    for side in range(2):
        for group in range(groups):
            for part in range(parts):
                start = (side * parts + part) * kept
                pieces = [
                    values[(group * packed + i) * bands : (group * packed + i + 1) * bands, start : start + kept]
                    for i in range(packed)
                ]
                place = (side * groups + group) * parts + part
                chunk_ref[pl.ds(place, bands, stride=2 * groups * parts), :] = jnp.concatenate(
                    pieces, axis=1
                )
    out_ref[...] = chunk_ref[...].astype(jnp.bfloat16).reshape(out_ref.shape)


def inverse_kernel(per_device, pieces_ref, dft_ref, out_ref, pieces_32_ref, rows_ref):
    owners, chunk_rows, width = pieces_ref.shape
    kept, row_count, lon_total = out_ref.shape
    packed = width // kept
    parts = 2 * per_device
    pieces_32_ref[...] = pieces_ref[...].astype(jnp.float32).reshape(owners * chunk_rows, width)
    dft = dft_ref[...]
    place = lax.broadcasted_iota(jnp.int32, (2 * owners * per_device, width), 0)
    factor = jnp.where((place == 0) | (place == owners * per_device), 1.0, 2.0)
    for group in range(chunk_rows // parts):
        found = [
            pieces_32_ref[pl.ds(group * parts + 2 * m + part, owners, stride=chunk_rows), :]
            for part in range(2)
            for m in range(per_device)
        ]
        found = (jnp.concatenate(found, axis=0) * factor).astype(jnp.bfloat16)
        values = lax.dot_general(
            found, dft, (((0,), (0,)), ((), ())), preferred_element_type=jnp.float32
        )
        for i in range(packed):
            for tile in range(lon_total // LANES):
                rows_ref[tile, pl.ds(group * packed + i, kept, stride=row_count), :] = values[
                    i * kept : (i + 1) * kept, tile * LANES : (tile + 1) * LANES
                ]
    for tile in range(lon_total // LANES):
        out_ref[:, :, tile * LANES : (tile + 1) * LANES] = (
            rows_ref[tile].astype(jnp.bfloat16).reshape(kept, row_count, LANES)
        )


def local(fields, conv_first, conv_second, mixing):
    lat_count = lax.axis_size("lat")
    lon_count = lax.axis_size("lon")
    channels, row_count, lon_part = fields.shape
    lat_total = row_count * lat_count
    lon_total = lon_part * lon_count
    orders = lat_total // 2
    degrees = mixing.shape[0]
    owners = lat_count * lon_count
    per_device = orders // owners
    half = row_count // 2
    kept = channels // 2
    swap = [(0, 1), (1, 0)]
    both = ("lat", "lon")
    bfloat = functools.partial(jax.ShapeDtypeStruct, dtype=jnp.bfloat16)

    other = lax.ppermute(fields, "lon", swap)
    unpacked = pltpu.VMEM((lon_part // LANES, channels * row_count, LANES), jnp.float32)
    columns = per_device * degrees
    span = 32 if degrees % 32 == 0 else degrees
    width = lat_total * per_device
    arguments = [
        pltpu.with_memory_space_constraint(value, pltpu.HBM)
        for value in (
            fields,
            jnp.transpose(conv_first, (2, 3, 0, 1)),
            jnp.transpose(conv_second, (2, 3, 0, 1)),
        )
    ]
    own, taps_first, taps_second = call(
        load_kernel,
        (
            bfloat((row_count, channels, lon_part)),
            bfloat(arguments[1].shape),
            bfloat(arguments[2].shape),
        ),
        [pltpu.VMEM(fields.shape, jnp.bfloat16), unpacked, pltpu.SemaphoreType.DMA((3,))],
        [HBM] * 3,
        pl.CostEstimate(flops=1 << 16, bytes_accessed=1 << 21, transcendentals=0),
    )(*arguments)
    message = call(
        message_kernel,
        bfloat((2, channels, lon_total)),
        [unpacked],
        [VMEM, VMEM],
        pl.CostEstimate(flops=1 << 16, bytes_accessed=1 << 18, transcendentals=0),
    )(own, other)
    pairs = []
    for i in range(lat_count - 1):
        lower, upper = 2 * i + i % 2, 2 * (i + 1) + i % 2
        pairs += [(lower, upper), (upper, lower)]
    halo = lax.ppermute(message, both, pairs)

    taps = (3 * channels, 3 * channels)
    first, second, dft, near, interior = call(
        functools.partial(interior_kernel, lat_total, owners),
        (
            bfloat(taps),
            bfloat(taps),
            bfloat((2 * orders, lon_total)),
            bfloat((2, channels, lon_total)),
            jax.ShapeDtypeStruct((half - 2, orders, 2 * channels), jnp.float32),
        ),
        [
            unpacked,
            pltpu.VMEM((half + 2, channels, lon_total), jnp.bfloat16),
            pltpu.VMEM((half, channels, lon_total), jnp.bfloat16),
            pltpu.VMEM((half - 2, channels, lon_total), jnp.bfloat16),
        ],
        [VMEM, VMEM, VMEM, VMEM, ANY],
        pl.CostEstimate(flops=1 << 28, bytes_accessed=1 << 22, transcendentals=0),
    )(
        own,
        other,
        taps_first,
        taps_second,
        message,
    )

    def mixing_table(values, after):
        return call(
            functools.partial(mixing_kernel, per_device),
            bfloat((channels, kept, columns)),
            [],
            [VMEM, ANY],
            pl.CostEstimate(flops=1 << 20, bytes_accessed=1 << 22, transcendentals=0),
        )(values, after)

    mine = mixing_table(mixing, near)
    analysis, synthesis = call(
        functools.partial(legendre_kernel, span, lat_count, row_count, per_device),
        (bfloat((columns, width)), bfloat((lat_total, columns))),
        [pltpu.VMEM((width // LANES, 2 * degrees, LANES), jnp.float32)],
        [ANY],
        pl.CostEstimate(flops=1 << 20, bytes_accessed=1 << 21, transcendentals=0),
    )(near)
    coeffs = call(
        functools.partial(edge_kernel, lat_total, half),
        bfloat((owners, per_device * half, 2 * channels)),
        [
            pltpu.VMEM((4, channels, lon_total), jnp.bfloat16),
            pltpu.VMEM((4, channels, lon_total), jnp.bfloat16),
            pltpu.VMEM((2, channels, lon_total), jnp.bfloat16),
            pltpu.VMEM((orders * half, 2 * channels), jnp.float32),
        ],
        [VMEM] * 7 + [ANY] * 2,
        pl.CostEstimate(flops=1 << 26, bytes_accessed=1 << 20, transcendentals=0),
    )(halo, message, near, first, second, dft, interior, mine, analysis)
    coeffs, late_mine = lax.optimization_barrier((coeffs, mine))
    theirs = lax.ppermute(late_mine, "lon", swap)
    pieces = lax.all_to_all(coeffs, both, split_axis=0, concat_axis=0, tiled=True)

    chunk_rows = row_count * 2 * per_device * kept // LANES
    chunks = call(
        functools.partial(spectral_kernel, per_device),
        bfloat((owners, chunk_rows, LANES)),
        [
            pltpu.VMEM((2 * channels, columns), jnp.float32),
            pltpu.VMEM((owners * chunk_rows, LANES), jnp.float32),
        ],
        [VMEM] * 5,
        pl.CostEstimate(flops=1 << 24, bytes_accessed=1 << 20, transcendentals=0),
    )(pieces, analysis, synthesis, mine, theirs)

    back = lax.all_to_all(chunks, both, split_axis=0, concat_axis=0, tiled=True)
    return call(
        functools.partial(inverse_kernel, per_device),
        bfloat((kept, row_count, lon_total)),
        [
            pltpu.VMEM((owners * chunk_rows, LANES), jnp.float32),
            pltpu.VMEM((lon_total // LANES, kept * row_count, LANES), jnp.float32),
        ],
        [VMEM] * 2,
        pl.CostEstimate(flops=1 << 24, bytes_accessed=1 << 19, transcendentals=0),
    )(back, dft)


def solution(mesh):
    in_specs = (P("groups", "lat", "lon"), P(), P(), P(None, "lon", None))
    out_specs = P(("groups", "lon"), "lat", None)
    return jax.shard_map(local, mesh=mesh, in_specs=in_specs, out_specs=out_specs, check_vma=False)
```

```python
import functools
import math

import jax
import jax.numpy as jnp
from jax import lax
from jax.experimental import pallas as pl
from jax.experimental.pallas import tpu as pltpu
from jax.sharding import PartitionSpec as P

VMEM = pl.BlockSpec(memory_space=pltpu.VMEM)
ANY = pl.BlockSpec(memory_space=pl.ANY)
HBM = pl.BlockSpec(memory_space=pltpu.HBM)
LIMIT = 40 * 1024 * 1024
LANES = 128


def call(kernel, out_shape, scratch, in_specs, cost):
    return pl.pallas_call(
        kernel,
        out_shape=out_shape,
        in_specs=in_specs,
        out_specs=jax.tree.map(lambda _: VMEM, out_shape),
        scratch_shapes=scratch,
        compiler_params=pltpu.CompilerParams(vmem_limit_bytes=LIMIT),
        cost_estimate=cost,
    )


def split_index(index, size):
    quotient = ((index.astype(jnp.float32) + 0.5) * (1.0 / size)).astype(jnp.int32)
    return quotient, index - quotient * size


def row_half():
    return (lax.axis_index("lat") + lax.axis_index("lon") + 1) & 1


def unpack_rows(source_ref, rows_ref):
    channels, row_count, lon_part = source_ref.shape
    for tile in range(lon_part // LANES):
        rows_ref[tile] = (
            source_ref[:, :, tile * LANES : (tile + 1) * LANES]
            .astype(jnp.float32)
            .reshape(channels * row_count, LANES)
        )


def packed_row(rows_ref, row, channels):
    tiles, count, _ = rows_ref.shape
    found = [
        rows_ref[tile, pl.ds(row, channels, stride=count // channels), :] for tile in range(tiles)
    ]
    return jnp.concatenate(found, axis=1).astype(jnp.bfloat16)


def load_kernel(
    fields_ref,
    conv_first_ref,
    conv_second_ref,
    own_ref,
    first_ref,
    second_ref,
    fields_copy_ref,
    rows_ref,
    arrived,
):
    copies = [
        pltpu.make_async_copy(source, target, arrived.at[i])
        for i, (source, target) in enumerate(
            (
                (fields_ref, fields_copy_ref),
                (conv_first_ref, first_ref),
                (conv_second_ref, second_ref),
            )
        )
    ]
    for copy in copies:
        copy.start()
    copies[0].wait()
    unpack_rows(fields_copy_ref, rows_ref)
    for row in range(own_ref.shape[0]):
        own_ref[row] = packed_row(rows_ref, row, own_ref.shape[1])
    for copy in copies[1:]:
        copy.wait()


def place_row(out_ref, place, side, mine, theirs):
    lon_part = mine.shape[1]
    for position, values in ((side, mine), (1 - side, theirs)):
        start = pl.multiple_of(position * lon_part, LANES)
        out_ref[place, :, pl.ds(start, lon_part)] = values


def message_kernel(own_ref, other_ref, out_ref, rows_ref):
    row_count, channels, _ = own_ref.shape
    side = lax.axis_index("lon")
    unpack_rows(other_ref, rows_ref)
    for i in range(2):
        row = row_half() * (row_count - 2) + i
        place_row(out_ref, i, side, own_ref[row], packed_row(rows_ref, row, channels))


def layer(source_ref, weights, row):
    channels, lon_total = source_ref.shape[1:]
    taps = source_ref[row : row + 3].reshape(3 * channels, lon_total)
    sums = jnp.dot(weights, taps, preferred_element_type=jnp.float32)
    total = (
        sums[channels : 2 * channels]
        + pltpu.roll(sums[:channels], 1, 1)
        + pltpu.roll(sums[2 * channels :], lon_total - 1, 1)
    )
    return jnp.maximum(total, 0.0)


def row_weight(row, lat_total, lon_total):
    place = jnp.full((1, LANES), row, jnp.int32).astype(jnp.float32)
    return jnp.sin((place + 0.5) * (math.pi / lat_total)) * (math.pi / lat_total / lon_total)


def row_spectra(dft, hidden, first_row, lat_total):
    count, channels, lon_total = hidden.shape
    spectra = lax.dot_general(
        dft,
        hidden.reshape(count * channels, lon_total),
        (((1,), (1,)), ((), ())),
        preferred_element_type=jnp.float32,
    )
    orders = spectra.shape[0] // 2
    found = []
    for i in range(count):
        columns = slice(i * channels, (i + 1) * channels)
        parts = jnp.concatenate([spectra[:orders, columns], spectra[orders:, columns]], axis=1)
        found.append(parts * row_weight(first_row + i, lat_total, lon_total))
    return found


def interior_kernel(
    lat_total,
    owners,
    own_ref,
    other_ref,
    first_ref,
    second_ref,
    after_ref,
    first_out,
    second_out,
    dft_out,
    near_out,
    coeffs_out,
    rows_ref,
    band_ref,
    mid_ref,
    hidden_ref,
):
    del after_ref
    row_count, channels, lon_part = own_ref.shape
    lon_total = 2 * lon_part
    half = row_count // 2
    side, part = lax.axis_index("lon"), row_half()
    for source, target in ((first_ref, first_out), (second_ref, second_out)):
        for b in range(3):
            target[b * channels : (b + 1) * channels, :] = jnp.concatenate(
                [source[a, b] for a in range(3)], axis=1
            )
    orders = dft_out.shape[0] // 2
    place = lax.broadcasted_iota(jnp.int32, (orders, lon_total), 0)
    order, owner = split_index(place, owners)
    waves = owner * (orders // owners) + order
    points = lax.broadcasted_iota(jnp.int32, (orders, lon_total), 1)
    angle = ((waves * points) & (lon_total - 1)).astype(jnp.float32) * (2.0 * math.pi / lon_total)
    dft_out[:orders, :] = jnp.cos(angle).astype(jnp.bfloat16)
    dft_out[orders:, :] = (-jnp.sin(angle)).astype(jnp.bfloat16)
    unpack_rows(other_ref, rows_ref)
    for i in range(half + 2):
        row = 2 * part + i
        place_row(band_ref, i, side, own_ref[row], packed_row(rows_ref, row, channels))
    weights = first_out[...]
    for i in range(half):
        mid_ref[i] = layer(band_ref, weights, i).astype(jnp.bfloat16)
    near_out[...] = mid_ref[pl.ds((half - 2) * part, 2)]
    weights = second_out[...]
    for i in range(half - 2):
        hidden_ref[i] = layer(mid_ref, weights, i).astype(jnp.bfloat16)
    first_row = lax.axis_index("lat") * row_count + part * half + 2 * (1 - part)
    found = row_spectra(dft_out[...], hidden_ref[...], first_row, lat_total)
    for i, values in enumerate(found):
        coeffs_out[i] = values


def edge_kernel(
    lat_total,
    half,
    halo_ref,
    message_ref,
    near_ref,
    first_ref,
    second_ref,
    dft_ref,
    coeffs_ref,
    mine_ref,
    analysis_ref,
    out_ref,
    band_ref,
    mid_ref,
    hidden_ref,
    packed_ref,
):
    del mine_ref, analysis_ref
    part = row_half()
    first_row = lax.axis_index("lat") * (2 * half) + part * half
    band_ref[pl.ds(2 * part, 2)] = halo_ref[...]
    band_ref[pl.ds(2 - 2 * part, 2)] = message_ref[...]
    mid_ref[pl.ds(2 - 2 * part, 2)] = near_ref[...]
    weights = first_ref[...]
    for i in range(2):
        place = first_row - 1 + part * half + i
        values = layer(band_ref, weights, i)
        values = jnp.where((place >= 0) & (place < lat_total), values, 0.0)
        mid_ref[2 * part + i] = values.astype(jnp.bfloat16)
    weights = second_ref[...]
    for i in range(2):
        hidden_ref[i] = layer(mid_ref, weights, i).astype(jnp.bfloat16)
    edge = part * (half - 2)
    found = row_spectra(dft_ref[...], hidden_ref[...], first_row + edge, lat_total)
    owners, chunk_rows, _ = out_ref.shape
    for m in range(chunk_rows // half):
        own = slice(m * owners, (m + 1) * owners)
        for i in range(2):
            start = m * half + edge + i
            packed_ref[pl.ds(start, owners, stride=chunk_rows), :] = found[i][own]
        for i in range(half - 2):
            start = m * half + 2 - 2 * part + i
            packed_ref[pl.ds(start, owners, stride=chunk_rows), :] = coeffs_ref[i, own]
    out_ref[...] = packed_ref[...].astype(jnp.bfloat16).reshape(out_ref.shape)


def mixing_kernel(per_device, mixing_ref, after_ref, out_ref):
    del after_ref
    values = jnp.transpose(mixing_ref[...].astype(jnp.float32), (1, 0, 2))
    blocks = [
        jnp.concatenate([values[o]] * per_device, axis=0).T for o in range(values.shape[0])
    ]
    out_ref[...] = jnp.transpose(jnp.stack(blocks), (1, 0, 2))


def legendre_kernel(
    span, bands, row_count, per_device, after_ref, analysis_ref, synthesis_ref, values_ref
):
    del after_ref
    tiles, count, _ = values_ref.shape
    degrees, width = count // 2, tiles * LANES
    lat_total = bands * row_count
    half = row_count // 2
    first_order = (2 * lax.axis_index("lat") + lax.axis_index("lon")) * per_device
    lane = lax.broadcasted_iota(jnp.int32, (2, width), 1)
    form = lax.broadcasted_iota(jnp.int32, (2, width), 0)
    rest, low = split_index(lane, half)
    device, own_first = split_index(rest, per_device)
    rest, band = split_index(lane, bands)
    own_second, inner = split_index(rest, row_count)
    own = jnp.where(form == 0, own_first, own_second)
    place = (device >> 1) * row_count + (((device >> 1) + device + 1) & 1) * half + low
    row = jnp.where(form == 0, place, band * row_count + inner)
    south = row >= lat_total // 2
    row = jnp.where(south, lat_total - 1 - row, row)
    colatitude = (row.astype(jnp.float32) + 0.5) * (math.pi / lat_total)
    cosine, sine_theta = jnp.cos(colatitude), jnp.sin(colatitude)
    order_ids = first_order + own
    orders = order_ids.astype(jnp.float32)
    counter = 1.0 + lax.broadcasted_iota(jnp.int32, (1, max(degrees, LANES)), 1).astype(jnp.float32)
    log_terms = jnp.log((2.0 * counter - 1.0) / (2.0 * counter))
    log_start = 0.5 * jnp.log(orders + 0.5) + orders * jnp.log(sine_theta)
    for m in range(per_device):
        below = counter <= jnp.full(counter.shape, first_order + m, jnp.int32).astype(jnp.float32)
        total = jnp.sum(jnp.where(below, log_terms, 0.0), axis=1, keepdims=True)
        log_start = log_start + jnp.where(own == m, 0.5 * total, 0.0)
    parity = (1 - 2 * (order_ids & 1)).astype(jnp.float32)
    even_sign, odd_sign = jnp.where(south, parity, 1.0), jnp.where(south, -parity, 1.0)
    orders_squared = orders * orders
    start_scale = jnp.exp(log_start)
    current = previous = scale = log_scale = jnp.zeros_like(cosine)
    root = jnp.zeros_like(cosine)
    for degree in range(degrees):
        distance = float(degree * degree) - orders_squared
        inverse_root = lax.rsqrt(jnp.maximum(distance, 1.0))
        above = math.sqrt(max(4.0 * degree * degree - 1.0, 1.0))
        below = math.sqrt(max(4.0 * (degree - 1) * (degree - 1) - 1.0, 1.0))
        newest = (above * inverse_root) * (cosine * current - (root * (1.0 / below)) * previous)
        root = jnp.maximum(distance, 0.0) * inverse_root
        is_start = orders == float(degree)
        newest = jnp.where(is_start, 1.0, newest)
        scale = jnp.where(is_start, start_scale, scale)
        log_scale = jnp.where(is_start, log_start, log_scale)
        previous, current = current, newest
        emitted = newest * scale * (even_sign if degree % 2 == 0 else odd_sign)
        for tile in range(tiles):
            values_ref[tile, 2 * degree : 2 * degree + 2, :] = emitted[
                :, tile * LANES : (tile + 1) * LANES
            ]
        if degree % span == span - 1 and degree < degrees - 1:
            size_now = jnp.maximum(jnp.abs(current), jnp.abs(previous))
            safe_size = jnp.where(size_now > 0.0, size_now, 1.0)
            current, previous = current / safe_size, previous / safe_size
            log_scale = log_scale + jnp.log(safe_size)
            scale = jnp.where(degree >= orders, jnp.exp(log_scale), 0.0)
    first, second = (
        jnp.concatenate(
            [values_ref[tile, pl.ds(i, degrees, stride=2), :] for tile in range(tiles)], axis=1
        )
        for i in range(2)
    )
    for m in range(per_device):
        analysis_ref[m * degrees : (m + 1) * degrees, :] = jnp.where(
            own[0:1] == m, first, 0.0
        ).astype(jnp.bfloat16)
    stacked = jnp.concatenate(
        [second[:, m * lat_total : (m + 1) * lat_total] for m in range(per_device)], axis=0
    )
    synthesis_ref[...] = stacked.T.astype(jnp.bfloat16)


def spectral_kernel(
    per_device,
    pieces_ref,
    analysis_ref,
    synthesis_ref,
    mine_ref,
    theirs_ref,
    out_ref,
    spectral_ref,
    chunk_ref,
):
    owners, chunk_rows, width = pieces_ref.shape
    channels, kept, columns = mine_ref.shape
    degrees = columns // per_device
    parts = 2 * per_device
    groups = chunk_rows // parts
    packed = width // kept
    bands = synthesis_ref.shape[0] // (groups * packed)

    pieces = pieces_ref[...].reshape(owners * chunk_rows, width)
    spectral = lax.dot_general(
        pieces, analysis_ref[...], (((0,), (1,)), ((), ())), preferred_element_type=jnp.float32
    )
    spectral_ref[...] = spectral.astype(jnp.bfloat16).astype(jnp.float32)

    def add_channel(channel, totals):
        rows = [spectral_ref[pl.ds(part * channels + channel, 1), :] for part in range(2)]
        mine, theirs = mine_ref[channel], theirs_ref[channel]
        return (
            totals[0] + mine * rows[0],
            totals[1] + mine * rows[1],
            totals[2] + theirs * rows[0],
            totals[3] + theirs * rows[1],
        )

    zeros = jnp.zeros((kept, columns), jnp.float32)
    totals = lax.fori_loop(0, channels, add_channel, (zeros,) * 4, unroll=64)
    upper = lax.axis_index("lon") == 0
    mixed = [
        [jnp.where(upper, totals[part], totals[2 + part]) for part in range(2)],
        [jnp.where(upper, totals[2 + part], totals[part]) for part in range(2)],
    ]
    lane = lax.broadcasted_iota(jnp.int32, (kept, columns), 1)
    blocks = []
    for side in range(2):
        for m in range(per_device):
            own = (lane >= m * degrees) & (lane < (m + 1) * degrees)
            for part in range(2):
                blocks.append(jnp.where(own, mixed[side][part], 0.0).astype(jnp.bfloat16))
    values = lax.dot_general(
        synthesis_ref[...],
        jnp.concatenate(blocks, axis=0),
        (((1,), (1,)), ((), ())),
        preferred_element_type=jnp.float32,
    )
    for side in range(2):
        for group in range(groups):
            for part in range(parts):
                start = (side * parts + part) * kept
                pieces = [
                    values[(group * packed + i) * bands : (group * packed + i + 1) * bands, start : start + kept]
                    for i in range(packed)
                ]
                place = (side * groups + group) * parts + part
                chunk_ref[pl.ds(place, bands, stride=2 * groups * parts), :] = jnp.concatenate(
                    pieces, axis=1
                )
    out_ref[...] = chunk_ref[...].astype(jnp.bfloat16).reshape(out_ref.shape)


def inverse_kernel(per_device, pieces_ref, dft_ref, out_ref, pieces_32_ref, rows_ref):
    owners, chunk_rows, width = pieces_ref.shape
    kept, row_count, lon_total = out_ref.shape
    packed = width // kept
    parts = 2 * per_device
    pieces_32_ref[...] = pieces_ref[...].astype(jnp.float32).reshape(owners * chunk_rows, width)
    dft = dft_ref[...]
    place = lax.broadcasted_iota(jnp.int32, (2 * owners * per_device, width), 0)
    factor = jnp.where((place == 0) | (place == owners * per_device), 1.0, 2.0)
    for group in range(chunk_rows // parts):
        found = [
            pieces_32_ref[pl.ds(group * parts + 2 * m + part, owners, stride=chunk_rows), :]
            for part in range(2)
            for m in range(per_device)
        ]
        found = (jnp.concatenate(found, axis=0) * factor).astype(jnp.bfloat16)
        values = lax.dot_general(
            found, dft, (((0,), (0,)), ((), ())), preferred_element_type=jnp.float32
        )
        for i in range(packed):
            for tile in range(lon_total // LANES):
                rows_ref[tile, pl.ds(group * packed + i, kept, stride=row_count), :] = values[
                    i * kept : (i + 1) * kept, tile * LANES : (tile + 1) * LANES
                ]
    for tile in range(lon_total // LANES):
        out_ref[:, :, tile * LANES : (tile + 1) * LANES] = (
            rows_ref[tile].astype(jnp.bfloat16).reshape(kept, row_count, LANES)
        )


def local(fields, conv_first, conv_second, mixing):
    lat_count = lax.axis_size("lat")
    lon_count = lax.axis_size("lon")
    channels, row_count, lon_part = fields.shape
    lat_total = row_count * lat_count
    lon_total = lon_part * lon_count
    orders = lat_total // 2
    degrees = mixing.shape[0]
    owners = lat_count * lon_count
    per_device = orders // owners
    half = row_count // 2
    kept = channels // 2
    swap = [(0, 1), (1, 0)]
    both = ("lat", "lon")
    bfloat = functools.partial(jax.ShapeDtypeStruct, dtype=jnp.bfloat16)

    other = lax.ppermute(fields, "lon", swap)
    unpacked = pltpu.VMEM((lon_part // LANES, channels * row_count, LANES), jnp.float32)
    columns = per_device * degrees
    span = 32 if degrees % 32 == 0 else degrees
    width = lat_total * per_device
    arguments = [
        pltpu.with_memory_space_constraint(value, pltpu.HBM)
        for value in (
            fields,
            jnp.transpose(conv_first, (2, 3, 0, 1)),
            jnp.transpose(conv_second, (2, 3, 0, 1)),
        )
    ]
    own, taps_first, taps_second = call(
        load_kernel,
        (
            bfloat((row_count, channels, lon_part)),
            bfloat(arguments[1].shape),
            bfloat(arguments[2].shape),
        ),
        [pltpu.VMEM(fields.shape, jnp.bfloat16), unpacked, pltpu.SemaphoreType.DMA((3,))],
        [HBM] * 3,
        pl.CostEstimate(flops=1 << 16, bytes_accessed=1 << 21, transcendentals=0),
    )(*arguments)
    message = call(
        message_kernel,
        bfloat((2, channels, lon_total)),
        [unpacked],
        [VMEM, VMEM],
        pl.CostEstimate(flops=1 << 16, bytes_accessed=1 << 18, transcendentals=0),
    )(own, other)
    pairs = []
    for i in range(lat_count - 1):
        lower, upper = 2 * i + i % 2, 2 * (i + 1) + i % 2
        pairs += [(lower, upper), (upper, lower)]
    halo = lax.ppermute(message, both, pairs)

    taps = (3 * channels, 3 * channels)
    first, second, dft, near, interior = call(
        functools.partial(interior_kernel, lat_total, owners),
        (
            bfloat(taps),
            bfloat(taps),
            bfloat((2 * orders, lon_total)),
            bfloat((2, channels, lon_total)),
            jax.ShapeDtypeStruct((half - 2, orders, 2 * channels), jnp.float32),
        ),
        [
            unpacked,
            pltpu.VMEM((half + 2, channels, lon_total), jnp.bfloat16),
            pltpu.VMEM((half, channels, lon_total), jnp.bfloat16),
            pltpu.VMEM((half - 2, channels, lon_total), jnp.bfloat16),
        ],
        [VMEM, VMEM, VMEM, VMEM, ANY],
        pl.CostEstimate(flops=1 << 28, bytes_accessed=1 << 22, transcendentals=0),
    )(
        own,
        other,
        taps_first,
        taps_second,
        message,
    )

    def mixing_table(values, after):
        return call(
            functools.partial(mixing_kernel, per_device),
            jax.ShapeDtypeStruct((channels, kept, columns), jnp.float32),
            [],
            [VMEM, ANY],
            pl.CostEstimate(flops=1 << 20, bytes_accessed=1 << 22, transcendentals=0),
        )(values, after)

    mine = mixing_table(mixing, near)
    theirs = lax.ppermute(mine, "lon", swap)
    analysis, synthesis = call(
        functools.partial(legendre_kernel, span, lat_count, row_count, per_device),
        (bfloat((columns, width)), bfloat((lat_total, columns))),
        [pltpu.VMEM((width // LANES, 2 * degrees, LANES), jnp.float32)],
        [ANY],
        pl.CostEstimate(flops=1 << 35, bytes_accessed=1 << 26, transcendentals=0),
    )(near)
    coeffs = call(
        functools.partial(edge_kernel, lat_total, half),
        bfloat((owners, per_device * half, 2 * channels)),
        [
            pltpu.VMEM((4, channels, lon_total), jnp.bfloat16),
            pltpu.VMEM((4, channels, lon_total), jnp.bfloat16),
            pltpu.VMEM((2, channels, lon_total), jnp.bfloat16),
            pltpu.VMEM((orders * half, 2 * channels), jnp.float32),
        ],
        [VMEM] * 7 + [ANY] * 2,
        pl.CostEstimate(flops=1 << 26, bytes_accessed=1 << 20, transcendentals=0),
    )(halo, message, near, first, second, dft, interior, mine, analysis)
    pieces = lax.all_to_all(coeffs, both, split_axis=0, concat_axis=0, tiled=True)

    chunk_rows = row_count * 2 * per_device * kept // LANES
    chunks = call(
        functools.partial(spectral_kernel, per_device),
        bfloat((owners, chunk_rows, LANES)),
        [
            pltpu.VMEM((2 * channels, columns), jnp.float32),
            pltpu.VMEM((owners * chunk_rows, LANES), jnp.float32),
        ],
        [VMEM] * 5,
        pl.CostEstimate(flops=1 << 24, bytes_accessed=1 << 20, transcendentals=0),
    )(pieces, analysis, synthesis, mine, theirs)

    back = lax.all_to_all(chunks, both, split_axis=0, concat_axis=0, tiled=True)
    return call(
        functools.partial(inverse_kernel, per_device),
        bfloat((kept, row_count, lon_total)),
        [
            pltpu.VMEM((owners * chunk_rows, LANES), jnp.float32),
            pltpu.VMEM((lon_total // LANES, kept * row_count, LANES), jnp.float32),
        ],
        [VMEM] * 2,
        pl.CostEstimate(flops=1 << 24, bytes_accessed=1 << 19, transcendentals=0),
    )(back, dft)


def solution(mesh):
    in_specs = (P("groups", "lat", "lon"), P(), P(), P(None, "lon", None))
    out_specs = P(("groups", "lon"), "lat", None)
    return jax.shard_map(local, mesh=mesh, in_specs=in_specs, out_specs=out_specs, check_vma=False)
```

```python
import functools
import math

import jax
import jax.numpy as jnp
from jax import lax
from jax.experimental import pallas as pl
from jax.experimental.pallas import tpu as pltpu
from jax.sharding import PartitionSpec as P

VMEM = pl.BlockSpec(memory_space=pltpu.VMEM)
ANY = pl.BlockSpec(memory_space=pl.ANY)
HBM = pl.BlockSpec(memory_space=pltpu.HBM)
LIMIT = 40 * 1024 * 1024
LANES = 128


def call(kernel, out_shape, scratch, in_specs, cost):
    return pl.pallas_call(
        kernel,
        out_shape=out_shape,
        in_specs=in_specs,
        out_specs=jax.tree.map(lambda _: VMEM, out_shape),
        scratch_shapes=scratch,
        compiler_params=pltpu.CompilerParams(vmem_limit_bytes=LIMIT),
        cost_estimate=cost,
    )


def split_index(index, size):
    quotient = ((index.astype(jnp.float32) + 0.5) * (1.0 / size)).astype(jnp.int32)
    return quotient, index - quotient * size


def half_of(lat, lon, bands):
    last = (lat + 1) // bands if isinstance(lat, int) else (lat + 1 == bands).astype(jnp.int32)
    return (lat + lon + 1 + last) & 1


def row_half():
    return half_of(lax.axis_index("lat"), lax.axis_index("lon"), lax.axis_size("lat"))


def unpack_rows(source_ref, rows_ref):
    channels, row_count, lon_part = source_ref.shape
    for tile in range(lon_part // LANES):
        rows_ref[tile] = (
            source_ref[:, :, tile * LANES : (tile + 1) * LANES]
            .astype(jnp.float32)
            .reshape(channels * row_count, LANES)
        )


def packed_row(rows_ref, row, channels):
    tiles, count, _ = rows_ref.shape
    found = [
        rows_ref[tile, pl.ds(row, channels, stride=count // channels), :] for tile in range(tiles)
    ]
    return jnp.concatenate(found, axis=1).astype(jnp.bfloat16)


def load_kernel(
    fields_ref,
    conv_first_ref,
    conv_second_ref,
    own_ref,
    first_ref,
    second_ref,
    fields_copy_ref,
    rows_ref,
    arrived,
):
    copies = [
        pltpu.make_async_copy(source, target, arrived.at[i])
        for i, (source, target) in enumerate(
            (
                (fields_ref, fields_copy_ref),
                (conv_first_ref, first_ref),
                (conv_second_ref, second_ref),
            )
        )
    ]
    for copy in copies:
        copy.start()
    copies[0].wait()
    unpack_rows(fields_copy_ref, rows_ref)
    for row in range(own_ref.shape[0]):
        own_ref[row] = packed_row(rows_ref, row, own_ref.shape[1])
    for copy in copies[1:]:
        copy.wait()


def place_row(out_ref, place, side, mine, theirs):
    lon_part = mine.shape[1]
    for position, values in ((side, mine), (1 - side, theirs)):
        start = pl.multiple_of(position * lon_part, LANES)
        out_ref[place, :, pl.ds(start, lon_part)] = values


def message_kernel(own_ref, other_ref, out_ref, rows_ref):
    row_count, channels, _ = own_ref.shape
    side = lax.axis_index("lon")
    unpack_rows(other_ref, rows_ref)
    for i in range(2):
        row = row_half() * (row_count - 2) + i
        place_row(out_ref, i, side, own_ref[row], packed_row(rows_ref, row, channels))


def layer(source_ref, weights, row):
    channels, lon_total = source_ref.shape[1:]
    taps = source_ref[row : row + 3].reshape(3 * channels, lon_total)
    sums = jnp.dot(weights, taps, preferred_element_type=jnp.float32)
    total = (
        sums[channels : 2 * channels]
        + pltpu.roll(sums[:channels], 1, 1)
        + pltpu.roll(sums[2 * channels :], lon_total - 1, 1)
    )
    return jnp.maximum(total, 0.0)


def row_weight(row, lat_total, lon_total):
    place = jnp.full((1, LANES), row, jnp.int32).astype(jnp.float32)
    return jnp.sin((place + 0.5) * (math.pi / lat_total)) * (math.pi / lat_total / lon_total)


def row_spectra(dft, hidden, first_row, lat_total):
    count, channels, lon_total = hidden.shape
    spectra = lax.dot_general(
        dft,
        hidden.reshape(count * channels, lon_total),
        (((1,), (1,)), ((), ())),
        preferred_element_type=jnp.float32,
    )
    orders = spectra.shape[0] // 2
    found = []
    for i in range(count):
        columns = slice(i * channels, (i + 1) * channels)
        parts = jnp.concatenate([spectra[:orders, columns], spectra[orders:, columns]], axis=1)
        found.append(parts * row_weight(first_row + i, lat_total, lon_total))
    return found


def interior_kernel(
    lat_total,
    owners,
    own_ref,
    other_ref,
    first_ref,
    second_ref,
    after_ref,
    first_out,
    second_out,
    dft_out,
    near_out,
    coeffs_out,
    rows_ref,
    band_ref,
    mid_ref,
    hidden_ref,
):
    del after_ref
    row_count, channels, lon_part = own_ref.shape
    lon_total = 2 * lon_part
    half = row_count // 2
    side, part = lax.axis_index("lon"), row_half()
    for source, target in ((first_ref, first_out), (second_ref, second_out)):
        for b in range(3):
            target[b * channels : (b + 1) * channels, :] = jnp.concatenate(
                [source[a, b] for a in range(3)], axis=1
            )
    orders = dft_out.shape[0] // 2
    place = lax.broadcasted_iota(jnp.int32, (orders, lon_total), 0)
    order, owner = split_index(place, owners)
    waves = owner * (orders // owners) + order
    points = lax.broadcasted_iota(jnp.int32, (orders, lon_total), 1)
    angle = ((waves * points) & (lon_total - 1)).astype(jnp.float32) * (2.0 * math.pi / lon_total)
    dft_out[:orders, :] = jnp.cos(angle).astype(jnp.bfloat16)
    dft_out[orders:, :] = (-jnp.sin(angle)).astype(jnp.bfloat16)
    unpack_rows(other_ref, rows_ref)
    for i in range(half + 2):
        row = 2 * part + i
        place_row(band_ref, i, side, own_ref[row], packed_row(rows_ref, row, channels))
    weights = first_out[...]
    for i in range(half):
        mid_ref[i] = layer(band_ref, weights, i).astype(jnp.bfloat16)
    near_out[...] = mid_ref[pl.ds((half - 2) * part, 2)]
    weights = second_out[...]
    for i in range(half - 2):
        hidden_ref[i] = layer(mid_ref, weights, i).astype(jnp.bfloat16)
    first_row = lax.axis_index("lat") * row_count + part * half + 2 * (1 - part)
    found = row_spectra(dft_out[...], hidden_ref[...], first_row, lat_total)
    for i, values in enumerate(found):
        coeffs_out[i] = values


def edge_kernel(
    lat_total,
    half,
    halo_ref,
    message_ref,
    near_ref,
    first_ref,
    second_ref,
    dft_ref,
    coeffs_ref,
    mine_ref,
    analysis_ref,
    out_ref,
    band_ref,
    mid_ref,
    hidden_ref,
    packed_ref,
):
    del mine_ref, analysis_ref
    part = row_half()
    first_row = lax.axis_index("lat") * (2 * half) + part * half
    band_ref[pl.ds(2 * part, 2)] = halo_ref[...]
    band_ref[pl.ds(2 - 2 * part, 2)] = message_ref[...]
    mid_ref[pl.ds(2 - 2 * part, 2)] = near_ref[...]
    weights = first_ref[...]
    for i in range(2):
        place = first_row - 1 + part * half + i
        values = layer(band_ref, weights, i)
        values = jnp.where((place >= 0) & (place < lat_total), values, 0.0)
        mid_ref[2 * part + i] = values.astype(jnp.bfloat16)
    weights = second_ref[...]
    for i in range(2):
        hidden_ref[i] = layer(mid_ref, weights, i).astype(jnp.bfloat16)
    edge = part * (half - 2)
    found = row_spectra(dft_ref[...], hidden_ref[...], first_row + edge, lat_total)
    owners, chunk_rows, _ = out_ref.shape
    for m in range(chunk_rows // half):
        own = slice(m * owners, (m + 1) * owners)
        for i in range(2):
            start = m * half + edge + i
            packed_ref[pl.ds(start, owners, stride=chunk_rows), :] = found[i][own]
        for i in range(half - 2):
            start = m * half + 2 - 2 * part + i
            packed_ref[pl.ds(start, owners, stride=chunk_rows), :] = coeffs_ref[i, own]
    out_ref[...] = packed_ref[...].astype(jnp.bfloat16).reshape(out_ref.shape)


def mixing_kernel(per_device, mixing_ref, after_ref, out_ref):
    del after_ref
    values = jnp.transpose(mixing_ref[...].astype(jnp.float32), (1, 0, 2))
    blocks = [
        jnp.concatenate([values[o]] * per_device, axis=0).T for o in range(values.shape[0])
    ]
    out_ref[...] = jnp.transpose(jnp.stack(blocks), (1, 0, 2))


def legendre_kernel(
    span, bands, row_count, per_device, after_ref, analysis_ref, synthesis_ref, values_ref
):
    del after_ref
    tiles, count, _ = values_ref.shape
    degrees, width = count // 2, tiles * LANES
    lat_total = bands * row_count
    half = row_count // 2
    first_order = (2 * lax.axis_index("lat") + lax.axis_index("lon")) * per_device
    lane = lax.broadcasted_iota(jnp.int32, (2, width), 1)
    form = lax.broadcasted_iota(jnp.int32, (2, width), 0)
    rest, low = split_index(lane, half)
    device, own_first = split_index(rest, per_device)
    rest, band = split_index(lane, bands)
    own_second, inner = split_index(rest, row_count)
    own = jnp.where(form == 0, own_first, own_second)
    place = (device >> 1) * row_count + half_of(device >> 1, device & 1, bands) * half + low
    row = jnp.where(form == 0, place, band * row_count + inner)
    south = row >= lat_total // 2
    row = jnp.where(south, lat_total - 1 - row, row)
    colatitude = (row.astype(jnp.float32) + 0.5) * (math.pi / lat_total)
    cosine, sine_theta = jnp.cos(colatitude), jnp.sin(colatitude)
    order_ids = first_order + own
    orders = order_ids.astype(jnp.float32)
    counter = 1.0 + lax.broadcasted_iota(jnp.int32, (1, max(degrees, LANES)), 1).astype(jnp.float32)
    log_terms = jnp.log((2.0 * counter - 1.0) / (2.0 * counter))
    log_start = 0.5 * jnp.log(orders + 0.5) + orders * jnp.log(sine_theta)
    for m in range(per_device):
        below = counter <= jnp.full(counter.shape, first_order + m, jnp.int32).astype(jnp.float32)
        total = jnp.sum(jnp.where(below, log_terms, 0.0), axis=1, keepdims=True)
        log_start = log_start + jnp.where(own == m, 0.5 * total, 0.0)
    parity = (1 - 2 * (order_ids & 1)).astype(jnp.float32)
    even_sign, odd_sign = jnp.where(south, parity, 1.0), jnp.where(south, -parity, 1.0)
    orders_squared = orders * orders
    start_scale = jnp.exp(log_start)
    current = previous = scale = log_scale = jnp.zeros_like(cosine)
    root = jnp.zeros_like(cosine)
    for degree in range(degrees):
        distance = float(degree * degree) - orders_squared
        inverse_root = lax.rsqrt(jnp.maximum(distance, 1.0))
        above = math.sqrt(max(4.0 * degree * degree - 1.0, 1.0))
        below = math.sqrt(max(4.0 * (degree - 1) * (degree - 1) - 1.0, 1.0))
        newest = (above * inverse_root) * (cosine * current - (root * (1.0 / below)) * previous)
        root = jnp.maximum(distance, 0.0) * inverse_root
        is_start = orders == float(degree)
        newest = jnp.where(is_start, 1.0, newest)
        scale = jnp.where(is_start, start_scale, scale)
        log_scale = jnp.where(is_start, log_start, log_scale)
        previous, current = current, newest
        emitted = newest * scale * (even_sign if degree % 2 == 0 else odd_sign)
        for tile in range(tiles):
            values_ref[tile, 2 * degree : 2 * degree + 2, :] = emitted[
                :, tile * LANES : (tile + 1) * LANES
            ]
        if degree % span == span - 1 and degree < degrees - 1:
            size_now = jnp.maximum(jnp.abs(current), jnp.abs(previous))
            safe_size = jnp.where(size_now > 0.0, size_now, 1.0)
            current, previous = current / safe_size, previous / safe_size
            log_scale = log_scale + jnp.log(safe_size)
            scale = jnp.where(degree >= orders, jnp.exp(log_scale), 0.0)
    first, second = (
        jnp.concatenate(
            [values_ref[tile, pl.ds(i, degrees, stride=2), :] for tile in range(tiles)], axis=1
        )
        for i in range(2)
    )
    for m in range(per_device):
        analysis_ref[m * degrees : (m + 1) * degrees, :] = jnp.where(
            own[0:1] == m, first, 0.0
        ).astype(jnp.bfloat16)
    stacked = jnp.concatenate(
        [second[:, m * lat_total : (m + 1) * lat_total] for m in range(per_device)], axis=0
    )
    synthesis_ref[...] = stacked.T.astype(jnp.bfloat16)


def spectral_kernel(
    per_device,
    pieces_ref,
    analysis_ref,
    synthesis_ref,
    mine_ref,
    theirs_ref,
    out_ref,
    spectral_ref,
    chunk_ref,
):
    owners, chunk_rows, width = pieces_ref.shape
    channels, kept, columns = mine_ref.shape
    degrees = columns // per_device
    parts = 2 * per_device
    groups = chunk_rows // parts
    packed = width // kept
    bands = synthesis_ref.shape[0] // (groups * packed)

    pieces = pieces_ref[...].reshape(owners * chunk_rows, width)
    spectral = lax.dot_general(
        pieces, analysis_ref[...], (((0,), (1,)), ((), ())), preferred_element_type=jnp.float32
    )
    spectral_ref[...] = spectral.astype(jnp.bfloat16).astype(jnp.float32)

    def add_channel(channel, totals):
        rows = [spectral_ref[pl.ds(part * channels + channel, 1), :] for part in range(2)]
        mine, theirs = mine_ref[channel], theirs_ref[channel]
        return (
            totals[0] + mine * rows[0],
            totals[1] + mine * rows[1],
            totals[2] + theirs * rows[0],
            totals[3] + theirs * rows[1],
        )

    zeros = jnp.zeros((kept, columns), jnp.float32)
    totals = lax.fori_loop(0, channels, add_channel, (zeros,) * 4, unroll=64)
    upper = lax.axis_index("lon") == 0
    mixed = [
        [jnp.where(upper, totals[part], totals[2 + part]) for part in range(2)],
        [jnp.where(upper, totals[2 + part], totals[part]) for part in range(2)],
    ]
    lane = lax.broadcasted_iota(jnp.int32, (kept, columns), 1)
    blocks = []
    for side in range(2):
        for m in range(per_device):
            own = (lane >= m * degrees) & (lane < (m + 1) * degrees)
            for part in range(2):
                blocks.append(jnp.where(own, mixed[side][part], 0.0).astype(jnp.bfloat16))
    values = lax.dot_general(
        synthesis_ref[...],
        jnp.concatenate(blocks, axis=0),
        (((1,), (1,)), ((), ())),
        preferred_element_type=jnp.float32,
    )
    for side in range(2):
        for group in range(groups):
            for part in range(parts):
                start = (side * parts + part) * kept
                pieces = [
                    values[(group * packed + i) * bands : (group * packed + i + 1) * bands, start : start + kept]
                    for i in range(packed)
                ]
                place = (side * groups + group) * parts + part
                chunk_ref[pl.ds(place, bands, stride=2 * groups * parts), :] = jnp.concatenate(
                    pieces, axis=1
                )
    out_ref[...] = chunk_ref[...].astype(jnp.bfloat16).reshape(out_ref.shape)


def inverse_kernel(per_device, pieces_ref, dft_ref, out_ref, pieces_32_ref, rows_ref):
    owners, chunk_rows, width = pieces_ref.shape
    kept, row_count, lon_total = out_ref.shape
    packed = width // kept
    parts = 2 * per_device
    pieces_32_ref[...] = pieces_ref[...].astype(jnp.float32).reshape(owners * chunk_rows, width)
    dft = dft_ref[...]
    place = lax.broadcasted_iota(jnp.int32, (2 * owners * per_device, width), 0)
    factor = jnp.where((place == 0) | (place == owners * per_device), 1.0, 2.0)
    for group in range(chunk_rows // parts):
        found = [
            pieces_32_ref[pl.ds(group * parts + 2 * m + part, owners, stride=chunk_rows), :]
            for part in range(2)
            for m in range(per_device)
        ]
        found = (jnp.concatenate(found, axis=0) * factor).astype(jnp.bfloat16)
        values = lax.dot_general(
            found, dft, (((0,), (0,)), ((), ())), preferred_element_type=jnp.float32
        )
        for i in range(packed):
            for tile in range(lon_total // LANES):
                rows_ref[tile, pl.ds(group * packed + i, kept, stride=row_count), :] = values[
                    i * kept : (i + 1) * kept, tile * LANES : (tile + 1) * LANES
                ]
    for tile in range(lon_total // LANES):
        out_ref[:, :, tile * LANES : (tile + 1) * LANES] = (
            rows_ref[tile].astype(jnp.bfloat16).reshape(kept, row_count, LANES)
        )


def local(fields, conv_first, conv_second, mixing):
    lat_count = lax.axis_size("lat")
    lon_count = lax.axis_size("lon")
    channels, row_count, lon_part = fields.shape
    lat_total = row_count * lat_count
    lon_total = lon_part * lon_count
    orders = lat_total // 2
    degrees = mixing.shape[0]
    owners = lat_count * lon_count
    per_device = orders // owners
    half = row_count // 2
    kept = channels // 2
    swap = [(0, 1), (1, 0)]
    both = ("lat", "lon")
    bfloat = functools.partial(jax.ShapeDtypeStruct, dtype=jnp.bfloat16)

    other = lax.ppermute(fields, "lon", swap)
    unpacked = pltpu.VMEM((lon_part // LANES, channels * row_count, LANES), jnp.float32)
    columns = per_device * degrees
    span = 32 if degrees % 32 == 0 else degrees
    width = lat_total * per_device
    arguments = [
        pltpu.with_memory_space_constraint(value, pltpu.HBM)
        for value in (
            fields,
            jnp.transpose(conv_first, (2, 3, 0, 1)),
            jnp.transpose(conv_second, (2, 3, 0, 1)),
        )
    ]
    own, taps_first, taps_second = call(
        load_kernel,
        (
            bfloat((row_count, channels, lon_part)),
            bfloat(arguments[1].shape),
            bfloat(arguments[2].shape),
        ),
        [pltpu.VMEM(fields.shape, jnp.bfloat16), unpacked, pltpu.SemaphoreType.DMA((3,))],
        [HBM] * 3,
        pl.CostEstimate(flops=1 << 16, bytes_accessed=1 << 21, transcendentals=0),
    )(*arguments)
    message = call(
        message_kernel,
        bfloat((2, channels, lon_total)),
        [unpacked],
        [VMEM, VMEM],
        pl.CostEstimate(flops=1 << 16, bytes_accessed=1 << 18, transcendentals=0),
    )(own, other)
    pairs = []
    for i in range(lat_count - 1):
        lower = 2 * i + half_of(i, 1, lat_count)
        upper = 2 * (i + 1) + half_of(i + 1, 0, lat_count)
        pairs += [(lower, upper), (upper, lower)]
    halo = lax.ppermute(message, both, pairs)

    taps = (3 * channels, 3 * channels)
    first, second, dft, near, interior = call(
        functools.partial(interior_kernel, lat_total, owners),
        (
            bfloat(taps),
            bfloat(taps),
            bfloat((2 * orders, lon_total)),
            bfloat((2, channels, lon_total)),
            jax.ShapeDtypeStruct((half - 2, orders, 2 * channels), jnp.float32),
        ),
        [
            unpacked,
            pltpu.VMEM((half + 2, channels, lon_total), jnp.bfloat16),
            pltpu.VMEM((half, channels, lon_total), jnp.bfloat16),
            pltpu.VMEM((half - 2, channels, lon_total), jnp.bfloat16),
        ],
        [VMEM, VMEM, VMEM, VMEM, ANY],
        pl.CostEstimate(flops=1 << 28, bytes_accessed=1 << 22, transcendentals=0),
    )(
        own,
        other,
        taps_first,
        taps_second,
        message,
    )

    def mixing_table(values, after):
        return call(
            functools.partial(mixing_kernel, per_device),
            jax.ShapeDtypeStruct((channels, kept, columns), jnp.float32),
            [],
            [VMEM, ANY],
            pl.CostEstimate(flops=1 << 20, bytes_accessed=1 << 22, transcendentals=0),
        )(values, after)

    mine = mixing_table(mixing, near)
    theirs = lax.ppermute(mine, "lon", swap)
    analysis, synthesis = call(
        functools.partial(legendre_kernel, span, lat_count, row_count, per_device),
        (bfloat((columns, width)), bfloat((lat_total, columns))),
        [pltpu.VMEM((width // LANES, 2 * degrees, LANES), jnp.float32)],
        [ANY],
        pl.CostEstimate(flops=1 << 35, bytes_accessed=1 << 26, transcendentals=0),
    )(near)
    coeffs = call(
        functools.partial(edge_kernel, lat_total, half),
        bfloat((owners, per_device * half, 2 * channels)),
        [
            pltpu.VMEM((4, channels, lon_total), jnp.bfloat16),
            pltpu.VMEM((4, channels, lon_total), jnp.bfloat16),
            pltpu.VMEM((2, channels, lon_total), jnp.bfloat16),
            pltpu.VMEM((orders * half, 2 * channels), jnp.float32),
        ],
        [VMEM] * 7 + [ANY] * 2,
        pl.CostEstimate(flops=1 << 26, bytes_accessed=1 << 20, transcendentals=0),
    )(halo, message, near, first, second, dft, interior, mine, analysis)
    pieces = lax.all_to_all(coeffs, both, split_axis=0, concat_axis=0, tiled=True)

    chunk_rows = row_count * 2 * per_device * kept // LANES
    chunks = call(
        functools.partial(spectral_kernel, per_device),
        bfloat((owners, chunk_rows, LANES)),
        [
            pltpu.VMEM((2 * channels, columns), jnp.float32),
            pltpu.VMEM((owners * chunk_rows, LANES), jnp.float32),
        ],
        [VMEM] * 5,
        pl.CostEstimate(flops=1 << 24, bytes_accessed=1 << 20, transcendentals=0),
    )(pieces, analysis, synthesis, mine, theirs)

    back = lax.all_to_all(chunks, both, split_axis=0, concat_axis=0, tiled=True)
    return call(
        functools.partial(inverse_kernel, per_device),
        bfloat((kept, row_count, lon_total)),
        [
            pltpu.VMEM((owners * chunk_rows, LANES), jnp.float32),
            pltpu.VMEM((lon_total // LANES, kept * row_count, LANES), jnp.float32),
        ],
        [VMEM] * 2,
        pl.CostEstimate(flops=1 << 24, bytes_accessed=1 << 19, transcendentals=0),
    )(back, dft)


def solution(mesh):
    in_specs = (P("groups", "lat", "lon"), P(), P(), P(None, "lon", None))
    out_specs = P(("groups", "lon"), "lat", None)
    return jax.shard_map(local, mesh=mesh, in_specs=in_specs, out_specs=out_specs, check_vma=False)
```

```python
import functools
import math

import jax
import jax.numpy as jnp
from jax import lax
from jax.experimental import pallas as pl
from jax.experimental.pallas import tpu as pltpu
from jax.sharding import PartitionSpec as P

VMEM = pl.BlockSpec(memory_space=pltpu.VMEM)
ANY = pl.BlockSpec(memory_space=pl.ANY)
HBM = pl.BlockSpec(memory_space=pltpu.HBM)
LIMIT = 40 * 1024 * 1024
LANES = 128


def call(kernel, out_shape, scratch, in_specs, cost):
    return pl.pallas_call(
        kernel,
        out_shape=out_shape,
        in_specs=in_specs,
        out_specs=jax.tree.map(lambda _: VMEM, out_shape),
        scratch_shapes=scratch,
        compiler_params=pltpu.CompilerParams(vmem_limit_bytes=LIMIT),
        cost_estimate=cost,
    )


def split_index(index, size):
    quotient = ((index.astype(jnp.float32) + 0.5) * (1.0 / size)).astype(jnp.int32)
    return quotient, index - quotient * size


def half_of(lat, lon, bands):
    last = (lat + 1) // bands if isinstance(lat, int) else (lat + 1 == bands).astype(jnp.int32)
    return (lat + lon + 1 + last) & 1


def row_half():
    return half_of(lax.axis_index("lat"), lax.axis_index("lon"), lax.axis_size("lat"))


def unpack_rows(source_ref, rows_ref):
    channels, row_count, lon_part = source_ref.shape
    for tile in range(lon_part // LANES):
        rows_ref[tile] = (
            source_ref[:, :, tile * LANES : (tile + 1) * LANES]
            .astype(jnp.float32)
            .reshape(channels * row_count, LANES)
        )


def packed_row(rows_ref, row, channels):
    tiles, count, _ = rows_ref.shape
    found = [
        rows_ref[tile, pl.ds(row, channels, stride=count // channels), :] for tile in range(tiles)
    ]
    return jnp.concatenate(found, axis=1).astype(jnp.bfloat16)


def load_kernel(
    fields_ref,
    conv_first_ref,
    conv_second_ref,
    own_ref,
    first_ref,
    second_ref,
    fields_copy_ref,
    rows_ref,
    arrived,
):
    copies = [
        pltpu.make_async_copy(source, target, arrived.at[i])
        for i, (source, target) in enumerate(
            (
                (fields_ref, fields_copy_ref),
                (conv_first_ref, first_ref),
                (conv_second_ref, second_ref),
            )
        )
    ]
    for copy in copies:
        copy.start()
    copies[0].wait()
    unpack_rows(fields_copy_ref, rows_ref)
    for row in range(own_ref.shape[0]):
        own_ref[row] = packed_row(rows_ref, row, own_ref.shape[1])
    for copy in copies[1:]:
        copy.wait()


def place_row(out_ref, place, side, mine, theirs):
    lon_part = mine.shape[1]
    for position, values in ((side, mine), (1 - side, theirs)):
        start = pl.multiple_of(position * lon_part, LANES)
        out_ref[place, :, pl.ds(start, lon_part)] = values


def message_kernel(own_ref, other_ref, out_ref, rows_ref):
    row_count, channels, _ = own_ref.shape
    side = lax.axis_index("lon")
    unpack_rows(other_ref, rows_ref)
    for i in range(2):
        row = row_half() * (row_count - 2) + i
        place_row(out_ref, i, side, own_ref[row], packed_row(rows_ref, row, channels))


def layer(source_ref, weights, row):
    channels, lon_total = source_ref.shape[1:]
    taps = source_ref[row : row + 3].reshape(3 * channels, lon_total)
    sums = jnp.dot(weights, taps, preferred_element_type=jnp.float32)
    total = (
        sums[channels : 2 * channels]
        + pltpu.roll(sums[:channels], 1, 1)
        + pltpu.roll(sums[2 * channels :], lon_total - 1, 1)
    )
    return jnp.maximum(total, 0.0)


def two_rows(weights, pair):
    _, channels, lon_total = pair.shape
    sums = jnp.dot(
        weights, pair.reshape(2 * channels, lon_total), preferred_element_type=jnp.float32
    )
    found = []
    for i in range(2):
        part = sums[3 * channels * i : 3 * channels * (i + 1)]
        found.append(
            part[channels : 2 * channels]
            + pltpu.roll(part[:channels], 1, 1)
            + pltpu.roll(part[2 * channels :], lon_total - 1, 1)
        )
    return found


def two_row_weights(taps, out_ref):
    height, width = taps.shape
    channels = width // 3
    zeros = jnp.zeros((height, channels), jnp.bfloat16)
    out_ref[0, :height, :] = taps[:, : 2 * channels]
    out_ref[0, height:, :] = jnp.concatenate([zeros, taps[:, :channels]], axis=1)
    out_ref[1, :height, :] = jnp.concatenate([taps[:, 2 * channels :], zeros], axis=1)
    out_ref[1, height:, :] = taps[:, channels:]


def row_weight(row, lat_total, lon_total):
    place = jnp.full((1, LANES), row, jnp.int32).astype(jnp.float32)
    return jnp.sin((place + 0.5) * (math.pi / lat_total)) * (math.pi / lat_total / lon_total)


def row_spectra(dft, hidden, first_row, lat_total):
    count, channels, lon_total = hidden.shape
    spectra = lax.dot_general(
        dft,
        hidden.reshape(count * channels, lon_total),
        (((1,), (1,)), ((), ())),
        preferred_element_type=jnp.float32,
    )
    orders = spectra.shape[0] // 2
    found = []
    for i in range(count):
        columns = slice(i * channels, (i + 1) * channels)
        parts = jnp.concatenate([spectra[:orders, columns], spectra[orders:, columns]], axis=1)
        found.append(parts * row_weight(first_row + i, lat_total, lon_total))
    return found


def interior_kernel(
    lat_total,
    owners,
    own_ref,
    other_ref,
    first_ref,
    second_ref,
    message_ref,
    first_out,
    second_out,
    dft_out,
    first_part_out,
    second_part_out,
    coeffs_out,
    rows_ref,
    band_ref,
    mid_ref,
    hidden_ref,
    taps_ref,
    forms_ref,
):
    row_count, channels, lon_part = own_ref.shape
    lon_total = 2 * lon_part
    half = row_count // 2
    side, part = lax.axis_index("lon"), row_half()
    for layer_id, source in enumerate((first_ref, second_ref)):
        target = taps_ref.at[layer_id]
        for b in range(3):
            target[b * channels : (b + 1) * channels, :] = jnp.concatenate(
                [source[a, b] for a in range(3)], axis=1
            )
    orders = dft_out.shape[0] // 2
    place = lax.broadcasted_iota(jnp.int32, (orders, lon_total), 0)
    order, owner = split_index(place, owners)
    waves = owner * (orders // owners) + order
    points = lax.broadcasted_iota(jnp.int32, (orders, lon_total), 1)
    angle = ((waves * points) & (lon_total - 1)).astype(jnp.float32) * (2.0 * math.pi / lon_total)
    dft_out[:orders, :] = jnp.cos(angle).astype(jnp.bfloat16)
    dft_out[orders:, :] = (-jnp.sin(angle)).astype(jnp.bfloat16)
    unpack_rows(other_ref, rows_ref)
    for i in range(half + 2):
        row = 2 * part + i
        place_row(band_ref, i, side, own_ref[row], packed_row(rows_ref, row, channels))
    weights = taps_ref[0]
    for i in range(half):
        mid_ref[i] = layer(band_ref, weights, i).astype(jnp.bfloat16)
    for layer_id, (weights_out, part_out, pair) in enumerate(
        (
            (first_out, first_part_out, message_ref[...]),
            (second_out, second_part_out, mid_ref[pl.ds((half - 2) * part, 2)]),
        )
    ):
        two_row_weights(taps_ref[layer_id], forms_ref.at[layer_id])
        weights_out[...] = forms_ref[layer_id, part]
        for i, values in enumerate(two_rows(forms_ref[layer_id, 1 - part], pair)):
            part_out[i] = values
    weights = taps_ref[1]
    for i in range(half - 2):
        hidden_ref[i] = layer(mid_ref, weights, i).astype(jnp.bfloat16)
    first_row = lax.axis_index("lat") * row_count + part * half + 2 * (1 - part)
    found = row_spectra(dft_out[...], hidden_ref[...], first_row, lat_total)
    for i, values in enumerate(found):
        coeffs_out[i] = values


def edge_kernel(
    lat_total,
    half,
    halo_ref,
    first_ref,
    second_ref,
    dft_ref,
    first_part_ref,
    second_part_ref,
    coeffs_ref,
    mine_ref,
    analysis_ref,
    out_ref,
    packed_ref,
):
    del mine_ref, analysis_ref
    part = row_half()
    first_row = lax.axis_index("lat") * (2 * half) + part * half
    mid = []
    for i, values in enumerate(two_rows(first_ref[...], halo_ref[...])):
        place = first_row - 1 + part * half + i
        values = jnp.maximum(values + first_part_ref[i], 0.0)
        values = jnp.where((place >= 0) & (place < lat_total), values, 0.0)
        mid.append(values.astype(jnp.bfloat16))
    hidden = [
        jnp.maximum(values + second_part_ref[i], 0.0).astype(jnp.bfloat16)
        for i, values in enumerate(two_rows(second_ref[...], jnp.stack(mid)))
    ]
    edge = part * (half - 2)
    found = row_spectra(dft_ref[...], jnp.stack(hidden), first_row + edge, lat_total)
    owners, chunk_rows, _ = out_ref.shape
    for m in range(chunk_rows // half):
        own = slice(m * owners, (m + 1) * owners)
        for i in range(2):
            start = m * half + edge + i
            packed_ref[pl.ds(start, owners, stride=chunk_rows), :] = found[i][own]
        for i in range(half - 2):
            start = m * half + 2 - 2 * part + i
            packed_ref[pl.ds(start, owners, stride=chunk_rows), :] = coeffs_ref[i, own]
    out_ref[...] = packed_ref[...].astype(jnp.bfloat16).reshape(out_ref.shape)


def mixing_kernel(per_device, mixing_ref, after_ref, out_ref):
    del after_ref
    values = jnp.transpose(mixing_ref[...].astype(jnp.float32), (1, 0, 2))
    blocks = [
        jnp.concatenate([values[o]] * per_device, axis=0).T for o in range(values.shape[0])
    ]
    out_ref[...] = jnp.transpose(jnp.stack(blocks), (1, 0, 2))


def legendre_kernel(
    span, bands, row_count, per_device, after_ref, analysis_ref, synthesis_ref, values_ref
):
    del after_ref
    tiles, count, _ = values_ref.shape
    degrees, width = count // 2, tiles * LANES
    lat_total = bands * row_count
    half = row_count // 2
    first_order = (2 * lax.axis_index("lat") + lax.axis_index("lon")) * per_device
    lane = lax.broadcasted_iota(jnp.int32, (2, width), 1)
    form = lax.broadcasted_iota(jnp.int32, (2, width), 0)
    rest, low = split_index(lane, half)
    device, own_first = split_index(rest, per_device)
    rest, band = split_index(lane, bands)
    own_second, inner = split_index(rest, row_count)
    own = jnp.where(form == 0, own_first, own_second)
    place = (device >> 1) * row_count + half_of(device >> 1, device & 1, bands) * half + low
    row = jnp.where(form == 0, place, band * row_count + inner)
    south = row >= lat_total // 2
    row = jnp.where(south, lat_total - 1 - row, row)
    colatitude = (row.astype(jnp.float32) + 0.5) * (math.pi / lat_total)
    cosine, sine_theta = jnp.cos(colatitude), jnp.sin(colatitude)
    order_ids = first_order + own
    orders = order_ids.astype(jnp.float32)
    counter = 1.0 + lax.broadcasted_iota(jnp.int32, (1, max(degrees, LANES)), 1).astype(jnp.float32)
    log_terms = jnp.log((2.0 * counter - 1.0) / (2.0 * counter))
    log_start = 0.5 * jnp.log(orders + 0.5) + orders * jnp.log(sine_theta)
    for m in range(per_device):
        below = counter <= jnp.full(counter.shape, first_order + m, jnp.int32).astype(jnp.float32)
        total = jnp.sum(jnp.where(below, log_terms, 0.0), axis=1, keepdims=True)
        log_start = log_start + jnp.where(own == m, 0.5 * total, 0.0)
    parity = (1 - 2 * (order_ids & 1)).astype(jnp.float32)
    even_sign, odd_sign = jnp.where(south, parity, 1.0), jnp.where(south, -parity, 1.0)
    orders_squared = orders * orders
    start_scale = jnp.exp(log_start)
    current = previous = scale = log_scale = jnp.zeros_like(cosine)
    root = jnp.zeros_like(cosine)
    for degree in range(degrees):
        distance = float(degree * degree) - orders_squared
        inverse_root = lax.rsqrt(jnp.maximum(distance, 1.0))
        above = math.sqrt(max(4.0 * degree * degree - 1.0, 1.0))
        below = math.sqrt(max(4.0 * (degree - 1) * (degree - 1) - 1.0, 1.0))
        newest = (above * inverse_root) * (cosine * current - (root * (1.0 / below)) * previous)
        root = jnp.maximum(distance, 0.0) * inverse_root
        is_start = orders == float(degree)
        newest = jnp.where(is_start, 1.0, newest)
        scale = jnp.where(is_start, start_scale, scale)
        log_scale = jnp.where(is_start, log_start, log_scale)
        previous, current = current, newest
        emitted = newest * scale * (even_sign if degree % 2 == 0 else odd_sign)
        for tile in range(tiles):
            values_ref[tile, 2 * degree : 2 * degree + 2, :] = emitted[
                :, tile * LANES : (tile + 1) * LANES
            ]
        if degree % span == span - 1 and degree < degrees - 1:
            size_now = jnp.maximum(jnp.abs(current), jnp.abs(previous))
            safe_size = jnp.where(size_now > 0.0, size_now, 1.0)
            current, previous = current / safe_size, previous / safe_size
            log_scale = log_scale + jnp.log(safe_size)
            scale = jnp.where(degree >= orders, jnp.exp(log_scale), 0.0)
    first, second = (
        jnp.concatenate(
            [values_ref[tile, pl.ds(i, degrees, stride=2), :] for tile in range(tiles)], axis=1
        )
        for i in range(2)
    )
    for m in range(per_device):
        analysis_ref[m * degrees : (m + 1) * degrees, :] = jnp.where(
            own[0:1] == m, first, 0.0
        ).astype(jnp.bfloat16)
    stacked = jnp.concatenate(
        [second[:, m * lat_total : (m + 1) * lat_total] for m in range(per_device)], axis=0
    )
    synthesis_ref[...] = stacked.T.astype(jnp.bfloat16)


def spectral_kernel(
    per_device,
    pieces_ref,
    analysis_ref,
    synthesis_ref,
    mine_ref,
    theirs_ref,
    out_ref,
    spectral_ref,
    chunk_ref,
):
    owners, chunk_rows, width = pieces_ref.shape
    channels, kept, columns = mine_ref.shape
    degrees = columns // per_device
    parts = 2 * per_device
    groups = chunk_rows // parts
    packed = width // kept
    bands = synthesis_ref.shape[0] // (groups * packed)

    pieces = pieces_ref[...].reshape(owners * chunk_rows, width)
    spectral = lax.dot_general(
        pieces, analysis_ref[...], (((0,), (1,)), ((), ())), preferred_element_type=jnp.float32
    )
    spectral_ref[...] = spectral.astype(jnp.bfloat16).astype(jnp.float32)

    def add_channel(channel, totals):
        rows = [spectral_ref[pl.ds(part * channels + channel, 1), :] for part in range(2)]
        mine, theirs = mine_ref[channel], theirs_ref[channel]
        return (
            totals[0] + mine * rows[0],
            totals[1] + mine * rows[1],
            totals[2] + theirs * rows[0],
            totals[3] + theirs * rows[1],
        )

    zeros = jnp.zeros((kept, columns), jnp.float32)
    totals = lax.fori_loop(0, channels, add_channel, (zeros,) * 4, unroll=64)
    upper = lax.axis_index("lon") == 0
    mixed = [
        [jnp.where(upper, totals[part], totals[2 + part]) for part in range(2)],
        [jnp.where(upper, totals[2 + part], totals[part]) for part in range(2)],
    ]
    lane = lax.broadcasted_iota(jnp.int32, (kept, columns), 1)
    blocks = []
    for side in range(2):
        for m in range(per_device):
            own = (lane >= m * degrees) & (lane < (m + 1) * degrees)
            for part in range(2):
                blocks.append(jnp.where(own, mixed[side][part], 0.0).astype(jnp.bfloat16))
    values = lax.dot_general(
        synthesis_ref[...],
        jnp.concatenate(blocks, axis=0),
        (((1,), (1,)), ((), ())),
        preferred_element_type=jnp.float32,
    )
    for side in range(2):
        for group in range(groups):
            for part in range(parts):
                start = (side * parts + part) * kept
                pieces = [
                    values[(group * packed + i) * bands : (group * packed + i + 1) * bands, start : start + kept]
                    for i in range(packed)
                ]
                place = (side * groups + group) * parts + part
                chunk_ref[pl.ds(place, bands, stride=2 * groups * parts), :] = jnp.concatenate(
                    pieces, axis=1
                )
    out_ref[...] = chunk_ref[...].astype(jnp.bfloat16).reshape(out_ref.shape)


def inverse_kernel(per_device, pieces_ref, dft_ref, out_ref, pieces_32_ref, rows_ref):
    owners, chunk_rows, width = pieces_ref.shape
    kept, row_count, lon_total = out_ref.shape
    packed = width // kept
    parts = 2 * per_device
    pieces_32_ref[...] = pieces_ref[...].astype(jnp.float32).reshape(owners * chunk_rows, width)
    dft = dft_ref[...]
    place = lax.broadcasted_iota(jnp.int32, (2 * owners * per_device, width), 0)
    factor = jnp.where((place == 0) | (place == owners * per_device), 1.0, 2.0)
    for group in range(chunk_rows // parts):
        found = [
            pieces_32_ref[pl.ds(group * parts + 2 * m + part, owners, stride=chunk_rows), :]
            for part in range(2)
            for m in range(per_device)
        ]
        found = (jnp.concatenate(found, axis=0) * factor).astype(jnp.bfloat16)
        values = lax.dot_general(
            found, dft, (((0,), (0,)), ((), ())), preferred_element_type=jnp.float32
        )
        for i in range(packed):
            for tile in range(lon_total // LANES):
                rows_ref[tile, pl.ds(group * packed + i, kept, stride=row_count), :] = values[
                    i * kept : (i + 1) * kept, tile * LANES : (tile + 1) * LANES
                ]
    for tile in range(lon_total // LANES):
        out_ref[:, :, tile * LANES : (tile + 1) * LANES] = (
            rows_ref[tile].astype(jnp.bfloat16).reshape(kept, row_count, LANES)
        )


def local(fields, conv_first, conv_second, mixing):
    lat_count = lax.axis_size("lat")
    lon_count = lax.axis_size("lon")
    channels, row_count, lon_part = fields.shape
    lat_total = row_count * lat_count
    lon_total = lon_part * lon_count
    orders = lat_total // 2
    degrees = mixing.shape[0]
    owners = lat_count * lon_count
    per_device = orders // owners
    half = row_count // 2
    kept = channels // 2
    swap = [(0, 1), (1, 0)]
    both = ("lat", "lon")
    bfloat = functools.partial(jax.ShapeDtypeStruct, dtype=jnp.bfloat16)

    other = lax.ppermute(fields, "lon", swap)
    unpacked = pltpu.VMEM((lon_part // LANES, channels * row_count, LANES), jnp.float32)
    columns = per_device * degrees
    span = 32 if degrees % 32 == 0 else degrees
    width = lat_total * per_device
    arguments = [
        pltpu.with_memory_space_constraint(value, pltpu.HBM)
        for value in (
            fields,
            jnp.transpose(conv_first, (2, 3, 0, 1)),
            jnp.transpose(conv_second, (2, 3, 0, 1)),
        )
    ]
    own, taps_first, taps_second = call(
        load_kernel,
        (
            bfloat((row_count, channels, lon_part)),
            bfloat(arguments[1].shape),
            bfloat(arguments[2].shape),
        ),
        [pltpu.VMEM(fields.shape, jnp.bfloat16), unpacked, pltpu.SemaphoreType.DMA((3,))],
        [HBM] * 3,
        pl.CostEstimate(flops=1 << 16, bytes_accessed=1 << 21, transcendentals=0),
    )(*arguments)
    message = call(
        message_kernel,
        bfloat((2, channels, lon_total)),
        [unpacked],
        [VMEM, VMEM],
        pl.CostEstimate(flops=1 << 16, bytes_accessed=1 << 18, transcendentals=0),
    )(own, other)
    pairs = []
    for i in range(lat_count - 1):
        lower = 2 * i + half_of(i, 1, lat_count)
        upper = 2 * (i + 1) + half_of(i + 1, 0, lat_count)
        pairs += [(lower, upper), (upper, lower)]
    halo = lax.ppermute(message, both, pairs)

    taps = (6 * channels, 2 * channels)
    pair = jax.ShapeDtypeStruct((2, channels, lon_total), jnp.float32)
    first, second, dft, first_part, second_part, interior = call(
        functools.partial(interior_kernel, lat_total, owners),
        (
            bfloat(taps),
            bfloat(taps),
            bfloat((2 * orders, lon_total)),
            pair,
            pair,
            jax.ShapeDtypeStruct((half - 2, orders, 2 * channels), jnp.float32),
        ),
        [
            unpacked,
            pltpu.VMEM((half + 2, channels, lon_total), jnp.bfloat16),
            pltpu.VMEM((half, channels, lon_total), jnp.bfloat16),
            pltpu.VMEM((half - 2, channels, lon_total), jnp.bfloat16),
            pltpu.VMEM((2, 3 * channels, 3 * channels), jnp.bfloat16),
            pltpu.VMEM((2, 2) + taps, jnp.bfloat16),
        ],
        [VMEM] * 5,
        pl.CostEstimate(flops=1 << 28, bytes_accessed=1 << 22, transcendentals=0),
    )(
        own,
        other,
        taps_first,
        taps_second,
        message,
    )

    def mixing_table(values, after):
        return call(
            functools.partial(mixing_kernel, per_device),
            jax.ShapeDtypeStruct((channels, kept, columns), jnp.float32),
            [],
            [VMEM, ANY],
            pl.CostEstimate(flops=1 << 20, bytes_accessed=1 << 22, transcendentals=0),
        )(values, after)

    mine = mixing_table(mixing, second_part)
    theirs = lax.ppermute(mine, "lon", swap)
    analysis, synthesis = call(
        functools.partial(legendre_kernel, span, lat_count, row_count, per_device),
        (bfloat((columns, width)), bfloat((lat_total, columns))),
        [pltpu.VMEM((width // LANES, 2 * degrees, LANES), jnp.float32)],
        [ANY],
        pl.CostEstimate(flops=1 << 35, bytes_accessed=1 << 26, transcendentals=0),
    )(second_part)
    coeffs = call(
        functools.partial(edge_kernel, lat_total, half),
        bfloat((owners, per_device * half, 2 * channels)),
        [pltpu.VMEM((orders * half, 2 * channels), jnp.float32)],
        [VMEM] * 7 + [ANY] * 2,
        pl.CostEstimate(flops=1 << 26, bytes_accessed=1 << 20, transcendentals=0),
    )(halo, first, second, dft, first_part, second_part, interior, mine, analysis)
    pieces = lax.all_to_all(coeffs, both, split_axis=0, concat_axis=0, tiled=True)

    chunk_rows = row_count * 2 * per_device * kept // LANES
    chunks = call(
        functools.partial(spectral_kernel, per_device),
        bfloat((owners, chunk_rows, LANES)),
        [
            pltpu.VMEM((2 * channels, columns), jnp.float32),
            pltpu.VMEM((owners * chunk_rows, LANES), jnp.float32),
        ],
        [VMEM] * 5,
        pl.CostEstimate(flops=1 << 24, bytes_accessed=1 << 20, transcendentals=0),
    )(pieces, analysis, synthesis, mine, theirs)

    back = lax.all_to_all(chunks, both, split_axis=0, concat_axis=0, tiled=True)
    return call(
        functools.partial(inverse_kernel, per_device),
        bfloat((kept, row_count, lon_total)),
        [
            pltpu.VMEM((owners * chunk_rows, LANES), jnp.float32),
            pltpu.VMEM((lon_total // LANES, kept * row_count, LANES), jnp.float32),
        ],
        [VMEM] * 2,
        pl.CostEstimate(flops=1 << 24, bytes_accessed=1 << 19, transcendentals=0),
    )(back, dft)


def solution(mesh):
    in_specs = (P("groups", "lat", "lon"), P(), P(), P(None, "lon", None))
    out_specs = P(("groups", "lon"), "lat", None)
    return jax.shard_map(local, mesh=mesh, in_specs=in_specs, out_specs=out_specs, check_vma=False)
```

```python
import functools
import math

import jax
import jax.numpy as jnp
from jax import lax
from jax.experimental import pallas as pl
from jax.experimental.pallas import tpu as pltpu
from jax.sharding import PartitionSpec as P

VMEM = pl.BlockSpec(memory_space=pltpu.VMEM)
ANY = pl.BlockSpec(memory_space=pl.ANY)
HBM = pl.BlockSpec(memory_space=pltpu.HBM)
LIMIT = 40 * 1024 * 1024
LANES = 128


def call(kernel, out_shape, scratch, in_specs, cost):
    return pl.pallas_call(
        kernel,
        out_shape=out_shape,
        in_specs=in_specs,
        out_specs=jax.tree.map(lambda _: VMEM, out_shape),
        scratch_shapes=scratch,
        compiler_params=pltpu.CompilerParams(vmem_limit_bytes=LIMIT),
        cost_estimate=cost,
    )


def split_index(index, size):
    quotient = ((index.astype(jnp.float32) + 0.5) * (1.0 / size)).astype(jnp.int32)
    return quotient, index - quotient * size


def half_of(lat, lon, bands):
    if isinstance(lat, int):
        end = int(lat in (0, bands - 1))
    else:
        end = ((lat == 0) | (lat + 1 == bands)).astype(jnp.int32)
    return (lat + lon + 1 + end) & 1


def row_half():
    return half_of(lax.axis_index("lat"), lax.axis_index("lon"), lax.axis_size("lat"))


def unpack_rows(source_ref, rows_ref):
    channels, row_count, lon_part = source_ref.shape
    for tile in range(lon_part // LANES):
        rows_ref[tile] = (
            source_ref[:, :, tile * LANES : (tile + 1) * LANES]
            .astype(jnp.float32)
            .reshape(channels * row_count, LANES)
        )


def packed_row(rows_ref, row, channels):
    tiles, count, _ = rows_ref.shape
    found = [
        rows_ref[tile, pl.ds(row, channels, stride=count // channels), :] for tile in range(tiles)
    ]
    return jnp.concatenate(found, axis=1).astype(jnp.bfloat16)


def load_kernel(
    fields_ref,
    conv_first_ref,
    conv_second_ref,
    own_ref,
    first_ref,
    second_ref,
    fields_copy_ref,
    rows_ref,
    arrived,
):
    copies = [
        pltpu.make_async_copy(source, target, arrived.at[i])
        for i, (source, target) in enumerate(
            (
                (fields_ref, fields_copy_ref),
                (conv_first_ref, first_ref),
                (conv_second_ref, second_ref),
            )
        )
    ]
    for copy in copies:
        copy.start()
    copies[0].wait()
    unpack_rows(fields_copy_ref, rows_ref)
    for row in range(own_ref.shape[0]):
        own_ref[row] = packed_row(rows_ref, row, own_ref.shape[1])
    for copy in copies[1:]:
        copy.wait()


def place_row(out_ref, place, side, mine, theirs):
    lon_part = mine.shape[1]
    for position, values in ((side, mine), (1 - side, theirs)):
        start = pl.multiple_of(position * lon_part, LANES)
        out_ref[place, :, pl.ds(start, lon_part)] = values


def message_kernel(own_ref, other_ref, out_ref, rows_ref):
    row_count, channels, _ = own_ref.shape
    side = lax.axis_index("lon")
    unpack_rows(other_ref, rows_ref)
    for i in range(2):
        row = row_half() * (row_count - 2) + i
        place_row(out_ref, i, side, own_ref[row], packed_row(rows_ref, row, channels))


def layer(source_ref, weights, row):
    channels, lon_total = source_ref.shape[1:]
    taps = source_ref[row : row + 3].reshape(3 * channels, lon_total)
    sums = jnp.dot(weights, taps, preferred_element_type=jnp.float32)
    total = (
        sums[channels : 2 * channels]
        + pltpu.roll(sums[:channels], 1, 1)
        + pltpu.roll(sums[2 * channels :], lon_total - 1, 1)
    )
    return jnp.maximum(total, 0.0)


def row_weight(row, lat_total, lon_total):
    place = jnp.full((1, LANES), row, jnp.int32).astype(jnp.float32)
    return jnp.sin((place + 0.5) * (math.pi / lat_total)) * (math.pi / lat_total / lon_total)


def row_spectra(dft, hidden, first_row, lat_total):
    count, channels, lon_total = hidden.shape
    spectra = lax.dot_general(
        dft,
        hidden.reshape(count * channels, lon_total),
        (((1,), (1,)), ((), ())),
        preferred_element_type=jnp.float32,
    )
    orders = spectra.shape[0] // 2
    found = []
    for i in range(count):
        columns = slice(i * channels, (i + 1) * channels)
        parts = jnp.concatenate([spectra[:orders, columns], spectra[orders:, columns]], axis=1)
        found.append(parts * row_weight(first_row + i, lat_total, lon_total))
    return found


def interior_kernel(
    lat_total,
    owners,
    own_ref,
    other_ref,
    first_ref,
    second_ref,
    after_ref,
    first_out,
    second_out,
    dft_out,
    near_out,
    coeffs_out,
    rows_ref,
    band_ref,
    mid_ref,
    hidden_ref,
):
    del after_ref
    row_count, channels, lon_part = own_ref.shape
    lon_total = 2 * lon_part
    half = row_count // 2
    side, part = lax.axis_index("lon"), row_half()
    for source, target in ((first_ref, first_out), (second_ref, second_out)):
        for b in range(3):
            target[b * channels : (b + 1) * channels, :] = jnp.concatenate(
                [source[a, b] for a in range(3)], axis=1
            )
    orders = dft_out.shape[0] // 2
    place = lax.broadcasted_iota(jnp.int32, (orders, lon_total), 0)
    order, owner = split_index(place, owners)
    waves = owner * (orders // owners) + order
    points = lax.broadcasted_iota(jnp.int32, (orders, lon_total), 1)
    angle = ((waves * points) & (lon_total - 1)).astype(jnp.float32) * (2.0 * math.pi / lon_total)
    dft_out[:orders, :] = jnp.cos(angle).astype(jnp.bfloat16)
    dft_out[orders:, :] = (-jnp.sin(angle)).astype(jnp.bfloat16)
    unpack_rows(other_ref, rows_ref)
    for i in range(half + 2):
        row = 2 * part + i
        place_row(band_ref, i, side, own_ref[row], packed_row(rows_ref, row, channels))
    weights = first_out[...]
    for i in range(half):
        mid_ref[i] = layer(band_ref, weights, i).astype(jnp.bfloat16)
    near_out[...] = mid_ref[pl.ds((half - 2) * part, 2)]
    weights = second_out[...]
    for i in range(half - 2):
        hidden_ref[i] = layer(mid_ref, weights, i).astype(jnp.bfloat16)
    first_row = lax.axis_index("lat") * row_count + part * half + 2 * (1 - part)
    found = row_spectra(dft_out[...], hidden_ref[...], first_row, lat_total)
    for i, values in enumerate(found):
        coeffs_out[i] = values


def edge_kernel(
    lat_total,
    half,
    halo_ref,
    message_ref,
    near_ref,
    first_ref,
    second_ref,
    dft_ref,
    coeffs_ref,
    mine_ref,
    analysis_ref,
    out_ref,
    band_ref,
    mid_ref,
    hidden_ref,
    packed_ref,
):
    del mine_ref, analysis_ref
    part = row_half()
    first_row = lax.axis_index("lat") * (2 * half) + part * half
    band_ref[pl.ds(2 * part, 2)] = halo_ref[...]
    band_ref[pl.ds(2 - 2 * part, 2)] = message_ref[...]
    mid_ref[pl.ds(2 - 2 * part, 2)] = near_ref[...]
    weights = first_ref[...]
    for i in range(2):
        place = first_row - 1 + part * half + i
        values = layer(band_ref, weights, i)
        values = jnp.where((place >= 0) & (place < lat_total), values, 0.0)
        mid_ref[2 * part + i] = values.astype(jnp.bfloat16)
    weights = second_ref[...]
    for i in range(2):
        hidden_ref[i] = layer(mid_ref, weights, i).astype(jnp.bfloat16)
    edge = part * (half - 2)
    found = row_spectra(dft_ref[...], hidden_ref[...], first_row + edge, lat_total)
    owners, chunk_rows, _ = out_ref.shape
    for m in range(chunk_rows // half):
        own = slice(m * owners, (m + 1) * owners)
        for i in range(2):
            start = m * half + edge + i
            packed_ref[pl.ds(start, owners, stride=chunk_rows), :] = found[i][own]
        for i in range(half - 2):
            start = m * half + 2 - 2 * part + i
            packed_ref[pl.ds(start, owners, stride=chunk_rows), :] = coeffs_ref[i, own]
    out_ref[...] = packed_ref[...].astype(jnp.bfloat16).reshape(out_ref.shape)


def mixing_kernel(per_device, mixing_ref, after_ref, out_ref):
    del after_ref
    values = jnp.transpose(mixing_ref[...].astype(jnp.float32), (1, 0, 2))
    blocks = [
        jnp.concatenate([values[o]] * per_device, axis=0).T for o in range(values.shape[0])
    ]
    out_ref[...] = jnp.transpose(jnp.stack(blocks), (1, 0, 2))


def legendre_kernel(
    span, bands, row_count, per_device, after_ref, analysis_ref, synthesis_ref, values_ref
):
    del after_ref
    tiles, count, _ = values_ref.shape
    degrees, width = count // 2, tiles * LANES
    lat_total = bands * row_count
    half = row_count // 2
    first_order = (2 * lax.axis_index("lat") + lax.axis_index("lon")) * per_device
    lane = lax.broadcasted_iota(jnp.int32, (2, width), 1)
    form = lax.broadcasted_iota(jnp.int32, (2, width), 0)
    rest, low = split_index(lane, half)
    device, own_first = split_index(rest, per_device)
    rest, band = split_index(lane, bands)
    own_second, inner = split_index(rest, row_count)
    own = jnp.where(form == 0, own_first, own_second)
    place = (device >> 1) * row_count + half_of(device >> 1, device & 1, bands) * half + low
    row = jnp.where(form == 0, place, band * row_count + inner)
    south = row >= lat_total // 2
    row = jnp.where(south, lat_total - 1 - row, row)
    colatitude = (row.astype(jnp.float32) + 0.5) * (math.pi / lat_total)
    cosine, sine_theta = jnp.cos(colatitude), jnp.sin(colatitude)
    order_ids = first_order + own
    orders = order_ids.astype(jnp.float32)
    counter = 1.0 + lax.broadcasted_iota(jnp.int32, (1, max(degrees, LANES)), 1).astype(jnp.float32)
    log_terms = jnp.log((2.0 * counter - 1.0) / (2.0 * counter))
    log_start = 0.5 * jnp.log(orders + 0.5) + orders * jnp.log(sine_theta)
    for m in range(per_device):
        below = counter <= jnp.full(counter.shape, first_order + m, jnp.int32).astype(jnp.float32)
        total = jnp.sum(jnp.where(below, log_terms, 0.0), axis=1, keepdims=True)
        log_start = log_start + jnp.where(own == m, 0.5 * total, 0.0)
    parity = (1 - 2 * (order_ids & 1)).astype(jnp.float32)
    even_sign, odd_sign = jnp.where(south, parity, 1.0), jnp.where(south, -parity, 1.0)
    orders_squared = orders * orders
    start_scale = jnp.exp(log_start)
    current = previous = scale = log_scale = jnp.zeros_like(cosine)
    root = jnp.zeros_like(cosine)
    for degree in range(degrees):
        distance = float(degree * degree) - orders_squared
        inverse_root = lax.rsqrt(jnp.maximum(distance, 1.0))
        above = math.sqrt(max(4.0 * degree * degree - 1.0, 1.0))
        below = math.sqrt(max(4.0 * (degree - 1) * (degree - 1) - 1.0, 1.0))
        newest = (above * inverse_root) * (cosine * current - (root * (1.0 / below)) * previous)
        root = jnp.maximum(distance, 0.0) * inverse_root
        is_start = orders == float(degree)
        newest = jnp.where(is_start, 1.0, newest)
        scale = jnp.where(is_start, start_scale, scale)
        log_scale = jnp.where(is_start, log_start, log_scale)
        previous, current = current, newest
        emitted = newest * scale * (even_sign if degree % 2 == 0 else odd_sign)
        for tile in range(tiles):
            values_ref[tile, 2 * degree : 2 * degree + 2, :] = emitted[
                :, tile * LANES : (tile + 1) * LANES
            ]
        if degree % span == span - 1 and degree < degrees - 1:
            size_now = jnp.maximum(jnp.abs(current), jnp.abs(previous))
            safe_size = jnp.where(size_now > 0.0, size_now, 1.0)
            current, previous = current / safe_size, previous / safe_size
            log_scale = log_scale + jnp.log(safe_size)
            scale = jnp.where(degree >= orders, jnp.exp(log_scale), 0.0)
    first, second = (
        jnp.concatenate(
            [values_ref[tile, pl.ds(i, degrees, stride=2), :] for tile in range(tiles)], axis=1
        )
        for i in range(2)
    )
    for m in range(per_device):
        analysis_ref[m * degrees : (m + 1) * degrees, :] = jnp.where(
            own[0:1] == m, first, 0.0
        ).astype(jnp.bfloat16)
    stacked = jnp.concatenate(
        [second[:, m * lat_total : (m + 1) * lat_total] for m in range(per_device)], axis=0
    )
    synthesis_ref[...] = stacked.T.astype(jnp.bfloat16)


def spectral_kernel(
    per_device,
    pieces_ref,
    analysis_ref,
    synthesis_ref,
    mine_ref,
    theirs_ref,
    out_ref,
    spectral_ref,
    chunk_ref,
):
    owners, chunk_rows, width = pieces_ref.shape
    channels, kept, columns = mine_ref.shape
    degrees = columns // per_device
    parts = 2 * per_device
    groups = chunk_rows // parts
    packed = width // kept
    bands = synthesis_ref.shape[0] // (groups * packed)

    pieces = pieces_ref[...].reshape(owners * chunk_rows, width)
    spectral = lax.dot_general(
        pieces, analysis_ref[...], (((0,), (1,)), ((), ())), preferred_element_type=jnp.float32
    )
    spectral_ref[...] = spectral.astype(jnp.bfloat16).astype(jnp.float32)

    def add_channel(channel, totals):
        rows = [spectral_ref[pl.ds(part * channels + channel, 1), :] for part in range(2)]
        mine, theirs = mine_ref[channel], theirs_ref[channel]
        return (
            totals[0] + mine * rows[0],
            totals[1] + mine * rows[1],
            totals[2] + theirs * rows[0],
            totals[3] + theirs * rows[1],
        )

    zeros = jnp.zeros((kept, columns), jnp.float32)
    totals = lax.fori_loop(0, channels, add_channel, (zeros,) * 4, unroll=64)
    upper = lax.axis_index("lon") == 0
    mixed = [
        [jnp.where(upper, totals[part], totals[2 + part]) for part in range(2)],
        [jnp.where(upper, totals[2 + part], totals[part]) for part in range(2)],
    ]
    lane = lax.broadcasted_iota(jnp.int32, (kept, columns), 1)
    blocks = []
    for side in range(2):
        for m in range(per_device):
            own = (lane >= m * degrees) & (lane < (m + 1) * degrees)
            for part in range(2):
                blocks.append(jnp.where(own, mixed[side][part], 0.0).astype(jnp.bfloat16))
    values = lax.dot_general(
        synthesis_ref[...],
        jnp.concatenate(blocks, axis=0),
        (((1,), (1,)), ((), ())),
        preferred_element_type=jnp.float32,
    )
    for side in range(2):
        for group in range(groups):
            for part in range(parts):
                start = (side * parts + part) * kept
                pieces = [
                    values[(group * packed + i) * bands : (group * packed + i + 1) * bands, start : start + kept]
                    for i in range(packed)
                ]
                place = (side * groups + group) * parts + part
                chunk_ref[pl.ds(place, bands, stride=2 * groups * parts), :] = jnp.concatenate(
                    pieces, axis=1
                )
    out_ref[...] = chunk_ref[...].astype(jnp.bfloat16).reshape(out_ref.shape)


def inverse_kernel(per_device, pieces_ref, dft_ref, out_ref, pieces_32_ref, rows_ref):
    owners, chunk_rows, width = pieces_ref.shape
    kept, row_count, lon_total = out_ref.shape
    packed = width // kept
    parts = 2 * per_device
    pieces_32_ref[...] = pieces_ref[...].astype(jnp.float32).reshape(owners * chunk_rows, width)
    dft = dft_ref[...]
    place = lax.broadcasted_iota(jnp.int32, (2 * owners * per_device, width), 0)
    factor = jnp.where((place == 0) | (place == owners * per_device), 1.0, 2.0)
    for group in range(chunk_rows // parts):
        found = [
            pieces_32_ref[pl.ds(group * parts + 2 * m + part, owners, stride=chunk_rows), :]
            for part in range(2)
            for m in range(per_device)
        ]
        found = (jnp.concatenate(found, axis=0) * factor).astype(jnp.bfloat16)
        values = lax.dot_general(
            found, dft, (((0,), (0,)), ((), ())), preferred_element_type=jnp.float32
        )
        for i in range(packed):
            for tile in range(lon_total // LANES):
                rows_ref[tile, pl.ds(group * packed + i, kept, stride=row_count), :] = values[
                    i * kept : (i + 1) * kept, tile * LANES : (tile + 1) * LANES
                ]
    for tile in range(lon_total // LANES):
        out_ref[:, :, tile * LANES : (tile + 1) * LANES] = (
            rows_ref[tile].astype(jnp.bfloat16).reshape(kept, row_count, LANES)
        )


def local(fields, conv_first, conv_second, mixing):
    lat_count = lax.axis_size("lat")
    lon_count = lax.axis_size("lon")
    channels, row_count, lon_part = fields.shape
    lat_total = row_count * lat_count
    lon_total = lon_part * lon_count
    orders = lat_total // 2
    degrees = mixing.shape[0]
    owners = lat_count * lon_count
    per_device = orders // owners
    half = row_count // 2
    kept = channels // 2
    swap = [(0, 1), (1, 0)]
    both = ("lat", "lon")
    bfloat = functools.partial(jax.ShapeDtypeStruct, dtype=jnp.bfloat16)

    other = lax.ppermute(fields, "lon", swap)
    unpacked = pltpu.VMEM((lon_part // LANES, channels * row_count, LANES), jnp.float32)
    columns = per_device * degrees
    span = 32 if degrees % 32 == 0 else degrees
    width = lat_total * per_device
    arguments = [
        pltpu.with_memory_space_constraint(value, pltpu.HBM)
        for value in (
            fields,
            jnp.transpose(conv_first, (2, 3, 0, 1)),
            jnp.transpose(conv_second, (2, 3, 0, 1)),
        )
    ]
    own, taps_first, taps_second = call(
        load_kernel,
        (
            bfloat((row_count, channels, lon_part)),
            bfloat(arguments[1].shape),
            bfloat(arguments[2].shape),
        ),
        [pltpu.VMEM(fields.shape, jnp.bfloat16), unpacked, pltpu.SemaphoreType.DMA((3,))],
        [HBM] * 3,
        pl.CostEstimate(flops=1 << 16, bytes_accessed=1 << 21, transcendentals=0),
    )(*arguments)
    message = call(
        message_kernel,
        bfloat((2, channels, lon_total)),
        [unpacked],
        [VMEM, VMEM],
        pl.CostEstimate(flops=1 << 16, bytes_accessed=1 << 18, transcendentals=0),
    )(own, other)
    pairs = []
    for i in range(lat_count - 1):
        lower = 2 * i + half_of(i, 1, lat_count)
        upper = 2 * (i + 1) + half_of(i + 1, 0, lat_count)
        pairs += [(lower, upper), (upper, lower)]
    halo = lax.ppermute(message, both, pairs)

    taps = (3 * channels, 3 * channels)
    first, second, dft, near, interior = call(
        functools.partial(interior_kernel, lat_total, owners),
        (
            bfloat(taps),
            bfloat(taps),
            bfloat((2 * orders, lon_total)),
            bfloat((2, channels, lon_total)),
            jax.ShapeDtypeStruct((half - 2, orders, 2 * channels), jnp.float32),
        ),
        [
            unpacked,
            pltpu.VMEM((half + 2, channels, lon_total), jnp.bfloat16),
            pltpu.VMEM((half, channels, lon_total), jnp.bfloat16),
            pltpu.VMEM((half - 2, channels, lon_total), jnp.bfloat16),
        ],
        [VMEM, VMEM, VMEM, VMEM, ANY],
        pl.CostEstimate(flops=1 << 28, bytes_accessed=1 << 22, transcendentals=0),
    )(
        own,
        other,
        taps_first,
        taps_second,
        message,
    )

    def mixing_table(values, after):
        return call(
            functools.partial(mixing_kernel, per_device),
            jax.ShapeDtypeStruct((channels, kept, columns), jnp.float32),
            [],
            [VMEM, ANY],
            pl.CostEstimate(flops=1 << 20, bytes_accessed=1 << 22, transcendentals=0),
        )(values, after)

    mine = mixing_table(mixing, near)
    theirs = lax.ppermute(mine, "lon", swap)
    analysis, synthesis = call(
        functools.partial(legendre_kernel, span, lat_count, row_count, per_device),
        (bfloat((columns, width)), bfloat((lat_total, columns))),
        [pltpu.VMEM((width // LANES, 2 * degrees, LANES), jnp.float32)],
        [ANY],
        pl.CostEstimate(flops=1 << 35, bytes_accessed=1 << 26, transcendentals=0),
    )(near)
    coeffs = call(
        functools.partial(edge_kernel, lat_total, half),
        bfloat((owners, per_device * half, 2 * channels)),
        [
            pltpu.VMEM((4, channels, lon_total), jnp.bfloat16),
            pltpu.VMEM((4, channels, lon_total), jnp.bfloat16),
            pltpu.VMEM((2, channels, lon_total), jnp.bfloat16),
            pltpu.VMEM((orders * half, 2 * channels), jnp.float32),
        ],
        [VMEM] * 7 + [ANY] * 2,
        pl.CostEstimate(flops=1 << 26, bytes_accessed=1 << 20, transcendentals=0),
    )(halo, message, near, first, second, dft, interior, mine, analysis)
    pieces = lax.all_to_all(coeffs, both, split_axis=0, concat_axis=0, tiled=True)

    chunk_rows = row_count * 2 * per_device * kept // LANES
    chunks = call(
        functools.partial(spectral_kernel, per_device),
        bfloat((owners, chunk_rows, LANES)),
        [
            pltpu.VMEM((2 * channels, columns), jnp.float32),
            pltpu.VMEM((owners * chunk_rows, LANES), jnp.float32),
        ],
        [VMEM] * 5,
        pl.CostEstimate(flops=1 << 24, bytes_accessed=1 << 20, transcendentals=0),
    )(pieces, analysis, synthesis, mine, theirs)

    back = lax.all_to_all(chunks, both, split_axis=0, concat_axis=0, tiled=True)
    return call(
        functools.partial(inverse_kernel, per_device),
        bfloat((kept, row_count, lon_total)),
        [
            pltpu.VMEM((owners * chunk_rows, LANES), jnp.float32),
            pltpu.VMEM((lon_total // LANES, kept * row_count, LANES), jnp.float32),
        ],
        [VMEM] * 2,
        pl.CostEstimate(flops=1 << 24, bytes_accessed=1 << 19, transcendentals=0),
    )(back, dft)


def solution(mesh):
    in_specs = (P("groups", "lat", "lon"), P(), P(), P(None, "lon", None))
    out_specs = P(("groups", "lon"), "lat", None)
    return jax.shard_map(local, mesh=mesh, in_specs=in_specs, out_specs=out_specs, check_vma=False)
```

```python
import functools
import math

import jax
import jax.numpy as jnp
from jax import lax
from jax.experimental import pallas as pl
from jax.experimental.pallas import tpu as pltpu
from jax.sharding import PartitionSpec as P

VMEM = pl.BlockSpec(memory_space=pltpu.VMEM)
ANY = pl.BlockSpec(memory_space=pl.ANY)
HBM = pl.BlockSpec(memory_space=pltpu.HBM)
LIMIT = 40 * 1024 * 1024
LANES = 128


def call(kernel, out_shape, scratch, in_specs, cost, place=VMEM):
    return pl.pallas_call(
        kernel,
        out_shape=out_shape,
        in_specs=in_specs,
        out_specs=jax.tree.map(lambda _: place, out_shape),
        scratch_shapes=scratch,
        compiler_params=pltpu.CompilerParams(vmem_limit_bytes=LIMIT),
        cost_estimate=cost,
    )


def split_index(index, size):
    quotient = ((index.astype(jnp.float32) + 0.5) * (1.0 / size)).astype(jnp.int32)
    return quotient, index - quotient * size


def half_of(lat, lon, bands):
    last = (lat + 1) // bands if isinstance(lat, int) else (lat + 1 == bands).astype(jnp.int32)
    return (lat + lon + 1 + last) & 1


def row_half():
    return half_of(lax.axis_index("lat"), lax.axis_index("lon"), lax.axis_size("lat"))


def unpack_rows(source_ref, rows_ref):
    channels, row_count, lon_part = source_ref.shape
    for tile in range(lon_part // LANES):
        rows_ref[tile] = (
            source_ref[:, :, tile * LANES : (tile + 1) * LANES]
            .astype(jnp.float32)
            .reshape(channels * row_count, LANES)
        )


def packed_row(rows_ref, row, channels):
    tiles, count, _ = rows_ref.shape
    found = [
        rows_ref[tile, pl.ds(row, channels, stride=count // channels), :] for tile in range(tiles)
    ]
    return jnp.concatenate(found, axis=1).astype(jnp.bfloat16)


def load_kernel(
    fields_ref,
    conv_first_ref,
    conv_second_ref,
    own_ref,
    first_ref,
    second_ref,
    fields_copy_ref,
    rows_ref,
    arrived,
):
    copies = [
        pltpu.make_async_copy(source, target, arrived.at[i])
        for i, (source, target) in enumerate(
            (
                (fields_ref, fields_copy_ref),
                (conv_first_ref, first_ref),
                (conv_second_ref, second_ref),
            )
        )
    ]
    for copy in copies:
        copy.start()
    copies[0].wait()
    unpack_rows(fields_copy_ref, rows_ref)
    for row in range(own_ref.shape[0]):
        own_ref[row] = packed_row(rows_ref, row, own_ref.shape[1])
    for copy in copies[1:]:
        copy.wait()


def place_row(out_ref, place, side, mine, theirs):
    lon_part = mine.shape[1]
    for position, values in ((side, mine), (1 - side, theirs)):
        start = pl.multiple_of(position * lon_part, LANES)
        out_ref[place, :, pl.ds(start, lon_part)] = values


def message_kernel(own_ref, other_ref, out_ref, rows_ref):
    row_count, channels, _ = own_ref.shape
    side = lax.axis_index("lon")
    unpack_rows(other_ref, rows_ref)
    for i in range(2):
        row = row_half() * (row_count - 2) + i
        place_row(out_ref, i, side, own_ref[row], packed_row(rows_ref, row, channels))


def layer(source_ref, weights, row):
    channels, lon_total = source_ref.shape[1:]
    taps = source_ref[row : row + 3].reshape(3 * channels, lon_total)
    sums = jnp.dot(weights, taps, preferred_element_type=jnp.float32)
    total = (
        sums[channels : 2 * channels]
        + pltpu.roll(sums[:channels], 1, 1)
        + pltpu.roll(sums[2 * channels :], lon_total - 1, 1)
    )
    return jnp.maximum(total, 0.0)


def row_weight(row, lat_total, lon_total):
    place = jnp.full((1, LANES), row, jnp.int32).astype(jnp.float32)
    return jnp.sin((place + 0.5) * (math.pi / lat_total)) * (math.pi / lat_total / lon_total)


def row_spectra(dft, hidden, first_row, lat_total):
    count, channels, lon_total = hidden.shape
    spectra = lax.dot_general(
        dft,
        hidden.reshape(count * channels, lon_total),
        (((1,), (1,)), ((), ())),
        preferred_element_type=jnp.float32,
    )
    orders = spectra.shape[0] // 2
    found = []
    for i in range(count):
        columns = slice(i * channels, (i + 1) * channels)
        parts = jnp.concatenate([spectra[:orders, columns], spectra[orders:, columns]], axis=1)
        found.append(parts * row_weight(first_row + i, lat_total, lon_total))
    return found


def interior_kernel(
    lat_total,
    owners,
    own_ref,
    other_ref,
    first_ref,
    second_ref,
    after_ref,
    first_out,
    second_out,
    dft_out,
    near_out,
    coeffs_out,
    rows_ref,
    band_ref,
    mid_ref,
    hidden_ref,
):
    del after_ref
    row_count, channels, lon_part = own_ref.shape
    lon_total = 2 * lon_part
    half = row_count // 2
    side, part = lax.axis_index("lon"), row_half()
    for source, target in ((first_ref, first_out), (second_ref, second_out)):
        for b in range(3):
            target[b * channels : (b + 1) * channels, :] = jnp.concatenate(
                [source[a, b] for a in range(3)], axis=1
            )
    orders = dft_out.shape[0] // 2
    place = lax.broadcasted_iota(jnp.int32, (orders, lon_total), 0)
    order, owner = split_index(place, owners)
    waves = owner * (orders // owners) + order
    points = lax.broadcasted_iota(jnp.int32, (orders, lon_total), 1)
    angle = ((waves * points) & (lon_total - 1)).astype(jnp.float32) * (2.0 * math.pi / lon_total)
    dft_out[:orders, :] = jnp.cos(angle).astype(jnp.bfloat16)
    dft_out[orders:, :] = (-jnp.sin(angle)).astype(jnp.bfloat16)
    unpack_rows(other_ref, rows_ref)
    for i in range(half + 2):
        row = 2 * part + i
        place_row(band_ref, i, side, own_ref[row], packed_row(rows_ref, row, channels))
    weights = first_out[...]
    for i in range(half):
        mid_ref[i] = layer(band_ref, weights, i).astype(jnp.bfloat16)
    near_out[...] = mid_ref[pl.ds((half - 2) * part, 2)]
    weights = second_out[...]
    for i in range(half - 2):
        hidden_ref[i] = layer(mid_ref, weights, i).astype(jnp.bfloat16)
    first_row = lax.axis_index("lat") * row_count + part * half + 2 * (1 - part)
    found = row_spectra(dft_out[...], hidden_ref[...], first_row, lat_total)
    for i, values in enumerate(found):
        coeffs_out[i] = values


def edge_kernel(
    lat_total,
    half,
    halo_ref,
    message_ref,
    near_ref,
    first_ref,
    second_ref,
    dft_ref,
    coeffs_ref,
    mine_ref,
    analysis_ref,
    out_ref,
    band_ref,
    mid_ref,
    hidden_ref,
    packed_ref,
):
    del mine_ref, analysis_ref
    part = row_half()
    first_row = lax.axis_index("lat") * (2 * half) + part * half
    band_ref[pl.ds(2 * part, 2)] = halo_ref[...]
    band_ref[pl.ds(2 - 2 * part, 2)] = message_ref[...]
    mid_ref[pl.ds(2 - 2 * part, 2)] = near_ref[...]
    weights = first_ref[...]
    for i in range(2):
        place = first_row - 1 + part * half + i
        values = layer(band_ref, weights, i)
        values = jnp.where((place >= 0) & (place < lat_total), values, 0.0)
        mid_ref[2 * part + i] = values.astype(jnp.bfloat16)
    weights = second_ref[...]
    for i in range(2):
        hidden_ref[i] = layer(mid_ref, weights, i).astype(jnp.bfloat16)
    edge = part * (half - 2)
    found = row_spectra(dft_ref[...], hidden_ref[...], first_row + edge, lat_total)
    owners, chunk_rows, _ = out_ref.shape
    for m in range(chunk_rows // half):
        own = slice(m * owners, (m + 1) * owners)
        for i in range(2):
            start = m * half + edge + i
            packed_ref[pl.ds(start, owners, stride=chunk_rows), :] = found[i][own]
        for i in range(half - 2):
            start = m * half + 2 - 2 * part + i
            packed_ref[pl.ds(start, owners, stride=chunk_rows), :] = coeffs_ref[i, own]
    out_ref[...] = packed_ref[...].astype(jnp.bfloat16).reshape(out_ref.shape)


def mixing_kernel(per_device, mixing_ref, after_ref, out_ref):
    del after_ref
    values = jnp.transpose(mixing_ref[...].astype(jnp.float32), (1, 0, 2))
    blocks = [
        jnp.concatenate([values[o]] * per_device, axis=0).T for o in range(values.shape[0])
    ]
    out_ref[...] = jnp.transpose(jnp.stack(blocks), (1, 0, 2))


def legendre_kernel(
    span, bands, row_count, per_device, after_ref, analysis_ref, synthesis_ref, values_ref
):
    del after_ref
    tiles, count, _ = values_ref.shape
    degrees, width = count // 2, tiles * LANES
    lat_total = bands * row_count
    half = row_count // 2
    first_order = (2 * lax.axis_index("lat") + lax.axis_index("lon")) * per_device
    lane = lax.broadcasted_iota(jnp.int32, (2, width), 1)
    form = lax.broadcasted_iota(jnp.int32, (2, width), 0)
    rest, low = split_index(lane, half)
    device, own_first = split_index(rest, per_device)
    rest, band = split_index(lane, bands)
    own_second, inner = split_index(rest, row_count)
    own = jnp.where(form == 0, own_first, own_second)
    place = (device >> 1) * row_count + half_of(device >> 1, device & 1, bands) * half + low
    row = jnp.where(form == 0, place, band * row_count + inner)
    south = row >= lat_total // 2
    row = jnp.where(south, lat_total - 1 - row, row)
    colatitude = (row.astype(jnp.float32) + 0.5) * (math.pi / lat_total)
    cosine, sine_theta = jnp.cos(colatitude), jnp.sin(colatitude)
    order_ids = first_order + own
    orders = order_ids.astype(jnp.float32)
    counter = 1.0 + lax.broadcasted_iota(jnp.int32, (1, max(degrees, LANES)), 1).astype(jnp.float32)
    log_terms = jnp.log((2.0 * counter - 1.0) / (2.0 * counter))
    log_start = 0.5 * jnp.log(orders + 0.5) + orders * jnp.log(sine_theta)
    for m in range(per_device):
        below = counter <= jnp.full(counter.shape, first_order + m, jnp.int32).astype(jnp.float32)
        total = jnp.sum(jnp.where(below, log_terms, 0.0), axis=1, keepdims=True)
        log_start = log_start + jnp.where(own == m, 0.5 * total, 0.0)
    parity = (1 - 2 * (order_ids & 1)).astype(jnp.float32)
    even_sign, odd_sign = jnp.where(south, parity, 1.0), jnp.where(south, -parity, 1.0)
    orders_squared = orders * orders
    start_scale = jnp.exp(log_start)
    current = previous = scale = log_scale = jnp.zeros_like(cosine)
    root = jnp.zeros_like(cosine)
    for degree in range(degrees):
        distance = float(degree * degree) - orders_squared
        inverse_root = lax.rsqrt(jnp.maximum(distance, 1.0))
        above = math.sqrt(max(4.0 * degree * degree - 1.0, 1.0))
        below = math.sqrt(max(4.0 * (degree - 1) * (degree - 1) - 1.0, 1.0))
        newest = (above * inverse_root) * (cosine * current - (root * (1.0 / below)) * previous)
        root = jnp.maximum(distance, 0.0) * inverse_root
        is_start = orders == float(degree)
        newest = jnp.where(is_start, 1.0, newest)
        scale = jnp.where(is_start, start_scale, scale)
        log_scale = jnp.where(is_start, log_start, log_scale)
        previous, current = current, newest
        emitted = newest * scale * (even_sign if degree % 2 == 0 else odd_sign)
        for tile in range(tiles):
            values_ref[tile, 2 * degree : 2 * degree + 2, :] = emitted[
                :, tile * LANES : (tile + 1) * LANES
            ]
        if degree % span == span - 1 and degree < degrees - 1:
            size_now = jnp.maximum(jnp.abs(current), jnp.abs(previous))
            safe_size = jnp.where(size_now > 0.0, size_now, 1.0)
            current, previous = current / safe_size, previous / safe_size
            log_scale = log_scale + jnp.log(safe_size)
            scale = jnp.where(degree >= orders, jnp.exp(log_scale), 0.0)
    first, second = (
        jnp.concatenate(
            [values_ref[tile, pl.ds(i, degrees, stride=2), :] for tile in range(tiles)], axis=1
        )
        for i in range(2)
    )
    for m in range(per_device):
        analysis_ref[m * degrees : (m + 1) * degrees, :] = jnp.where(
            own[0:1] == m, first, 0.0
        ).astype(jnp.bfloat16)
    stacked = jnp.concatenate(
        [second[:, m * lat_total : (m + 1) * lat_total] for m in range(per_device)], axis=0
    )
    synthesis_ref[...] = stacked.T.astype(jnp.bfloat16)


def spectral_kernel(
    per_device,
    pieces_ref,
    analysis_ref,
    synthesis_ref,
    mine_ref,
    theirs_ref,
    out_ref,
    spectral_ref,
    chunk_ref,
):
    owners, chunk_rows, width = pieces_ref.shape
    channels, kept, columns = mine_ref.shape
    degrees = columns // per_device
    parts = 2 * per_device
    groups = chunk_rows // parts
    packed = width // kept
    bands = synthesis_ref.shape[0] // (groups * packed)

    pieces = pieces_ref[...].reshape(owners * chunk_rows, width)
    spectral = lax.dot_general(
        pieces, analysis_ref[...], (((0,), (1,)), ((), ())), preferred_element_type=jnp.float32
    )
    spectral_ref[...] = spectral.astype(jnp.bfloat16).astype(jnp.float32)

    def add_channel(channel, totals):
        rows = [spectral_ref[pl.ds(part * channels + channel, 1), :] for part in range(2)]
        mine, theirs = mine_ref[channel], theirs_ref[channel]
        return (
            totals[0] + mine * rows[0],
            totals[1] + mine * rows[1],
            totals[2] + theirs * rows[0],
            totals[3] + theirs * rows[1],
        )

    zeros = jnp.zeros((kept, columns), jnp.float32)
    totals = lax.fori_loop(0, channels, add_channel, (zeros,) * 4, unroll=64)
    upper = lax.axis_index("lon") == 0
    mixed = [
        [jnp.where(upper, totals[part], totals[2 + part]) for part in range(2)],
        [jnp.where(upper, totals[2 + part], totals[part]) for part in range(2)],
    ]
    lane = lax.broadcasted_iota(jnp.int32, (kept, columns), 1)
    blocks = []
    for side in range(2):
        for m in range(per_device):
            own = (lane >= m * degrees) & (lane < (m + 1) * degrees)
            for part in range(2):
                blocks.append(jnp.where(own, mixed[side][part], 0.0).astype(jnp.bfloat16))
    values = lax.dot_general(
        synthesis_ref[...],
        jnp.concatenate(blocks, axis=0),
        (((1,), (1,)), ((), ())),
        preferred_element_type=jnp.float32,
    )
    for side in range(2):
        for group in range(groups):
            for part in range(parts):
                start = (side * parts + part) * kept
                pieces = [
                    values[(group * packed + i) * bands : (group * packed + i + 1) * bands, start : start + kept]
                    for i in range(packed)
                ]
                place = (side * groups + group) * parts + part
                chunk_ref[pl.ds(place, bands, stride=2 * groups * parts), :] = jnp.concatenate(
                    pieces, axis=1
                )
    out_ref[...] = chunk_ref[...].astype(jnp.bfloat16).reshape(out_ref.shape)


def inverse_kernel(
    per_device, pieces_ref, dft_ref, out_ref, pieces_32_ref, rows_ref, staged_ref, sent
):
    owners, chunk_rows, width = pieces_ref.shape
    kept, row_count, lon_total = out_ref.shape
    packed = width // kept
    parts = 2 * per_device
    pieces_32_ref[...] = pieces_ref[...].astype(jnp.float32).reshape(owners * chunk_rows, width)
    dft = dft_ref[...]
    place = lax.broadcasted_iota(jnp.int32, (2 * owners * per_device, width), 0)
    factor = jnp.where((place == 0) | (place == owners * per_device), 1.0, 2.0)
    for group in range(chunk_rows // parts):
        found = [
            pieces_32_ref[pl.ds(group * parts + 2 * m + part, owners, stride=chunk_rows), :]
            for part in range(2)
            for m in range(per_device)
        ]
        found = (jnp.concatenate(found, axis=0) * factor).astype(jnp.bfloat16)
        values = lax.dot_general(
            found, dft, (((0,), (0,)), ((), ())), preferred_element_type=jnp.float32
        )
        for i in range(packed):
            for tile in range(lon_total // LANES):
                rows_ref[tile, pl.ds(group * packed + i, kept, stride=row_count), :] = values[
                    i * kept : (i + 1) * kept, tile * LANES : (tile + 1) * LANES
                ]
    copies = []
    size = kept // 4
    for i in range(4):
        own = pl.ds(i * size, size)
        for tile in range(lon_total // LANES):
            block = rows_ref[tile, i * size * row_count : (i + 1) * size * row_count, :]
            staged_ref[own, :, tile * LANES : (tile + 1) * LANES] = block.astype(
                jnp.bfloat16
            ).reshape(size, row_count, LANES)
        copies.append(pltpu.make_async_copy(staged_ref.at[own], out_ref.at[own], sent.at[i]))
        copies[-1].start()
    for copy in copies:
        copy.wait()


def local(fields, conv_first, conv_second, mixing):
    lat_count = lax.axis_size("lat")
    lon_count = lax.axis_size("lon")
    channels, row_count, lon_part = fields.shape
    lat_total = row_count * lat_count
    lon_total = lon_part * lon_count
    orders = lat_total // 2
    degrees = mixing.shape[0]
    owners = lat_count * lon_count
    per_device = orders // owners
    half = row_count // 2
    kept = channels // 2
    swap = [(0, 1), (1, 0)]
    both = ("lat", "lon")
    bfloat = functools.partial(jax.ShapeDtypeStruct, dtype=jnp.bfloat16)

    other = lax.ppermute(fields, "lon", swap)
    unpacked = pltpu.VMEM((lon_part // LANES, channels * row_count, LANES), jnp.float32)
    columns = per_device * degrees
    span = 32 if degrees % 32 == 0 else degrees
    width = lat_total * per_device
    arguments = [
        pltpu.with_memory_space_constraint(value, pltpu.HBM)
        for value in (
            fields,
            jnp.transpose(conv_first, (2, 3, 0, 1)),
            jnp.transpose(conv_second, (2, 3, 0, 1)),
        )
    ]
    own, taps_first, taps_second = call(
        load_kernel,
        (
            bfloat((row_count, channels, lon_part)),
            bfloat(arguments[1].shape),
            bfloat(arguments[2].shape),
        ),
        [pltpu.VMEM(fields.shape, jnp.bfloat16), unpacked, pltpu.SemaphoreType.DMA((3,))],
        [HBM] * 3,
        pl.CostEstimate(flops=1 << 16, bytes_accessed=1 << 21, transcendentals=0),
    )(*arguments)
    message = call(
        message_kernel,
        bfloat((2, channels, lon_total)),
        [unpacked],
        [VMEM, VMEM],
        pl.CostEstimate(flops=1 << 16, bytes_accessed=1 << 18, transcendentals=0),
    )(own, other)
    pairs = []
    for i in range(lat_count - 1):
        lower = 2 * i + half_of(i, 1, lat_count)
        upper = 2 * (i + 1) + half_of(i + 1, 0, lat_count)
        pairs += [(lower, upper), (upper, lower)]
    halo = lax.ppermute(message, both, pairs)

    taps = (3 * channels, 3 * channels)
    first, second, dft, near, interior = call(
        functools.partial(interior_kernel, lat_total, owners),
        (
            bfloat(taps),
            bfloat(taps),
            bfloat((2 * orders, lon_total)),
            bfloat((2, channels, lon_total)),
            jax.ShapeDtypeStruct((half - 2, orders, 2 * channels), jnp.float32),
        ),
        [
            unpacked,
            pltpu.VMEM((half + 2, channels, lon_total), jnp.bfloat16),
            pltpu.VMEM((half, channels, lon_total), jnp.bfloat16),
            pltpu.VMEM((half - 2, channels, lon_total), jnp.bfloat16),
        ],
        [VMEM, VMEM, VMEM, VMEM, ANY],
        pl.CostEstimate(flops=1 << 28, bytes_accessed=1 << 22, transcendentals=0),
    )(
        own,
        other,
        taps_first,
        taps_second,
        message,
    )

    def mixing_table(values, after):
        return call(
            functools.partial(mixing_kernel, per_device),
            jax.ShapeDtypeStruct((channels, kept, columns), jnp.float32),
            [],
            [VMEM, ANY],
            pl.CostEstimate(flops=1 << 20, bytes_accessed=1 << 22, transcendentals=0),
        )(values, after)

    mine = mixing_table(mixing, near)
    theirs = lax.ppermute(mine, "lon", swap)
    analysis, synthesis = call(
        functools.partial(legendre_kernel, span, lat_count, row_count, per_device),
        (bfloat((columns, width)), bfloat((lat_total, columns))),
        [pltpu.VMEM((width // LANES, 2 * degrees, LANES), jnp.float32)],
        [ANY],
        pl.CostEstimate(flops=1 << 35, bytes_accessed=1 << 26, transcendentals=0),
    )(near)
    coeffs = call(
        functools.partial(edge_kernel, lat_total, half),
        bfloat((owners, per_device * half, 2 * channels)),
        [
            pltpu.VMEM((4, channels, lon_total), jnp.bfloat16),
            pltpu.VMEM((4, channels, lon_total), jnp.bfloat16),
            pltpu.VMEM((2, channels, lon_total), jnp.bfloat16),
            pltpu.VMEM((orders * half, 2 * channels), jnp.float32),
        ],
        [VMEM] * 7 + [ANY] * 2,
        pl.CostEstimate(flops=1 << 26, bytes_accessed=1 << 20, transcendentals=0),
    )(halo, message, near, first, second, dft, interior, mine, analysis)
    pieces = lax.all_to_all(coeffs, both, split_axis=0, concat_axis=0, tiled=True)

    chunk_rows = row_count * 2 * per_device * kept // LANES
    chunks = call(
        functools.partial(spectral_kernel, per_device),
        bfloat((owners, chunk_rows, LANES)),
        [
            pltpu.VMEM((2 * channels, columns), jnp.float32),
            pltpu.VMEM((owners * chunk_rows, LANES), jnp.float32),
        ],
        [VMEM] * 5,
        pl.CostEstimate(flops=1 << 24, bytes_accessed=1 << 20, transcendentals=0),
    )(pieces, analysis, synthesis, mine, theirs)

    back = lax.all_to_all(chunks, both, split_axis=0, concat_axis=0, tiled=True)
    return call(
        functools.partial(inverse_kernel, per_device),
        bfloat((kept, row_count, lon_total)),
        [
            pltpu.VMEM((owners * chunk_rows, LANES), jnp.float32),
            pltpu.VMEM((lon_total // LANES, kept * row_count, LANES), jnp.float32),
            pltpu.VMEM((kept, row_count, lon_total), jnp.bfloat16),
            pltpu.SemaphoreType.DMA((4,)),
        ],
        [VMEM] * 2,
        pl.CostEstimate(flops=1 << 24, bytes_accessed=1 << 19, transcendentals=0),
        HBM,
    )(back, dft)


def solution(mesh):
    in_specs = (P("groups", "lat", "lon"), P(), P(), P(None, "lon", None))
    out_specs = P(("groups", "lon"), "lat", None)
    return jax.shard_map(local, mesh=mesh, in_specs=in_specs, out_specs=out_specs, check_vma=False)
```
